256 devices in a mesh: sect: 4 (over z_hi), ctx: 8 (over z_lo, y), tp: 8 (over x, core).
Axes of the slice: x: 4, y: 4, z: 8 (z_hi: 4, z_lo: 2; z = z_hi * 2 + z_lo), core: 2. Of those that a mesh axis runs over, the one named last changes fastest.
Arguments:
- patches: bfloat16 [4096, 1280], P(('sect', 'ctx')), may hold values from -6 to 6
- patch_gain: float32 [1280], replicated, may hold values from 0.25 to 1.75
- patch_shift: float32 [1280], replicated, may hold values from -3 to 3
- encoder_up: bfloat16 [1280, 5120], P(None, 'tp'), may hold values from -0.15625 to 0.15625
- encoder_down: bfloat16 [5120, 1280], P('tp'), may hold values from -0.078125 to 0.078125
- proj_weight: bfloat16 [1280, 8192], P(None, 'tp'), may hold values from -0.15625 to 0.15625
- hidden_text: bfloat16 [8192, 8192], P(('sect', 'ctx'), 'tp'), may hold values from -180 to 180
- slot_source: int32 [64], P(('sect', 'ctx')), may hold values from 0 to 4, as said below
- norm_gain: float32 [8192], P('tp'), may hold values from 0.25 to 1.75
- kv_weight: bfloat16 [2048, 8192], P(None, 'tp'), may hold values from -0.0625 to 0.0625
- queries: bfloat16 [8192, 4096], P(('sect', 'ctx'), 'tp'), may hold values from -40 to 40
Outputs:
- attended: bfloat16 [8192, 4096], P(('sect', 'ctx'), 'tp')
The draws below stay inside these ranges and needn't reach their ends.
Inputs may be any that keep to these rules, and one draw needn't show every extreme that they name: `slot_source`: for each ctx index, the slots of the blocks with that index carry each value 0 to 3 exactly once, all other slots 4.
All inputs are finite; a program needn't handle non-finite values.
Results may differ from the reference program's by a relative error of at most 0.019.
Values may be sent and summed in bfloat16 or wider, within the bound.
No kernel may reach another device: no remote copies, remote signals or barrier semaphores. Data moves between devices by JAX's collectives and lax.ppermute only.
A program may use at most 128 MiB of HBM per device.

```python
import math
import jax
import jax.numpy as jnp
from jax import lax

D = 8192
ENC = 1280
ENC_FF = 5120
HEAD = 128
Q_HEADS = 32
KV_HEADS = 8
PATCHES = 128
TOK_DEV = 256
BLOCKS = 32
TOKENS = 8192
IMAGES = 32
SLOTS_DEV = 2
SLOTS = 64
N_SECT = 4
N_CTX = 8


def draw_hidden_text(key, part):
    key_rows, key_cols, key_base = jax.random.split(key, 3)
    row_log = jax.random.uniform(key_rows, (TOKENS, 1), jnp.float32, 0.0, math.log(10.0))
    col_log = jax.random.uniform(key_cols, (1, D), jnp.float32, 0.0, math.log(10.0)) + 0.55 * jnp.arange(D, dtype=jnp.float32) / D
    base_values = jnp.clip(jax.random.normal(key_base, (TOKENS, D), jnp.float32), -5.0, 5.0)
    return (0.2 * base_values * jnp.exp(row_log) * jnp.exp(col_log)).astype(jnp.bfloat16)


def draw_slot_source(key, part):
    column_keys = jax.random.split(key, N_CTX)
    base_values = jnp.minimum(jnp.arange(N_SECT * SLOTS_DEV, dtype=jnp.int32), N_SECT).astype(jnp.int32)
    shuffled = jax.vmap(lambda column_key: jax.random.permutation(column_key, base_values))(column_keys)
    shuffled = shuffled.reshape(N_CTX, N_SECT, SLOTS_DEV)
    return jnp.transpose(shuffled, (1, 0, 2)).reshape(SLOTS).astype(jnp.int32)


def draw_queries(key, part):
    key_base = jax.random.fold_in(key, 0)
    shape_full = (TOKENS, Q_HEADS * HEAD)
    values_out = jnp.clip(jax.random.normal(key_base, shape_full, jnp.float32), -5.0, 5.0) * 0.6
    return values_out.astype(jnp.bfloat16)


def level_of(own_key, extent, cuts, low, top_value):
    factor_of, own = 1.0, jax.random.fold_in(own_key, 6)
    for axis_at, parts in cuts:
        steps = jnp.exp(jax.random.uniform(jax.random.fold_in(own, axis_at), (parts,), jnp.float32, low / len(cuts), top_value / len(cuts)))
        factor_of = factor_of * jnp.repeat(steps, extent[axis_at] // parts).reshape([-1 if axis == axis_at else 1 for axis in range(len(extent))])
    return factor_of


def centred(key, shape, scale, reach, cuts=(), kind=jnp.bfloat16):
    values = jax.random.normal(key, shape, jnp.float32) * scale
    if len(cuts) > 0:
        values = level_of(key, shape, cuts, -0.22, 0.18) * values
    return jnp.clip(values, min=-reach, max=reach).astype(kind)


def setup_inputs(seed: int = 0) -> dict:
    key_list = jax.random.split(jax.random.key(seed), 12)
    patches = centred(key_list[0], (IMAGES * PATCHES, ENC), 1.0, 6.0, ((0, 32),))
    patch_gain = jnp.clip(1.0 + 0.15 * jax.random.normal(key_list[1], (ENC,), jnp.float32), 0.25, 1.75)
    patch_shift = centred(key_list[2], (ENC,), 0.5, 3.0, (), jnp.float32)
    encoder_up = centred(key_list[3], (ENC, ENC_FF), ENC ** -0.5, 0.15625, ((1, 8),))
    encoder_down = centred(key_list[4], (ENC_FF, ENC), ENC_FF ** -0.5, 0.078125, ((0, 8),))
    proj_weight = centred(key_list[5], (ENC, D), ENC ** -0.5, 0.15625, ((1, 8),))
    hidden_text = draw_hidden_text(jax.random.fold_in(key_list[11], 71), 0)
    slot_source = draw_slot_source(jax.random.fold_in(key_list[11], 71), 0)
    norm_gain = jnp.clip(1.0 + 0.15 * jax.random.normal(key_list[8], (D,), jnp.float32), 0.25, 1.75)
    kv_weight = centred(key_list[9], (2 * KV_HEADS * HEAD, D), D ** -0.5, 0.0625, ((1, 8),))
    queries = draw_queries(jax.random.fold_in(key_list[11], 71), 0)
    return {"patches": patches, "patch_gain": patch_gain, "patch_shift": patch_shift, "encoder_up": encoder_up, "encoder_down": encoder_down, "proj_weight": proj_weight, "hidden_text": hidden_text, "slot_source": slot_source, "norm_gain": norm_gain, "kv_weight": kv_weight, "queries": queries}


def layer_norm(values, norm_scale, norm_shift):
    widened = values.astype(jnp.float32)
    center = lax.optimization_barrier(jnp.mean(widened, axis=-1, keepdims=True))
    spread = lax.optimization_barrier(jnp.mean(jnp.square(widened - center), axis=-1, keepdims=True))
    return ((widened - center) * lax.rsqrt(spread + 1e-06) * norm_scale + norm_shift).astype(jnp.bfloat16)

def rotate_keys(keys_in, positions):
    half_size = keys_in.shape[-2] // 2
    frequencies = jnp.exp(jnp.arange(half_size, dtype=jnp.float32) * (-2.0 * math.log(500000.0) / (2 * half_size)))
    angles = positions[None, :] * frequencies[:, None]
    cosine_table = jnp.cos(angles)
    sine_table = jnp.sin(angles)
    first_half = keys_in[..., :half_size, :]
    second_half = keys_in[..., half_size:, :]
    return jnp.concatenate([first_half * cosine_table - second_half * sine_table, second_half * cosine_table + first_half * sine_table], axis=-2)

def attend_update(state_now, queries_blk, query_pos, keys_blk, values_blk, key_pos):
    running_max, running_sum, accumulated = state_now
    scale_value = queries_blk.shape[-1] ** (-0.5)
    scores = jnp.einsum('rkgd,kdn->kgrn', queries_blk.astype(jnp.float32), keys_blk.astype(jnp.float32)) * scale_value
    allowed = query_pos[:, None] >= key_pos[None, :]
    scores = jnp.where(allowed, scores, -jnp.inf)
    new_max = jnp.maximum(running_max, lax.optimization_barrier(jnp.max(scores, axis=-1)))
    factor = jnp.exp(running_max - new_max)
    weights = jnp.exp(scores - new_max[..., None])
    running_sum = running_sum * factor + lax.optimization_barrier(jnp.sum(weights, axis=-1))
    rounded = lax.optimization_barrier(weights.astype(jnp.bfloat16))
    mixed_rows = jnp.einsum('kgrn,kdn->kgrd', rounded.astype(jnp.float32), values_blk.astype(jnp.float32))
    accumulated = accumulated * factor[..., None] + mixed_rows
    return (new_max, running_sum, accumulated)

def reference(patches, patch_gain, patch_shift, encoder_up, encoder_down, proj_weight, hidden_text, slot_source, norm_gain, kv_weight, queries):
    normed_patches = layer_norm(patches, patch_gain, patch_shift)
    enc_hidden = jax.nn.gelu(jnp.dot(normed_patches, encoder_up, preferred_element_type=jnp.float32), approximate=False).astype(jnp.bfloat16)
    encoded = (patches.astype(jnp.float32) + jnp.dot(enc_hidden, encoder_down, preferred_element_type=jnp.float32)).astype(jnp.bfloat16)
    image_emb = jnp.dot(encoded, proj_weight, preferred_element_type=jnp.float32).astype(jnp.bfloat16)
    image_emb = image_emb.reshape(N_SECT, N_CTX, PATCHES, D)
    merged = hidden_text.reshape(N_SECT, N_CTX, SLOTS_DEV, PATCHES, D)
    sources = slot_source.reshape(N_SECT, N_CTX, SLOTS_DEV)
    for source_index in range(N_SECT):
        chosen = (sources == source_index)[..., None, None]
        merged = jnp.where(chosen, image_emb[source_index][None, :, None], merged)
    merged = merged.reshape(TOKENS, D)
    widened = merged.astype(jnp.float32)
    inverse = lax.rsqrt(lax.optimization_barrier(jnp.mean(jnp.square(widened), axis=1, keepdims=True)) + 1e-05)
    normed_hidden = (widened * inverse * norm_gain[None, :]).astype(jnp.bfloat16)
    projected = jnp.dot(kv_weight, normed_hidden.T, preferred_element_type=jnp.float32).reshape(KV_HEADS, 2, HEAD, TOKENS)
    positions = jnp.arange(TOKENS, dtype=jnp.float32)
    keys_all = rotate_keys(projected[:, 0], positions).astype(jnp.bfloat16)
    values_all = projected[:, 1].astype(jnp.bfloat16)
    group_size = Q_HEADS // KV_HEADS
    query_blocks = queries.reshape(BLOCKS, TOK_DEV, KV_HEADS, group_size, HEAD)

    def one_block(block_number):
        block_queries = query_blocks[block_number]
        query_pos = block_number * TOK_DEV + jnp.arange(TOK_DEV, dtype=jnp.int32)
        start_state = (jnp.full((KV_HEADS, group_size, TOK_DEV), -1e+30, jnp.float32), jnp.zeros((KV_HEADS, group_size, TOK_DEV), jnp.float32), jnp.zeros((KV_HEADS, group_size, TOK_DEV, HEAD), jnp.float32))

        def key_step(key_block, state_now):
            offset = (key_block * TOK_DEV).astype(jnp.int32)
            key_tile = lax.dynamic_slice_in_dim(keys_all, offset, TOK_DEV, 2)
            value_tile = lax.dynamic_slice_in_dim(values_all, offset, TOK_DEV, 2)
            key_pos = offset + jnp.arange(TOK_DEV, dtype=jnp.int32)
            return attend_update(state_now, block_queries, query_pos, key_tile, value_tile, key_pos)
        final_max, final_sum, final_acc = lax.fori_loop(0, block_number + 1, key_step, start_state)
        result = final_acc / final_sum[..., None]
        return jnp.transpose(result, (2, 0, 1, 3)).reshape(TOK_DEV, Q_HEADS * HEAD).astype(jnp.bfloat16)
    outputs = lax.map(one_block, jnp.arange(BLOCKS, dtype=jnp.int32))
    return outputs.reshape(TOKENS, Q_HEADS * HEAD)
```

```python
import functools
import math

import jax
import jax.numpy as jnp
from jax import lax
from jax.experimental import pallas as pl
from jax.experimental.pallas import tpu as pltpu
from jax.sharding import Mesh
from jax.sharding import PartitionSpec as P

D = 8192
HEAD = 128
HALF = 64
GROUP = 4
TOK = 256
IMG = 128
ROWS = 272
TP = ("x", "core")
Z = ("zh", "zl")
BF16 = jnp.bfloat16
F32 = jnp.float32
NEG = -1e30
LOG2E = math.log2(math.e)
SCALE = HEAD ** (-0.5)


def shift(values, axis, step):
    count = lax.axis_size(axis)
    return lax.ppermute(values, axis, [(i, (i + step) % count) for i in range(count)])


def pick(values, index):
    return lax.dynamic_index_in_dim(values, index, 0, keepdims=False)


def tp_reduce_scatter(pieces):
    core, x_at = lax.axis_index("core"), lax.axis_index("x")
    pairs = jnp.swapaxes(pieces, 0, 1)
    got = shift(pick(pairs, 1 - core), "core", 1)
    summed = pick(pairs, core).astype(F32) + got.astype(F32)
    sent = summed.astype(BF16)
    total = pick(summed, x_at)
    for step in (2, 1, 3):
        total = total + shift(pick(sent, (x_at + step) % 4), "x", step).astype(F32)
    return total


def tp_all_gather(piece):
    core, x_at = lax.axis_index("core"), lax.axis_index("x")
    whole = jnp.zeros((4, *piece.shape), piece.dtype)
    whole = lax.dynamic_update_index_in_dim(whole, piece, x_at, 0)
    for step in (2, 1, 3):
        whole = lax.dynamic_update_index_in_dim(
            whole, shift(piece, "x", step), (x_at - step) % 4, 0
        )
    other = shift(whole, "core", 1)
    even = jnp.where(core == 0, whole, other)
    odd = jnp.where(core == 0, other, whole)
    return jnp.stack([even, odd], 1)


def layer_norm(values, norm_scale, norm_shift):
    widened = values.astype(F32)
    center = jnp.mean(widened, axis=-1, keepdims=True)
    spread = jnp.mean(jnp.square(widened - center), axis=-1, keepdims=True)
    return ((widened - center) * lax.rsqrt(spread + 1e-06) * norm_scale + norm_shift).astype(BF16)


def project(features, norm_gain, kv_weight):
    widened = features.astype(F32)
    squares = jnp.sum(jnp.square(widened), axis=1)
    gained = (widened * norm_gain[None, :]).astype(BF16)
    rows = lax.dot_general(
        kv_weight, gained, (((1,), (1,)), ((), ())), preferred_element_type=F32
    )
    return rows, squares


def attend_kernel(place, text_ref, image_ref, cos_ref, sin_ref, query_ref, out_ref, keys, values, scores, top):
    z_at, y_at = place[0], place[1]
    turn = pl.program_id(0)

    @pl.when(turn == 0)
    def merge():
        values[HEAD:, :] = jnp.ones((HEAD, 8 * TOK), BF16)
        for block in range(8):
            for slot in range(2):
                lanes = slice(slot * IMG, (slot + 1) * IMG)
                place_at = block * TOK + slot * IMG
                text = text_ref[block, :, lanes].astype(F32)
                source = text[TOK : TOK + 1, :]
                rows = text[:TOK, :]
                for r in range(4):
                    rows = jnp.where(
                        source == float(r), image_ref[2 * r + block % 2].astype(F32), rows
                    )
                cosine = cos_ref[:, place_at : place_at + IMG]
                sine = sin_ref[:, place_at : place_at + IMG]
                first, second = rows[:HALF], rows[HALF:HEAD]
                keys[:HALF, place_at : place_at + IMG] = (first * cosine - second * sine).astype(BF16)
                keys[HALF:, place_at : place_at + IMG] = (second * cosine + first * sine).astype(BF16)
                values[:HEAD, place_at : place_at + IMG] = rows[HEAD:].astype(BF16)

    block_at = lax.rem(y_at + 2 + turn, 4)
    queries = query_ref[...]
    full = z_at + jnp.where(y_at < block_at, 1, 0)
    count = z_at + jnp.where(y_at <= block_at, 1, 0)
    row_at = lax.broadcasted_iota(jnp.int32, (TOK, TOK), 0)
    lane_at = lax.broadcasted_iota(jnp.int32, (TOK, TOK), 1)
    allowed = row_at >= lane_at
    top[...] = jnp.full(top.shape, NEG, F32)

    def score(block, masked):
        at = pl.ds(pl.multiple_of(block * TOK, TOK), TOK)
        keys_now = keys[:, at]
        for h in range(GROUP):
            s = jnp.dot(
                queries[:, h * HEAD : (h + 1) * HEAD], keys_now, preferred_element_type=F32
            )
            if masked:
                s = jnp.where(allowed, s, -jnp.inf)
            scores[h, :, at] = s
            top[h] = jnp.maximum(top[h], jnp.maximum(s[:, :HEAD], s[:, HEAD:]))

    pl.loop(0, full)(lambda block: score(block, False))

    @pl.when(count > full)
    def diagonal():
        score(full, True)

    lane = lax.broadcasted_iota(jnp.int32, (TOK, HEAD), 1)
    stats = jnp.zeros((TOK, HEAD), F32)
    for h in range(GROUP):
        most = jnp.max(top[h], axis=1, keepdims=True)
        offset = most * (SCALE * LOG2E)

        def weigh(block, acc):
            at = pl.ds(pl.multiple_of(block * TOK, TOK), TOK)
            weights = jnp.exp2(scores[h, :, at] * (SCALE * LOG2E) - offset).astype(BF16)
            return acc + lax.dot_general(
                weights, values[:, at], (((1,), (1,)), ((), ())), preferred_element_type=F32
            )

        acc = lax.fori_loop(0, count, weigh, jnp.zeros((TOK, 2 * HEAD), F32))
        total = acc[:, HEAD : HEAD + 1]
        some = total > 0.0
        out_ref[0, :TOK, h * HEAD : (h + 1) * HEAD] = (
            acc[:, :HEAD] / jnp.where(some, total, 1.0)
        ).astype(BF16)
        level = jnp.where(some, offset + jnp.log2(jnp.where(some, total, 1.0)), NEG)
        for part in range(3):
            piece = level.astype(BF16).astype(F32)
            stats = jnp.where(lane == 3 * h + part, piece, stats)
            level = level - piece
    out_ref[0, TOK:, :TOK] = stats.T[: ROWS - TOK].astype(BF16)
    out_ref[0, TOK:, TOK:] = jnp.zeros((ROWS - TOK, 2 * HEAD), BF16)


def attend(place, text, images, cosine, sine, queries):
    def query_block(turn, place):
        return (lax.rem(place[1] + 2 + turn, 4), 0)

    whole = lambda rank: lambda turn, place: (0,) * rank
    return pl.pallas_call(
        attend_kernel,
        out_shape=jax.ShapeDtypeStruct((4, ROWS, GROUP * HEAD), BF16),
        grid_spec=pltpu.PrefetchScalarGridSpec(
            num_scalar_prefetch=1,
            grid=(4,),
            in_specs=[
                pl.BlockSpec(text.shape, whole(3)),
                pl.BlockSpec(images.shape, whole(3)),
                pl.BlockSpec(cosine.shape, whole(2)),
                pl.BlockSpec(sine.shape, whole(2)),
                pl.BlockSpec((TOK, GROUP * HEAD), query_block),
            ],
            out_specs=pl.BlockSpec((1, ROWS, GROUP * HEAD), lambda turn, place: (turn, 0, 0)),
            scratch_shapes=[
                pltpu.VMEM((HEAD, 8 * TOK), BF16),
                pltpu.VMEM((2 * HEAD, 8 * TOK), BF16),
                pltpu.VMEM((GROUP, TOK, 8 * TOK), F32),
                pltpu.VMEM((GROUP, TOK, HEAD), F32),
            ],
        ),
        compiler_params=pltpu.CompilerParams(vmem_limit_bytes=40 * 1024 * 1024),
        name="attend",
    )(place, text, images, cosine, sine, queries)


def combine_kernel(*refs):
    out_ref = refs[-1]
    levels = []
    for ref in refs[:-1]:
        rows = ref[TOK:, :TOK].astype(F32)
        levels.append(jnp.concatenate([rows, jnp.zeros((HEAD - rows.shape[0], TOK), F32)], 0).T)
    for h in range(GROUP):
        lanes = slice(h * HEAD, (h + 1) * HEAD)
        level = [
            l[:, 3 * h : 3 * h + 1] + l[:, 3 * h + 1 : 3 * h + 2] + l[:, 3 * h + 2 : 3 * h + 3]
            for l in levels
        ]
        most = functools.reduce(jnp.maximum, level)
        weights = [jnp.exp2(l - most) for l in level]
        total = sum(weights)
        mixed = sum(w * ref[:TOK, lanes].astype(F32) for w, ref in zip(weights, refs[:-1]))
        out_ref[:, lanes] = (mixed / total).astype(BF16)


def combine(parts):
    return pl.pallas_call(
        combine_kernel,
        out_shape=jax.ShapeDtypeStruct((TOK, GROUP * HEAD), BF16),
        name="combine",
    )(*parts)


def body(
    patches,
    patch_gain,
    patch_shift,
    encoder_up,
    encoder_down,
    proj_weight,
    hidden_text,
    slot_source,
    norm_gain,
    kv_weight,
    queries,
):
    z_at, y_at = lax.axis_index(Z), lax.axis_index("y")
    queries_all = lax.all_gather(queries, "y", axis=0, tiled=True)

    normed_patches = layer_norm(patches, patch_gain, patch_shift)
    enc_hidden = jax.nn.gelu(
        jnp.dot(normed_patches, encoder_up, preferred_element_type=F32), approximate=False
    ).astype(BF16)
    partial_out = jnp.dot(enc_hidden, encoder_down, preferred_element_type=F32).astype(BF16)
    share = tp_reduce_scatter(partial_out.reshape(4, 2, 16, -1))
    tp_at = lax.axis_index(TP)
    own_patches = pick(patches.reshape(8, 16, -1), tp_at)
    encoded = tp_all_gather((own_patches.astype(F32) + share).astype(BF16))
    encoded = encoded.reshape(patches.shape)

    rows, squares = project(hidden_text, norm_gain, kv_weight)
    packed = jnp.concatenate(
        [rows.reshape(8, TOK, TOK), jnp.broadcast_to(squares[None, None, :], (8, 8, TOK))], 1
    )
    summed = lax.psum_scatter(
        packed.reshape(-1, TOK), TP, scatter_dimension=0, tiled=True
    )
    inverse = lax.rsqrt(summed[TOK : TOK + 1] / D + 1e-05)
    sources = jnp.repeat(slot_source.astype(F32), IMG)[None, :]
    text_rows = jnp.concatenate(
        [summed[:TOK] * inverse, jnp.broadcast_to(sources, (ROWS - TOK, TOK))], 0
    ).astype(BF16)
    text_all = lax.all_gather(text_rows, Z, axis=0)

    image_emb = jnp.dot(encoded, proj_weight, preferred_element_type=F32).astype(BF16)
    rows, squares = project(image_emb, norm_gain, kv_weight)
    high = squares.astype(BF16)
    low = (squares - high.astype(F32)).astype(BF16)
    tail = jnp.concatenate(
        [high[None], low[None], jnp.zeros((ROWS - TOK - 2, IMG), BF16)], 0
    )
    packed = jnp.concatenate(
        [rows.astype(BF16).reshape(8, TOK, IMG), jnp.broadcast_to(tail[None], (8, *tail.shape))], 1
    )
    summed = tp_reduce_scatter(packed.reshape(4, 2, ROWS, IMG))
    inverse = lax.rsqrt((summed[TOK] + summed[TOK + 1])[None] / D + 1e-05)
    image_rows = (summed[:TOK] * inverse).astype(BF16)
    images_all = lax.all_to_all(
        jnp.broadcast_to(image_rows[None], (8, *image_rows.shape)), Z, 0, 0, tiled=True
    )

    frequencies = jnp.exp(
        jnp.arange(HALF, dtype=F32) * (-2.0 * math.log(500000.0) / (2 * HALF))
    )
    index = jnp.arange(8 * TOK, dtype=jnp.int32)
    positions = ((index // TOK) * 4 + y_at) * TOK + index % TOK
    angles = positions.astype(F32)[None, :] * frequencies[:, None]
    place = jnp.stack([z_at, y_at]).astype(jnp.int32)
    parts = attend(place, text_all, images_all, jnp.cos(angles), jnp.sin(angles), queries_all)
    received = [shift(parts[turn], "y", step) for turn, step in ((0, 2), (1, 3), (2, 0), (3, 1)) if step]
    return combine([parts[2], *received])


def solution(mesh):
    split = Mesh(mesh.devices.reshape(4, 2, 4, 4, 2), ("zh", "zl", "y", "x", "core"))
    seq = ("zh", "zl", "y")
    in_specs = (
        P(seq, None),
        P(),
        P(),
        P(None, TP),
        P(TP, None),
        P(None, TP),
        P(seq, TP),
        P(seq),
        P(TP),
        P(None, TP),
        P(seq, TP),
    )
    return jax.shard_map(
        body, mesh=split, in_specs=in_specs, out_specs=P(seq, TP), check_vma=False
    )
```

```python
import functools
import math

import jax
import jax.numpy as jnp
from jax import lax
from jax.experimental import pallas as pl
from jax.experimental.pallas import tpu as pltpu
from jax.sharding import Mesh
from jax.sharding import PartitionSpec as P

D = 8192
HEAD = 128
HALF = 64
GROUP = 4
TOK = 256
IMG = 128
ROWS = 272
TP = ("x", "core")
Z = ("zh", "zl")
BF16 = jnp.bfloat16
F32 = jnp.float32
NEG = -1e30
LOG2E = math.log2(math.e)
KEYS = 2048
CHUNK = 512
ROWS_Q = GROUP * TOK
SCALE = HEAD ** (-0.5)


def shift(values, axis, step):
    count = lax.axis_size(axis)
    return lax.ppermute(values, axis, [(i, (i + step) % count) for i in range(count)])


def pick(values, index):
    return lax.dynamic_index_in_dim(values, index, 0, keepdims=False)


def vmem(mib):
    return pltpu.CompilerParams(vmem_limit_bytes=mib * 1024 * 1024)


def split_squares(column, count):
    row = jnp.broadcast_to(column, (count, HEAD)).T[:16]
    high = row.astype(BF16).astype(F32)
    at = lax.broadcasted_iota(jnp.int32, row.shape, 0)
    return jnp.where(at == 0, high, jnp.where(at == 1, row - high, 0.0)).astype(BF16)


def head_rows(step, features, tail, weight_ref, give_ref, keep_ref):
    rows = lax.dot_general(
        weight_ref[...], features[...], (((1,), (1,)), ((), ())), preferred_element_type=F32
    ).astype(BF16)

    @pl.when(step < 4)
    def to_other_core():
        give_ref[0, :TOK, :] = rows
        give_ref[0, TOK:, :] = tail[...]

    @pl.when(step >= 4)
    def own_core():
        keep_ref[0, :TOK, :] = rows
        keep_ref[0, TOK:, :] = tail[...]


def gain_features(features, gain_ref, gained, tail):
    widened = features.astype(F32)
    squares = jnp.sum(jnp.square(widened), axis=1, keepdims=True)
    tail[...] = split_squares(squares, features.shape[0])
    gained[...] = (widened * gain_ref[...]).astype(BF16)


def text_project_kernel(core, hidden_ref, gain_ref, weight_ref, give_ref, keep_ref, gained, tail):
    step = pl.program_id(0)

    @pl.when(step == 0)
    def first():
        gain_features(hidden_ref[...], gain_ref, gained, tail)

    head_rows(step, gained, tail, weight_ref, give_ref, keep_ref)


def image_project_kernel(
    core, half_ref, other_ref, proj_ref, gain_ref, weight_ref, give_ref, keep_ref, encoded, gained, tail
):
    step = pl.program_id(0)

    @pl.when(step == 0)
    def first():
        @pl.when(core[0] == 0)
        def low():
            encoded[:HALF, :] = half_ref[...]
            encoded[HALF:, :] = other_ref[...]

        @pl.when(core[0] == 1)
        def high():
            encoded[:HALF, :] = other_ref[...]
            encoded[HALF:, :] = half_ref[...]

        image = jnp.dot(encoded[...], proj_ref[...], preferred_element_type=F32).astype(BF16)
        gain_features(image, gain_ref, gained, tail)

    head_rows(step, gained, tail, weight_ref, give_ref, keep_ref)


def project(kernel, features, norm_gain, kv_weight, core, count, scratch):
    whole = lambda step, core: (0, 0)
    mine = jnp.reshape(core, (1,)).astype(jnp.int32)

    def head(step, core):
        x_at = jnp.where(step < 4, step, step - 4)
        return (2 * x_at + jnp.where(step < 4, 1 - core[0], core[0]), 0)

    shape = jax.ShapeDtypeStruct((4, ROWS, count), BF16)
    return pl.pallas_call(
        kernel,
        out_shape=(shape, shape),
        grid_spec=pltpu.PrefetchScalarGridSpec(
            num_scalar_prefetch=1,
            grid=(8,),
            in_specs=[
                *[pl.BlockSpec(f.shape, whole) for f in features],
                pl.BlockSpec((1, norm_gain.shape[0]), whole),
                pl.BlockSpec((TOK, kv_weight.shape[1]), head),
            ],
            out_specs=(
                pl.BlockSpec((1, ROWS, count), lambda step, core: (jnp.minimum(step, 3), 0, 0)),
                pl.BlockSpec((1, ROWS, count), lambda step, core: (jnp.maximum(step, 4) - 4, 0, 0)),
            ),
            scratch_shapes=[
                *scratch,
                pltpu.VMEM((count, kv_weight.shape[1]), BF16),
                pltpu.VMEM((16, count), BF16),
            ],
        ),
        compiler_params=vmem(24),
    )(mine, *features, norm_gain[None, :], kv_weight)


def pair_kernel(place, keep_ref, got_ref, own_ref, two_ref, one_ref, three_ref):
    for step, ref in ((2, two_ref), (1, one_ref), (3, three_ref), (0, own_ref)):
        at = lax.rem(place[0] + step, 4)
        total = keep_ref[at].astype(F32) + got_ref[at].astype(F32)
        ref[...] = total.astype(ref.dtype)


def add_pair(keep, got, x_at):
    part = keep.shape[1:]
    return pl.pallas_call(
        pair_kernel,
        out_shape=(jax.ShapeDtypeStruct(part, F32), *[jax.ShapeDtypeStruct(part, BF16)] * 3),
        in_specs=[
            pl.BlockSpec(memory_space=pltpu.SMEM),
            *[pl.BlockSpec(memory_space=pltpu.VMEM)] * 2,
        ],
        name="add_pair",
    )(jnp.reshape(x_at, (1,)).astype(jnp.int32), keep, got)


def finish_kernel(slots, *refs):
    *inputs, out_ref = refs
    total = inputs[0][...]
    for ref in inputs[1:]:
        total = total + ref[...].astype(F32)
    inverse = lax.rsqrt((total[TOK : TOK + 1] + total[TOK + 1 : TOK + 2]) / D + 1e-05)
    rows = (total[:TOK] * inverse).astype(BF16)
    for copy in range(8):
        out_ref[copy, :TOK, :] = rows
    if out_ref.shape[1] > TOK:
        lane = lax.broadcasted_iota(jnp.int32, (ROWS - TOK, out_ref.shape[2]), 1)
        source = jnp.where(lane < IMG, slots[0], slots[1]).astype(F32).astype(BF16)
        for copy in range(8):
            out_ref[copy, TOK:, :] = source


def finish_rows(slots, pieces, row_count):
    count = pieces[0].shape[1]
    return pl.pallas_call(
        finish_kernel,
        out_shape=jax.ShapeDtypeStruct((8, row_count, count), BF16),
        in_specs=[
            pl.BlockSpec(memory_space=pltpu.SMEM),
            *[pl.BlockSpec(memory_space=pltpu.VMEM)] * 4,
        ],
        name="finish_rows",
    )(slots, *pieces)


def scatter_rows(give, keep, slots, x_at, row_count):
    got = shift(give, "core", 1)
    own, two, one, three = add_pair(keep, got, x_at)
    pieces = [own, shift(two, "x", 2), shift(one, "x", 1), shift(three, "x", 3)]
    return finish_rows(slots, pieces, row_count)


def merge_kernel(text_ref, image_ref, cos_ref, sin_ref, keys, values):
    values[:, HEAD:] = jnp.ones((KEYS, HEAD), BF16)
    for block in range(8):
        for slot in range(2):
            lanes = slice(slot * IMG, (slot + 1) * IMG)
            here = slice(block * TOK + slot * IMG, block * TOK + (slot + 1) * IMG)
            text = text_ref[block, :, lanes].astype(F32)
            source = text[TOK : TOK + 1, :]
            rows = text[:TOK, :]
            for r in range(4):
                rows = jnp.where(
                    source == float(r), image_ref[2 * r + block % 2].astype(F32), rows
                )
            cosine, sine = cos_ref[:, here], sin_ref[:, here]
            first, second = rows[:HALF], rows[HALF:HEAD]
            keys[:HALF, here] = (first * cosine - second * sine).astype(BF16)
            keys[HALF:, here] = (second * cosine + first * sine).astype(BF16)
            values[here, :HEAD] = rows[HEAD:].T.astype(BF16)


def merge(text, images, cosine, sine):
    return pl.pallas_call(
        merge_kernel,
        out_shape=(
            jax.ShapeDtypeStruct((HEAD, KEYS), BF16),
            jax.ShapeDtypeStruct((KEYS, 2 * HEAD), BF16),
        ),
        compiler_params=vmem(24),
        name="merge",
    )(text, images, cosine, sine)


def attend_kernel(step, place, keys, values, query_ref, out_ref, stacked, scores, top, mixed):
    z_at, y_at = place[0], place[1]
    block_at = lax.rem(y_at + step, 4)
    for h in range(GROUP):
        stacked[h * TOK : (h + 1) * TOK, :] = query_ref[:, h * HEAD : (h + 1) * HEAD]
    full = z_at + jnp.where(y_at < block_at, 1, 0)
    count = z_at + jnp.where(y_at <= block_at, 1, 0)
    plain = full // 2
    chunks = (count + 1) // 2
    top[...] = jnp.full(top.shape, NEG, F32)
    mixed[...] = jnp.zeros(mixed.shape, F32)

    def chunk_at(chunk):
        return pl.ds(pl.multiple_of(chunk * CHUNK, CHUNK), CHUNK)

    def score(chunk, masked):
        at = chunk_at(chunk)
        keys_now = keys[:, at]
        if masked:
            key_at = lax.broadcasted_iota(jnp.int32, (TOK, CHUNK), 1)
            low = jnp.where(key_at < TOK, key_at, key_at - TOK + 4 * TOK)
            query_at = lax.broadcasted_iota(jnp.int32, (TOK, CHUNK), 0)
            offset = ((2 * chunk - z_at) * 4 + y_at - block_at) * TOK
            allowed = low + offset <= query_at
        for h in range(GROUP):
            here = slice(h * TOK, (h + 1) * TOK)
            s = jnp.dot(stacked[here, :], keys_now, preferred_element_type=F32)
            if masked:
                s = jnp.where(allowed, s, -jnp.inf)
            scores[here, at] = s
            most = top[here, :]
            for lane in range(0, CHUNK, HEAD):
                most = jnp.maximum(most, s[:, lane : lane + HEAD])
            top[here, :] = most

    pl.loop(0, plain)(lambda chunk: score(chunk, False))

    @pl.when(chunks > plain)
    def last():
        score(plain, True)

    offset = jnp.max(top[...], axis=1, keepdims=True) * (SCALE * LOG2E)
    top[...] = jnp.broadcast_to(offset, top.shape)

    @pl.loop(0, chunks)
    def weigh(chunk):
        at = chunk_at(chunk)
        values_now = values[at, :]
        for h in range(GROUP):
            here = slice(h * TOK, (h + 1) * TOK)
            weights = jnp.exp2(scores[here, at] * (SCALE * LOG2E) - top[here, :1]).astype(BF16)
            mixed[here, :] += jnp.dot(weights, values_now, preferred_element_type=F32)

    lane = lax.broadcasted_iota(jnp.int32, (TOK, HEAD), 1)
    stats = jnp.zeros((TOK, HEAD), F32)
    for h in range(GROUP):
        here = slice(h * TOK, (h + 1) * TOK)
        total = mixed[here, HEAD:]
        some = total > 0.0
        safe = jnp.where(some, total, 1.0)
        out_ref[:TOK, h * HEAD : (h + 1) * HEAD] = (mixed[here, :HEAD] / safe).astype(BF16)
        level = jnp.where(some, top[here, :] + jnp.log2(safe), NEG)
        for part in range(3):
            piece = level.astype(BF16).astype(F32)
            stats = jnp.where(lane == 3 * h + part, piece, stats)
            level = level - piece
    out_ref[TOK:, :TOK] = stats.T[: ROWS - TOK].astype(BF16)
    out_ref[TOK:, TOK:] = jnp.zeros((ROWS - TOK, 2 * HEAD), BF16)


def attend(step, place, keys, values, queries):
    return pl.pallas_call(
        functools.partial(attend_kernel, step),
        out_shape=jax.ShapeDtypeStruct((ROWS, GROUP * HEAD), BF16),
        in_specs=[
            pl.BlockSpec(memory_space=pltpu.SMEM),
            *[pl.BlockSpec(memory_space=pltpu.VMEM)] * 3,
        ],
        scratch_shapes=[
            pltpu.VMEM((ROWS_Q, HEAD), BF16),
            pltpu.VMEM((ROWS_Q, KEYS), F32),
            pltpu.VMEM((ROWS_Q, HEAD), F32),
            pltpu.VMEM((ROWS_Q, 2 * HEAD), F32),
        ],
        compiler_params=vmem(40),
        cost_estimate=pl.CostEstimate(
            flops=4 * ROWS_Q * KEYS * HEAD, bytes_accessed=2 << 20, transcendentals=ROWS_Q * KEYS
        ),
        name="attend",
    )(place, keys, values, queries)


def layer_norm(values, norm_scale, norm_shift):
    widened = values.astype(F32)
    center = jnp.mean(widened, axis=-1, keepdims=True)
    spread = jnp.mean(jnp.square(widened - center), axis=-1, keepdims=True)
    return ((widened - center) * lax.rsqrt(spread + 1e-06) * norm_scale + norm_shift).astype(BF16)


def combine_kernel(*refs):
    out_ref = refs[-1]
    levels = []
    for ref in refs[:-1]:
        rows = ref[TOK:, :TOK].astype(F32)
        levels.append(jnp.concatenate([rows, jnp.zeros((HEAD - rows.shape[0], TOK), F32)], 0).T)
    for h in range(GROUP):
        lanes = slice(h * HEAD, (h + 1) * HEAD)
        level = [
            l[:, 3 * h : 3 * h + 1] + l[:, 3 * h + 1 : 3 * h + 2] + l[:, 3 * h + 2 : 3 * h + 3]
            for l in levels
        ]
        most = functools.reduce(jnp.maximum, level)
        weights = [jnp.exp2(l - most) for l in level]
        total = sum(weights)
        mixed = sum(w * ref[:TOK, lanes].astype(F32) for w, ref in zip(weights, refs[:-1]))
        out_ref[:, lanes] = (mixed / total).astype(BF16)


def combine(parts):
    return pl.pallas_call(
        combine_kernel,
        out_shape=jax.ShapeDtypeStruct((TOK, GROUP * HEAD), BF16),
        name="combine",
    )(*parts)


def body(
    patches,
    patch_gain,
    patch_shift,
    encoder_up,
    encoder_down,
    proj_weight,
    hidden_text,
    slot_source,
    norm_gain,
    kv_weight,
    queries,
):
    z_at, y_at = lax.axis_index(Z), lax.axis_index("y")
    x_at, core = lax.axis_index("x"), lax.axis_index("core")

    give, keep = project(text_project_kernel, [hidden_text], norm_gain, kv_weight, core, TOK, [])
    text_rows = scatter_rows(give, keep, slot_source, x_at, ROWS)
    text_all = lax.all_to_all(text_rows, Z, 0, 0, tiled=True)

    normed_patches = layer_norm(patches, patch_gain, patch_shift)
    enc_hidden = jax.nn.gelu(
        jnp.dot(normed_patches, encoder_up, preferred_element_type=F32), approximate=False
    ).astype(BF16)
    partial_out = jnp.dot(enc_hidden, encoder_down, preferred_element_type=F32).astype(BF16)
    halves = partial_out.reshape(2, HALF, -1)
    half = pick(halves, core).astype(F32) + shift(pick(halves, 1 - core), "core", 1).astype(F32)
    sent = half.astype(BF16)
    for step in (2, 1, 3):
        half = half + shift(sent, "x", step).astype(F32)
    half = (half + pick(patches.reshape(2, HALF, -1), core).astype(F32)).astype(BF16)
    other = shift(half, "core", 1)

    give, keep = project(
        image_project_kernel,
        [half, other, proj_weight],
        norm_gain,
        kv_weight,
        core,
        IMG,
        [pltpu.VMEM(patches.shape, BF16)],
    )
    image_rows = scatter_rows(give, keep, slot_source, x_at, TOK)
    images_all = lax.all_to_all(image_rows, Z, 0, 0, tiled=True)

    frequencies = jnp.exp(
        jnp.arange(HALF, dtype=F32) * (-2.0 * math.log(500000.0) / (2 * HALF))
    )
    index = jnp.arange(KEYS, dtype=jnp.int32)
    positions = ((index // TOK) * 4 + y_at) * TOK + index % TOK
    angles = positions.astype(F32)[None, :] * frequencies[:, None]
    keys, values = merge(text_all, images_all, jnp.cos(angles), jnp.sin(angles))
    place = jnp.stack([z_at, y_at]).astype(jnp.int32)
    received = []
    for step in (2, 1, 3):
        asked = shift(queries, "y", 4 - step)
        received.append(shift(attend(step, place, keys, values, asked), "y", step))
    return combine([attend(0, place, keys, values, queries), *received])


def solution(mesh):
    split = Mesh(mesh.devices.reshape(4, 2, 4, 4, 2), ("zh", "zl", "y", "x", "core"))
    seq = ("zh", "zl", "y")
    in_specs = (
        P(seq, None),
        P(),
        P(),
        P(None, TP),
        P(TP, None),
        P(None, TP),
        P(seq, TP),
        P(seq),
        P(TP),
        P(None, TP),
        P(seq, TP),
    )
    return jax.shard_map(
        body, mesh=split, in_specs=in_specs, out_specs=P(seq, TP), check_vma=False
    )
```

```python
import functools
import math

import jax
import jax.numpy as jnp
from jax import lax
from jax.experimental import pallas as pl
from jax.experimental.pallas import tpu as pltpu
from jax.sharding import Mesh
from jax.sharding import PartitionSpec as P

D = 8192
HEAD = 128
HALF = 64
GROUP = 4
TOK = 256
IMG = 128
ROWS = 272
TP = ("x", "core")
Z = ("zh", "zl")
BF16 = jnp.bfloat16
F32 = jnp.float32
NEG = -1e30
LOG2E = math.log2(math.e)
KEYS = 2048
CHUNK = 512
ROWS_Q = GROUP * TOK
SCALE = HEAD ** (-0.5)


def shift(values, axis, step):
    count = lax.axis_size(axis)
    return lax.ppermute(values, axis, [(i, (i + step) % count) for i in range(count)])


def pick(values, index):
    return lax.dynamic_index_in_dim(values, index, 0, keepdims=False)


def vmem(mib):
    return pltpu.CompilerParams(vmem_limit_bytes=mib * 1024 * 1024)


def split_squares(column, count):
    row = jnp.broadcast_to(column, (count, HEAD)).T[:16]
    high = row.astype(BF16).astype(F32)
    at = lax.broadcasted_iota(jnp.int32, row.shape, 0)
    return jnp.where(at == 0, high, jnp.where(at == 1, row - high, 0.0)).astype(BF16)


def head_rows(step, features, tail, weight_ref, give_ref, keep_ref):
    rows = lax.dot_general(
        weight_ref[...], features[...], (((1,), (1,)), ((), ())), preferred_element_type=F32
    ).astype(BF16)

    @pl.when(step < 4)
    def to_other_core():
        give_ref[0, :TOK, :] = rows
        give_ref[0, TOK:, :] = tail[...]

    @pl.when(step >= 4)
    def own_core():
        keep_ref[0, :TOK, :] = rows
        keep_ref[0, TOK:, :] = tail[...]


def gain_features(features, gain_ref, gained, tail):
    widened = features.astype(F32)
    squares = jnp.sum(jnp.square(widened), axis=1, keepdims=True)
    tail[...] = split_squares(squares, features.shape[0])
    gained[...] = (widened * gain_ref[...]).astype(BF16)


def text_project_kernel(core, hidden_ref, gain_ref, weight_ref, give_ref, keep_ref, gained, tail):
    step = pl.program_id(0)

    @pl.when(step == 0)
    def first():
        gain_features(hidden_ref[...], gain_ref, gained, tail)

    head_rows(step, gained, tail, weight_ref, give_ref, keep_ref)


def image_project_kernel(
    core, half_ref, other_ref, proj_ref, gain_ref, weight_ref, give_ref, keep_ref, encoded, gained, tail
):
    step = pl.program_id(0)

    @pl.when(step == 0)
    def first():
        @pl.when(core[0] == 0)
        def low():
            encoded[:HALF, :] = half_ref[...]
            encoded[HALF:, :] = other_ref[...]

        @pl.when(core[0] == 1)
        def high():
            encoded[:HALF, :] = other_ref[...]
            encoded[HALF:, :] = half_ref[...]

        image = jnp.dot(encoded[...], proj_ref[...], preferred_element_type=F32).astype(BF16)
        gain_features(image, gain_ref, gained, tail)

    head_rows(step, gained, tail, weight_ref, give_ref, keep_ref)


def project(kernel, features, norm_gain, kv_weight, core, count, scratch):
    whole = lambda step, core: (0, 0)
    mine = jnp.reshape(core, (1,)).astype(jnp.int32)

    def head(step, core):
        x_at = jnp.where(step < 4, step, step - 4)
        return (2 * x_at + jnp.where(step < 4, 1 - core[0], core[0]), 0)

    shape = jax.ShapeDtypeStruct((4, ROWS, count), BF16)
    return pl.pallas_call(
        kernel,
        out_shape=(shape, shape),
        grid_spec=pltpu.PrefetchScalarGridSpec(
            num_scalar_prefetch=1,
            grid=(8,),
            in_specs=[
                *[pl.BlockSpec(f.shape, whole) for f in features],
                pl.BlockSpec((1, norm_gain.shape[0]), whole),
                pl.BlockSpec((TOK, kv_weight.shape[1]), head),
            ],
            out_specs=(
                pl.BlockSpec((1, ROWS, count), lambda step, core: (jnp.minimum(step, 3), 0, 0)),
                pl.BlockSpec((1, ROWS, count), lambda step, core: (jnp.maximum(step, 4) - 4, 0, 0)),
            ),
            scratch_shapes=[
                *scratch,
                pltpu.VMEM((count, kv_weight.shape[1]), BF16),
                pltpu.VMEM((16, count), BF16),
            ],
        ),
        compiler_params=vmem(56),
    )(mine, *features, norm_gain[None, :], kv_weight)


def pair_kernel(place, keep_ref, got_ref, own_ref, two_ref, one_ref, three_ref):
    for step, ref in ((2, two_ref), (1, one_ref), (3, three_ref), (0, own_ref)):
        at = lax.rem(place[0] + step, 4)
        total = keep_ref[at].astype(F32) + got_ref[at].astype(F32)
        ref[...] = total.astype(ref.dtype)


def add_pair(keep, got, x_at):
    part = keep.shape[1:]
    return pl.pallas_call(
        pair_kernel,
        out_shape=(jax.ShapeDtypeStruct(part, F32), *[jax.ShapeDtypeStruct(part, BF16)] * 3),
        in_specs=[
            pl.BlockSpec(memory_space=pltpu.SMEM),
            *[pl.BlockSpec(memory_space=pltpu.VMEM)] * 2,
        ],
        compiler_params=vmem(6),
        name="add_pair",
    )(jnp.reshape(x_at, (1,)).astype(jnp.int32), keep, got)


def finish_kernel(slots, *refs):
    *inputs, out_ref = refs
    total = inputs[0][...]
    for ref in inputs[1:]:
        total = total + ref[...].astype(F32)
    inverse = lax.rsqrt((total[TOK : TOK + 1] + total[TOK + 1 : TOK + 2]) / D + 1e-05)
    rows = (total[:TOK] * inverse).astype(BF16)
    for copy in range(8):
        out_ref[copy, :TOK, :] = rows
    if out_ref.shape[1] > TOK:
        lane = lax.broadcasted_iota(jnp.int32, (ROWS - TOK, out_ref.shape[2]), 1)
        source = jnp.where(lane < IMG, slots[0], slots[1]).astype(F32).astype(BF16)
        for copy in range(8):
            out_ref[copy, TOK:, :] = source


def finish_rows(slots, pieces, row_count):
    count = pieces[0].shape[1]
    return pl.pallas_call(
        finish_kernel,
        out_shape=jax.ShapeDtypeStruct((8, row_count, count), BF16),
        in_specs=[
            pl.BlockSpec(memory_space=pltpu.SMEM),
            *[pl.BlockSpec(memory_space=pltpu.VMEM)] * 4,
        ],
        compiler_params=vmem(6),
        name="finish_rows",
    )(slots, *pieces)


def exchange(pieces):
    own, two, one, three = pieces
    return [own, shift(two, "x", 2), shift(one, "x", 1), shift(three, "x", 3)]


def merge_kernel(text_ref, image_ref, cos_ref, sin_ref, keys, values):
    values[:, HEAD:] = jnp.ones((KEYS, HEAD), BF16)
    for block in range(8):
        for slot in range(2):
            lanes = slice(slot * IMG, (slot + 1) * IMG)
            here = slice(block * TOK + slot * IMG, block * TOK + (slot + 1) * IMG)
            text = text_ref[block, :, lanes].astype(F32)
            source = text[TOK : TOK + 1, :]
            rows = text[:TOK, :]
            for r in range(4):
                rows = jnp.where(
                    source == float(r), image_ref[2 * r + block % 2].astype(F32), rows
                )
            cosine, sine = cos_ref[:, here] * (SCALE * LOG2E), sin_ref[:, here] * (SCALE * LOG2E)
            first, second = rows[:HALF], rows[HALF:HEAD]
            keys[:HALF, here] = (first * cosine - second * sine).astype(BF16)
            keys[HALF:, here] = (second * cosine + first * sine).astype(BF16)
            values[here, :HEAD] = rows[HEAD:].T.astype(BF16)


def merge(text, images, cosine, sine):
    return pl.pallas_call(
        merge_kernel,
        out_shape=(
            jax.ShapeDtypeStruct((HEAD, KEYS), BF16),
            jax.ShapeDtypeStruct((KEYS, 2 * HEAD), BF16),
        ),
        compiler_params=vmem(10),
        name="merge",
    )(text, images, cosine, sine)


def attend_kernel(step, place, keys, values, query_ref, out_ref, stacked, scores, top, mixed):
    z_at, y_at = place[0], place[1]
    block_at = lax.rem(y_at + step, 4)
    for h in range(GROUP):
        stacked[h * TOK : (h + 1) * TOK, :] = query_ref[:, h * HEAD : (h + 1) * HEAD]
    full = z_at + jnp.where(y_at < block_at, 1, 0)
    count = z_at + jnp.where(y_at <= block_at, 1, 0)
    plain = full // 2
    chunks = (count + 1) // 2
    top[...] = jnp.full(top.shape, NEG, F32)
    mixed[...] = jnp.zeros(mixed.shape, F32)

    def chunk_at(chunk):
        return pl.ds(pl.multiple_of(chunk * CHUNK, CHUNK), CHUNK)

    def score(chunk, masked):
        at = chunk_at(chunk)
        keys_now = keys[:, at]
        if masked:
            key_at = lax.broadcasted_iota(jnp.int32, (TOK, CHUNK), 1)
            low = jnp.where(key_at < TOK, key_at, key_at - TOK + 4 * TOK)
            query_at = lax.broadcasted_iota(jnp.int32, (TOK, CHUNK), 0)
            offset = ((2 * chunk - z_at) * 4 + y_at - block_at) * TOK
            allowed = low + offset <= query_at
        for h in range(GROUP):
            here = slice(h * TOK, (h + 1) * TOK)
            s = jnp.dot(stacked[here, :], keys_now, preferred_element_type=F32)
            if masked:
                s = jnp.where(allowed, s, -jnp.inf)
            scores[here, at] = s
            most = top[here, :]
            for lane in range(0, CHUNK, HEAD):
                most = jnp.maximum(most, s[:, lane : lane + HEAD])
            top[here, :] = most

    pl.loop(0, plain)(lambda chunk: score(chunk, False))

    @pl.when(chunks > plain)
    def last():
        score(plain, True)

    offset = jnp.max(top[...], axis=1, keepdims=True)
    top[...] = jnp.broadcast_to(offset, top.shape)

    @pl.loop(0, chunks)
    def weigh(chunk):
        at = chunk_at(chunk)
        values_now = values[at, :]
        for h in range(GROUP):
            here = slice(h * TOK, (h + 1) * TOK)
            weights = jnp.exp2(scores[here, at] - top[here, :1]).astype(BF16)
            mixed[here, :] += jnp.dot(weights, values_now, preferred_element_type=F32)

    lane = lax.broadcasted_iota(jnp.int32, (TOK, HEAD), 1)
    stats = jnp.zeros((TOK, HEAD), F32)
    for h in range(GROUP):
        here = slice(h * TOK, (h + 1) * TOK)
        total = mixed[here, HEAD:]
        some = total > 0.0
        safe = jnp.where(some, total, 1.0)
        out_ref[:TOK, h * HEAD : (h + 1) * HEAD] = (mixed[here, :HEAD] / safe).astype(BF16)
        level = jnp.where(some, top[here, :] + jnp.log2(safe), NEG)
        for part in range(3):
            piece = level.astype(BF16).astype(F32)
            stats = jnp.where(lane == 3 * h + part, piece, stats)
            level = level - piece
    out_ref[TOK:, :TOK] = stats.T[: ROWS - TOK].astype(BF16)
    out_ref[TOK:, TOK:] = jnp.zeros((ROWS - TOK, 2 * HEAD), BF16)


def attend(step, place, keys, values, queries):
    return pl.pallas_call(
        functools.partial(attend_kernel, step),
        out_shape=jax.ShapeDtypeStruct((ROWS, GROUP * HEAD), BF16),
        in_specs=[
            pl.BlockSpec(memory_space=pltpu.SMEM),
            *[pl.BlockSpec(memory_space=pltpu.VMEM)] * 3,
        ],
        scratch_shapes=[
            pltpu.VMEM((ROWS_Q, HEAD), BF16),
            pltpu.VMEM((ROWS_Q, KEYS), F32),
            pltpu.VMEM((ROWS_Q, HEAD), F32),
            pltpu.VMEM((ROWS_Q, 2 * HEAD), F32),
        ],
        compiler_params=vmem(24),
        cost_estimate=pl.CostEstimate(
            flops=4 * ROWS_Q * KEYS * HEAD, bytes_accessed=2 << 20, transcendentals=ROWS_Q * KEYS
        ),
        name="attend",
    )(place, keys, values, queries)


def layer_norm(values, norm_scale, norm_shift):
    widened = values.astype(F32)
    center = jnp.mean(widened, axis=-1, keepdims=True)
    spread = jnp.mean(jnp.square(widened - center), axis=-1, keepdims=True)
    return ((widened - center) * lax.rsqrt(spread + 1e-06) * norm_scale + norm_shift).astype(BF16)


def combine_kernel(*refs):
    *parts, out_ref = refs
    levels = []
    for ref in parts:
        rows = ref[TOK:, :TOK].astype(F32)
        levels.append(
            [rows[3 * h : 3 * h + 1] + rows[3 * h + 1 : 3 * h + 2] + rows[3 * h + 2 : 3 * h + 3] for h in range(GROUP)]
        )
    weights = []
    for h in range(GROUP):
        most = functools.reduce(jnp.maximum, [level[h] for level in levels])
        raised = [jnp.exp2(level[h] - most) for level in levels]
        total = sum(raised)
        weights += [r / total for r in raised]
    rows = jnp.concatenate([*weights, jnp.zeros((HEAD - len(weights), TOK), F32)], 0).T
    for h in range(GROUP):
        lanes = slice(h * HEAD, (h + 1) * HEAD)
        mixed = sum(
            rows[:, 4 * h + i : 4 * h + i + 1] * ref[:TOK, lanes].astype(F32)
            for i, ref in enumerate(parts)
        )
        out_ref[:, lanes] = mixed.astype(BF16)


def combine(parts):
    return pl.pallas_call(
        combine_kernel,
        out_shape=jax.ShapeDtypeStruct((TOK, GROUP * HEAD), BF16),
        compiler_params=vmem(6),
        name="combine",
    )(*parts)


def body(
    patches,
    patch_gain,
    patch_shift,
    encoder_up,
    encoder_down,
    proj_weight,
    hidden_text,
    slot_source,
    norm_gain,
    kv_weight,
    queries,
):
    z_at, y_at = lax.axis_index(Z), lax.axis_index("y")
    x_at, core = lax.axis_index("x"), lax.axis_index("core")

    give, keep = project(text_project_kernel, [hidden_text], norm_gain, kv_weight, core, TOK, [])
    patches, give, keep = lax.optimization_barrier((patches, give, keep))
    text_pieces = add_pair(keep, shift(give, "core", 1), x_at)

    normed_patches = layer_norm(patches, patch_gain, patch_shift)
    enc_hidden = jax.nn.gelu(
        jnp.dot(normed_patches, encoder_up, preferred_element_type=F32), approximate=False
    ).astype(BF16)
    partial_out = jnp.dot(enc_hidden, encoder_down, preferred_element_type=F32).astype(BF16)
    halves = partial_out.reshape(2, HALF, -1)
    half = pick(halves, core).astype(F32) + shift(pick(halves, 1 - core), "core", 1).astype(F32)
    half, text_pieces = lax.optimization_barrier((half, text_pieces))
    text_got = exchange(text_pieces)
    sent = half.astype(BF16)
    for step in (2, 1, 3):
        half = half + shift(sent, "x", step).astype(F32)
    half = (half + pick(patches.reshape(2, HALF, -1), core).astype(F32)).astype(BF16)
    text_rows = finish_rows(slot_source, text_got, ROWS)
    half, text_rows = lax.optimization_barrier((half, text_rows))
    text_all = lax.all_to_all(text_rows, Z, 0, 0, tiled=True)
    other = shift(half, "core", 1)

    give, keep = project(
        image_project_kernel,
        [half, other, proj_weight],
        norm_gain,
        kv_weight,
        core,
        IMG,
        [pltpu.VMEM(patches.shape, BF16)],
    )
    asked = {step: shift(queries, "y", 4 - step) for step in (2, 1, 3)}
    image_got = exchange(add_pair(keep, shift(give, "core", 1), x_at))
    image_rows = finish_rows(slot_source, image_got, TOK)
    image_rows, text_all, asked = lax.optimization_barrier((image_rows, text_all, asked))
    images_all = lax.all_to_all(image_rows, Z, 0, 0, tiled=True)

    frequencies = jnp.exp(
        jnp.arange(HALF, dtype=F32) * (-2.0 * math.log(500000.0) / (2 * HALF))
    )
    index = jnp.arange(KEYS, dtype=jnp.int32)
    positions = ((index // TOK) * 4 + y_at) * TOK + index % TOK
    angles = positions.astype(F32)[None, :] * frequencies[:, None]
    keys, values = merge(text_all, images_all, jnp.cos(angles), jnp.sin(angles))
    place = jnp.stack([z_at, y_at]).astype(jnp.int32)
    received = []
    for step in (2, 1, 3):
        received.append(shift(attend(step, place, keys, values, asked[step]), "y", step))
    return combine([attend(0, place, keys, values, queries), *received])


def solution(mesh):
    split = Mesh(mesh.devices.reshape(4, 2, 4, 4, 2), ("zh", "zl", "y", "x", "core"))
    seq = ("zh", "zl", "y")
    in_specs = (
        P(seq, None),
        P(),
        P(),
        P(None, TP),
        P(TP, None),
        P(None, TP),
        P(seq, TP),
        P(seq),
        P(TP),
        P(None, TP),
        P(seq, TP),
    )
    return jax.shard_map(
        body, mesh=split, in_specs=in_specs, out_specs=P(seq, TP), check_vma=False
    )
```

```python
import functools
import math

import jax
import jax.numpy as jnp
from jax import lax
from jax.experimental import pallas as pl
from jax.experimental.pallas import tpu as pltpu
from jax.sharding import Mesh
from jax.sharding import PartitionSpec as P

D = 8192
HEAD = 128
HALF = 64
GROUP = 4
TOK = 256
IMG = 128
ROWS = 272
TP = ("x", "core")
Z = ("zh", "zl")
BF16 = jnp.bfloat16
F32 = jnp.float32
NEG = -1e30
LOG2E = math.log2(math.e)
KEYS = 2048
CHUNK = 1024
PER = CHUNK // TOK
ROWS_Q = GROUP * TOK
SCALE = HEAD ** (-0.5)


def shift(values, axis, step):
    count = lax.axis_size(axis)
    return lax.ppermute(values, axis, [(i, (i + step) % count) for i in range(count)])


def pick(values, index):
    return lax.dynamic_index_in_dim(values, index, 0, keepdims=False)


def vmem(mib):
    return pltpu.CompilerParams(vmem_limit_bytes=mib * 1024 * 1024)


def split_squares(column, count):
    row = jnp.broadcast_to(column, (count, HEAD)).T[:16]
    high = row.astype(BF16).astype(F32)
    at = lax.broadcasted_iota(jnp.int32, row.shape, 0)
    return jnp.where(at == 0, high, jnp.where(at == 1, row - high, 0.0)).astype(BF16)


def head_rows(core, features, tail, weight_ref, give_ref, keep_ref):
    for x_at in range(4):
        for own, ref in ((0, give_ref), (1, keep_ref)):
            head = 2 * x_at + jnp.where(own == 1, core, 1 - core)
            weight = weight_ref[pl.ds(pl.multiple_of(head * TOK, TOK), TOK), :]
            rows = lax.dot_general(
                weight, features, (((1,), (1,)), ((), ())), preferred_element_type=F32
            )
            ref[x_at, :TOK, :] = rows.astype(BF16)
            ref[x_at, TOK:, :] = tail


def gain_features(features, gain_ref):
    widened = features.astype(F32)
    squares = jnp.sum(jnp.square(widened), axis=1, keepdims=True)
    return (widened * gain_ref[...]).astype(BF16), split_squares(squares, features.shape[0])


def text_project_kernel(core, hidden_ref, gain_ref, weight_ref, give_ref, keep_ref):
    gained, tail = gain_features(hidden_ref[...], gain_ref)
    head_rows(core[0], gained, tail, weight_ref, give_ref, keep_ref)


def image_project_kernel(
    core, half_ref, other_ref, proj_ref, gain_ref, weight_ref, give_ref, keep_ref, encoded
):
    at = pl.multiple_of(core[0] * HALF, HALF)
    encoded[pl.ds(at, HALF), :] = half_ref[...]
    encoded[pl.ds(HALF - at, HALF), :] = other_ref[...]
    image = jnp.dot(encoded[...], proj_ref[...], preferred_element_type=F32).astype(BF16)
    gained, tail = gain_features(image, gain_ref)
    head_rows(core[0], gained, tail, weight_ref, give_ref, keep_ref)


def project(kernel, features, norm_gain, kv_weight, core, count, scratch):
    mine = jnp.reshape(core, (1,)).astype(jnp.int32)
    shape = jax.ShapeDtypeStruct((4, ROWS, count), BF16)
    return pl.pallas_call(
        kernel,
        out_shape=(shape, shape),
        in_specs=[
            pl.BlockSpec(memory_space=pltpu.SMEM),
            *[pl.BlockSpec(memory_space=pltpu.VMEM)] * (len(features) + 2),
        ],
        scratch_shapes=scratch,
        compiler_params=vmem(8),
        name="project",
    )(mine, *features, norm_gain[None, :], kv_weight)


def pair_kernel(place, keep_ref, got_ref, own_ref, two_ref, one_ref, three_ref):
    for step, ref in ((2, two_ref), (1, one_ref), (3, three_ref), (0, own_ref)):
        at = lax.rem(place[0] + step, 4)
        total = keep_ref[at].astype(F32) + got_ref[at].astype(F32)
        ref[...] = total.astype(ref.dtype)


def add_pair(keep, got, x_at):
    part = keep.shape[1:]
    return pl.pallas_call(
        pair_kernel,
        out_shape=(jax.ShapeDtypeStruct(part, F32), *[jax.ShapeDtypeStruct(part, BF16)] * 3),
        in_specs=[
            pl.BlockSpec(memory_space=pltpu.SMEM),
            *[pl.BlockSpec(memory_space=pltpu.VMEM)] * 2,
        ],
        compiler_params=vmem(6),
        name="add_pair",
    )(jnp.reshape(x_at, (1,)).astype(jnp.int32), keep, got)


def finish_kernel(slots, *refs):
    *inputs, out_ref = refs
    total = inputs[0][...]
    for ref in inputs[1:]:
        total = total + ref[...].astype(F32)
    inverse = lax.rsqrt((total[TOK : TOK + 1] + total[TOK + 1 : TOK + 2]) / D + 1e-05)
    rows = (total[:TOK] * inverse).astype(BF16)
    for copy in range(8):
        out_ref[copy, :TOK, :] = rows
    if out_ref.shape[1] > TOK:
        lane = lax.broadcasted_iota(jnp.int32, (ROWS - TOK, out_ref.shape[2]), 1)
        source = jnp.where(lane < IMG, slots[0], slots[1]).astype(F32).astype(BF16)
        for copy in range(8):
            out_ref[copy, TOK:, :] = source


def finish_rows(slots, pieces, row_count):
    count = pieces[0].shape[1]
    return pl.pallas_call(
        finish_kernel,
        out_shape=jax.ShapeDtypeStruct((8, row_count, count), BF16),
        in_specs=[
            pl.BlockSpec(memory_space=pltpu.SMEM),
            *[pl.BlockSpec(memory_space=pltpu.VMEM)] * 4,
        ],
        compiler_params=vmem(6),
        name="finish_rows",
    )(slots, *pieces)


def exchange(pieces):
    own, two, one, three = pieces
    return [own, shift(two, "x", 2), shift(one, "x", 1), shift(three, "x", 3)]


def merge_kernel(text_ref, image_ref, cos_ref, sin_ref, keys, values):
    values[:, HEAD:] = jnp.ones((KEYS, HEAD), BF16)
    for block in range(8):
        for slot in range(2):
            lanes = slice(slot * IMG, (slot + 1) * IMG)
            here = slice(block * TOK + slot * IMG, block * TOK + (slot + 1) * IMG)
            text = text_ref[block, :, lanes].astype(F32)
            source = text[TOK : TOK + 1, :]
            rows = text[:TOK, :]
            for r in range(4):
                rows = jnp.where(
                    source == float(r), image_ref[2 * r + block % 2].astype(F32), rows
                )
            inner_cos, inner_sin = cos_ref[:, lanes], sin_ref[:, lanes]
            outer_cos = cos_ref[:, TOK + block : TOK + block + 1]
            outer_sin = sin_ref[:, TOK + block : TOK + block + 1]
            cosine = inner_cos * outer_cos - inner_sin * outer_sin
            sine = inner_sin * outer_cos + inner_cos * outer_sin
            first, second = rows[:HALF], rows[HALF:HEAD]
            keys[:HALF, here] = (first * cosine - second * sine).astype(BF16)
            keys[HALF:, here] = (second * cosine + first * sine).astype(BF16)
            values[here, :HEAD] = rows[HEAD:].T.astype(BF16)


def merge(text, images, cosine, sine):
    return pl.pallas_call(
        merge_kernel,
        out_shape=(
            jax.ShapeDtypeStruct((HEAD, KEYS), BF16),
            jax.ShapeDtypeStruct((KEYS, 2 * HEAD), BF16),
        ),
        compiler_params=vmem(10),
        name="merge",
    )(text, images, cosine, sine)


def attend_kernel(step, place, keys, values, query_ref, out_ref, scores, top, mixed):
    z_at, y_at = place[0], place[1]
    block_at = lax.rem(y_at + step, 4)
    full = z_at + jnp.where(y_at < block_at, 1, 0)
    count = z_at + jnp.where(y_at <= block_at, 1, 0)
    plain = full // PER
    chunks = (count + PER - 1) // PER
    top[...] = jnp.full(top.shape, NEG, F32)

    def chunk_at(chunk, offset=0, size=CHUNK):
        return pl.ds(pl.multiple_of(chunk * CHUNK + offset, HEAD), size)

    def score(chunk, masked):
        keys_now = keys[:, chunk_at(chunk)]
        if masked:
            key_at = lax.broadcasted_iota(jnp.int32, (TOK, CHUNK), 1)
            key_at = key_at + (key_at // TOK) * (3 * TOK)
            query_at = lax.broadcasted_iota(jnp.int32, (TOK, CHUNK), 0)
            offset = ((PER * chunk - z_at) * 4 + y_at - block_at) * TOK
            allowed = key_at + offset <= query_at
        for h in range(GROUP):
            here = slice(h * TOK, (h + 1) * TOK)
            s = jnp.dot(
                query_ref[:, h * HEAD : (h + 1) * HEAD], keys_now, preferred_element_type=F32
            )
            if masked:
                s = jnp.where(allowed, s, -jnp.inf)
            scores[here, chunk_at(chunk)] = s
            most = top[here, :]
            for lane in range(0, CHUNK, HEAD):
                most = jnp.maximum(most, s[:, lane : lane + HEAD])
            top[here, :] = most

    pl.loop(0, plain)(lambda chunk: score(chunk, False))

    @pl.when(chunks > plain)
    def last():
        score(plain, True)

    top[...] = jnp.broadcast_to(jnp.max(top[...], axis=1, keepdims=True), top.shape)

    def weigh(chunk, first):
        values_now = values[chunk_at(chunk), :]
        for h in range(GROUP):
            here = slice(h * TOK, (h + 1) * TOK)
            most = top[here, :]
            weights = jnp.concatenate(
                [
                    jnp.exp2(scores[here, chunk_at(chunk, lane, HEAD)] - most).astype(BF16)
                    for lane in range(0, CHUNK, HEAD)
                ],
                1,
            )
            rows = jnp.dot(weights, values_now, preferred_element_type=F32)
            mixed[here, :] = rows if first else mixed[here, :] + rows

    @pl.when(chunks > 0)
    def some_keys():
        weigh(0, True)

    @pl.when(chunks == 0)
    def no_keys():
        mixed[...] = jnp.zeros(mixed.shape, F32)

    pl.loop(1, chunks)(lambda chunk: weigh(chunk, False))

    lane = lax.broadcasted_iota(jnp.int32, (TOK, HEAD), 1)
    stats = jnp.zeros((TOK, HEAD), F32)
    for h in range(GROUP):
        here = slice(h * TOK, (h + 1) * TOK)
        total = mixed[here, HEAD:]
        safe = jnp.where(total > 0.0, total, 1.0)
        out_ref[:TOK, h * HEAD : (h + 1) * HEAD] = (mixed[here, :HEAD] / safe).astype(BF16)
        stats = jnp.where(lane == h, top[here, :], jnp.where(lane == GROUP + h, total, stats))
    rows = stats.T
    tops, totals = rows[:GROUP], rows[GROUP : 2 * GROUP]
    some = totals > 0.0
    level = jnp.where(some, tops + jnp.log2(jnp.where(some, totals, 1.0)), NEG)
    high = level.astype(BF16).astype(F32)
    middle = (level - high).astype(BF16).astype(F32)
    low = level - high - middle
    pad = jnp.zeros((ROWS - TOK - 3 * GROUP, TOK), F32)
    out_ref[TOK:, :TOK] = jnp.concatenate([high, middle, low, pad], 0).astype(BF16)
    out_ref[TOK:, TOK:] = jnp.zeros((ROWS - TOK, 2 * HEAD), BF16)


def attend(step, place, keys, values, queries):
    return pl.pallas_call(
        functools.partial(attend_kernel, step),
        out_shape=jax.ShapeDtypeStruct((ROWS, GROUP * HEAD), BF16),
        in_specs=[
            pl.BlockSpec(memory_space=pltpu.SMEM),
            *[pl.BlockSpec(memory_space=pltpu.VMEM)] * 3,
        ],
        scratch_shapes=[
            pltpu.VMEM((ROWS_Q, KEYS), F32),
            pltpu.VMEM((ROWS_Q, HEAD), F32),
            pltpu.VMEM((ROWS_Q, 2 * HEAD), F32),
        ],
        compiler_params=vmem(24),
        cost_estimate=pl.CostEstimate(
            flops=4 * ROWS_Q * KEYS * HEAD, bytes_accessed=2 << 20, transcendentals=ROWS_Q * KEYS
        ),
        name="attend",
    )(place, keys, values, queries)


def layer_norm(values, norm_scale, norm_shift):
    widened = values.astype(F32)
    center = jnp.mean(widened, axis=-1, keepdims=True)
    spread = jnp.mean(jnp.square(widened - center), axis=-1, keepdims=True)
    return ((widened - center) * lax.rsqrt(spread + 1e-06) * norm_scale + norm_shift).astype(BF16)


def combine_kernel(*refs):
    *parts, out_ref = refs
    levels = []
    for ref in parts:
        rows = ref[TOK:, :TOK].astype(F32)
        levels.append(
            [rows[h : h + 1] + rows[4 + h : 5 + h] + rows[8 + h : 9 + h] for h in range(GROUP)]
        )
    weights = []
    for h in range(GROUP):
        most = functools.reduce(jnp.maximum, [level[h] for level in levels])
        raised = [jnp.exp2(level[h] - most) for level in levels]
        total = sum(raised)
        weights += [r / total for r in raised]
    rows = jnp.concatenate([*weights, jnp.zeros((HEAD - len(weights), TOK), F32)], 0).T
    for h in range(GROUP):
        lanes = slice(h * HEAD, (h + 1) * HEAD)
        mixed = sum(
            rows[:, 4 * h + i : 4 * h + i + 1] * ref[:TOK, lanes].astype(F32)
            for i, ref in enumerate(parts)
        )
        out_ref[:, lanes] = mixed.astype(BF16)


def combine(parts):
    return pl.pallas_call(
        combine_kernel,
        out_shape=jax.ShapeDtypeStruct((TOK, GROUP * HEAD), BF16),
        compiler_params=vmem(6),
        name="combine",
    )(*parts)


def body(
    patches,
    patch_gain,
    patch_shift,
    encoder_up,
    encoder_down,
    proj_weight,
    hidden_text,
    slot_source,
    norm_gain,
    kv_weight,
    queries,
):
    z_at, y_at = lax.axis_index(Z), lax.axis_index("y")
    x_at, core = lax.axis_index("x"), lax.axis_index("core")

    give, keep = project(text_project_kernel, [hidden_text], norm_gain, kv_weight, core, TOK, [])
    text_pieces = add_pair(keep, shift(give, "core", 1), x_at)
    patches, text_pieces = lax.optimization_barrier((patches, text_pieces))
    text_got = exchange(text_pieces)

    normed_patches = layer_norm(patches, patch_gain, patch_shift)
    enc_hidden = jax.nn.gelu(
        jnp.dot(normed_patches, encoder_up, preferred_element_type=F32), approximate=False
    ).astype(BF16)
    partial_out = jnp.dot(enc_hidden, encoder_down, preferred_element_type=F32).astype(BF16)
    halves = partial_out.reshape(2, HALF, -1)
    half = pick(halves, core).astype(F32) + shift(pick(halves, 1 - core), "core", 1).astype(F32)
    sent = half.astype(BF16)
    for step in (2, 1, 3):
        half = half + shift(sent, "x", step).astype(F32)
    half = (half + pick(patches.reshape(2, HALF, -1), core).astype(F32)).astype(BF16)
    text_rows = finish_rows(slot_source, text_got, ROWS)
    half, text_rows = lax.optimization_barrier((half, text_rows))
    text_all = lax.all_to_all(text_rows, Z, 0, 0, tiled=True)
    other = shift(half, "core", 1)

    give, keep = project(
        image_project_kernel,
        [half, other, proj_weight],
        norm_gain,
        kv_weight,
        core,
        IMG,
        [pltpu.VMEM(patches.shape, BF16)],
    )
    asked = {step: shift(queries, "y", 4 - step) for step in (2, 1, 3)}
    image_got = exchange(add_pair(keep, shift(give, "core", 1), x_at))
    image_rows = finish_rows(slot_source, image_got, TOK)
    image_rows, text_all = lax.optimization_barrier((image_rows, text_all))
    images_all = lax.all_to_all(image_rows, Z, 0, 0, tiled=True)

    frequencies = jnp.exp(
        jnp.arange(HALF, dtype=F32) * (-2.0 * math.log(500000.0) / (2 * HALF))
    )
    lane = jnp.arange(TOK + HEAD, dtype=jnp.int32)
    positions = jnp.where(lane < TOK, lane, ((lane - TOK) * 4 + y_at) * TOK)
    angles = positions.astype(F32)[None, :] * frequencies[:, None]
    factor = jnp.where(lane < TOK, SCALE * LOG2E, 1.0)[None, :]
    tables = (jnp.cos(angles) * factor, jnp.sin(angles) * factor)
    keys, values = merge(text_all, images_all, *tables)
    place = jnp.stack([z_at, y_at]).astype(jnp.int32)
    received = []
    for step in (2, 1, 3):
        received.append(shift(attend(step, place, keys, values, asked[step]), "y", step))
    return combine([attend(0, place, keys, values, queries), *received])


def solution(mesh):
    split = Mesh(mesh.devices.reshape(4, 2, 4, 4, 2), ("zh", "zl", "y", "x", "core"))
    seq = ("zh", "zl", "y")
    in_specs = (
        P(seq, None),
        P(),
        P(),
        P(None, TP),
        P(TP, None),
        P(None, TP),
        P(seq, TP),
        P(seq),
        P(TP),
        P(None, TP),
        P(seq, TP),
    )
    return jax.shard_map(
        body, mesh=split, in_specs=in_specs, out_specs=P(seq, TP), check_vma=False
    )
```

```python
import functools
import math

import jax
import jax.numpy as jnp
from jax import lax
from jax.experimental import pallas as pl
from jax.experimental.pallas import tpu as pltpu
from jax.sharding import Mesh
from jax.sharding import PartitionSpec as P

D = 8192
HEAD = 128
HALF = 64
GROUP = 4
TOK = 256
IMG = 128
ROWS = 272
TP = ("x", "core")
Z = ("zh", "zl")
BF16 = jnp.bfloat16
F32 = jnp.float32
NEG = -1e30
LOG2E = math.log2(math.e)
WIDE = TOK + IMG
KEYS = 2048
CHUNK = 1024
PER = CHUNK // TOK
ROWS_Q = GROUP * TOK
SCALE = HEAD ** (-0.5)


def shift(values, axis, step):
    count = lax.axis_size(axis)
    return lax.ppermute(values, axis, [(i, (i + step) % count) for i in range(count)])


def pick(values, index):
    return lax.dynamic_index_in_dim(values, index, 0, keepdims=False)


def vmem(mib):
    return pltpu.CompilerParams(vmem_limit_bytes=mib * 1024 * 1024)


def split_squares(column, count):
    row = jnp.broadcast_to(column, (count, HEAD)).T[:16]
    high = row.astype(BF16).astype(F32)
    at = lax.broadcasted_iota(jnp.int32, row.shape, 0)
    return jnp.where(at == 0, high, jnp.where(at == 1, row - high, 0.0)).astype(BF16)


def head_rows(core, features, tail, weight_ref, give_ref, keep_ref):
    for x_at in range(4):
        for own, ref in ((0, give_ref), (1, keep_ref)):
            head = 2 * x_at + jnp.where(own == 1, core, 1 - core)
            weight = weight_ref[pl.ds(pl.multiple_of(head * TOK, TOK), TOK), :]
            rows = lax.dot_general(
                weight, features, (((1,), (1,)), ((), ())), preferred_element_type=F32
            )
            ref[x_at, :TOK, :] = rows.astype(BF16)
            ref[x_at, TOK:, :] = tail


def gain_features(features, gain_ref):
    widened = features.astype(F32)
    squares = jnp.sum(jnp.square(widened), axis=1, keepdims=True)
    return (widened * gain_ref[...]).astype(BF16), split_squares(squares, features.shape[0])


def text_project_kernel(core, hidden_ref, gain_ref, weight_ref, give_ref, keep_ref):
    gained, tail = gain_features(hidden_ref[...], gain_ref)
    head_rows(core[0], gained, tail, weight_ref, give_ref, keep_ref)


def image_project_kernel(
    core, half_ref, other_ref, proj_ref, gain_ref, weight_ref, give_ref, keep_ref, encoded
):
    at = pl.multiple_of(core[0] * HALF, HALF)
    encoded[pl.ds(at, HALF), :] = half_ref[...]
    encoded[pl.ds(HALF - at, HALF), :] = other_ref[...]
    image = jnp.dot(encoded[...], proj_ref[...], preferred_element_type=F32).astype(BF16)
    gained, tail = gain_features(image, gain_ref)
    head_rows(core[0], gained, tail, weight_ref, give_ref, keep_ref)


def project(kernel, features, norm_gain, kv_weight, core, count, scratch):
    mine = jnp.reshape(core, (1,)).astype(jnp.int32)
    shape = jax.ShapeDtypeStruct((4, ROWS, count), BF16)
    return pl.pallas_call(
        kernel,
        out_shape=(shape, shape),
        in_specs=[
            pl.BlockSpec(memory_space=pltpu.SMEM),
            *[pl.BlockSpec(memory_space=pltpu.VMEM)] * (len(features) + 2),
        ],
        scratch_shapes=scratch,
        compiler_params=vmem(8),
        name="project",
    )(mine, *features, norm_gain[None, :], kv_weight)


def pair_kernel(place, keep_ref, got_ref, own_ref, two_ref, one_ref, three_ref):
    for step, ref in ((2, two_ref), (1, one_ref), (3, three_ref), (0, own_ref)):
        at = lax.rem(place[0] + step, 4)
        total = keep_ref[at].astype(F32) + got_ref[at].astype(F32)
        ref[...] = total.astype(ref.dtype)


def add_pair(keep, got, x_at):
    part = keep.shape[1:]
    return pl.pallas_call(
        pair_kernel,
        out_shape=(jax.ShapeDtypeStruct(part, F32), *[jax.ShapeDtypeStruct(part, BF16)] * 3),
        in_specs=[
            pl.BlockSpec(memory_space=pltpu.SMEM),
            *[pl.BlockSpec(memory_space=pltpu.VMEM)] * 2,
        ],
        compiler_params=vmem(6),
        name="add_pair",
    )(jnp.reshape(x_at, (1,)).astype(jnp.int32), keep, got)


def finish_kernel(slots, *refs):
    *inputs, out_ref = refs
    for lanes, pieces in ((slice(0, TOK), inputs[:4]), (slice(TOK, WIDE), inputs[4:])):
        total = pieces[0][...]
        for ref in pieces[1:]:
            total = total + ref[...].astype(F32)
        inverse = lax.rsqrt((total[TOK : TOK + 1] + total[TOK + 1 : TOK + 2]) / D + 1e-05)
        out_ref[:TOK, lanes] = (total[:TOK] * inverse).astype(BF16)
    lane = lax.broadcasted_iota(jnp.int32, (ROWS - TOK, WIDE), 1)
    out_ref[TOK:, :] = jnp.where(lane < IMG, slots[0], slots[1]).astype(F32).astype(BF16)


def finish_rows(slots, text, image):
    return pl.pallas_call(
        finish_kernel,
        out_shape=jax.ShapeDtypeStruct((ROWS, WIDE), BF16),
        in_specs=[
            pl.BlockSpec(memory_space=pltpu.SMEM),
            *[pl.BlockSpec(memory_space=pltpu.VMEM)] * 8,
        ],
        compiler_params=vmem(6),
        name="finish_rows",
    )(slots, *text, *image)


def ring_gather(block):
    blocks, up, down = [block], block, block
    for _ in range(3):
        up, down = shift(up, Z, 1), shift(down, Z, 7)
        blocks += [up, down]
    return [*blocks, shift(up[:IMG], Z, 1), shift(down[IMG:], Z, 7)]


def exchange(pieces):
    own, two, one, three = pieces
    return [own, shift(two, "x", 2), shift(one, "x", 1), shift(three, "x", 3)]


def merge_kernel(place, *refs):
    *blocks, cos_ref, sin_ref, keys, values, gathered = refs
    for step, ref in zip((0, 7, 1, 6, 2, 5, 3), blocks):
        gathered[lax.rem(place[0] + step, 8)] = ref[...]
    far = lax.rem(place[0] + 4, 8)
    gathered[far, :IMG, :] = blocks[7][...]
    gathered[far, IMG:, :] = blocks[8][...]
    values[:, HEAD:] = jnp.ones((KEYS, HEAD), BF16)
    for block in range(8):
        for slot in range(2):
            lanes = slice(slot * IMG, (slot + 1) * IMG)
            here = slice(block * TOK + slot * IMG, block * TOK + (slot + 1) * IMG)
            text = gathered[block, :, lanes].astype(F32)
            source = text[TOK : TOK + 1, :]
            rows = text[:TOK, :]
            for r in range(4):
                image = gathered[2 * r + block % 2, :TOK, TOK:]
                rows = jnp.where(source == float(r), image.astype(F32), rows)
            inner_cos, inner_sin = cos_ref[:, lanes], sin_ref[:, lanes]
            outer_cos = cos_ref[:, TOK + block : TOK + block + 1]
            outer_sin = sin_ref[:, TOK + block : TOK + block + 1]
            cosine = inner_cos * outer_cos - inner_sin * outer_sin
            sine = inner_sin * outer_cos + inner_cos * outer_sin
            first, second = rows[:HALF], rows[HALF:HEAD]
            keys[:HALF, here] = (first * cosine - second * sine).astype(BF16)
            keys[HALF:, here] = (second * cosine + first * sine).astype(BF16)
            values[here, :HEAD] = rows[HEAD:].T.astype(BF16)


def merge(place, blocks, cosine, sine):
    return pl.pallas_call(
        merge_kernel,
        out_shape=(
            jax.ShapeDtypeStruct((HEAD, KEYS), BF16),
            jax.ShapeDtypeStruct((KEYS, 2 * HEAD), BF16),
        ),
        in_specs=[
            pl.BlockSpec(memory_space=pltpu.SMEM),
            *[pl.BlockSpec(memory_space=pltpu.VMEM)] * (len(blocks) + 2),
        ],
        scratch_shapes=[pltpu.VMEM((8, ROWS, WIDE), BF16)],
        compiler_params=vmem(10),
        name="merge",
    )(place, *blocks, cosine, sine)


def attend_kernel(step, place, keys, values, query_ref, out_ref, scores, top, mixed):
    z_at, y_at = place[0], place[1]
    block_at = lax.rem(y_at + step, 4)
    full = z_at + jnp.where(y_at < block_at, 1, 0)
    count = z_at + jnp.where(y_at <= block_at, 1, 0)
    plain = full // PER
    chunks = (count + PER - 1) // PER
    top[...] = jnp.full(top.shape, NEG, F32)

    def chunk_at(chunk, offset=0, size=CHUNK):
        return pl.ds(pl.multiple_of(chunk * CHUNK + offset, HEAD), size)

    def score(chunk, masked):
        keys_now = keys[:, chunk_at(chunk)]
        if masked:
            key_at = lax.broadcasted_iota(jnp.int32, (TOK, CHUNK), 1)
            key_at = key_at + (key_at // TOK) * (3 * TOK)
            query_at = lax.broadcasted_iota(jnp.int32, (TOK, CHUNK), 0)
            offset = ((PER * chunk - z_at) * 4 + y_at - block_at) * TOK
            allowed = key_at + offset <= query_at
        for h in range(GROUP):
            here = slice(h * TOK, (h + 1) * TOK)
            s = jnp.dot(
                query_ref[:, h * HEAD : (h + 1) * HEAD], keys_now, preferred_element_type=F32
            )
            if masked:
                s = jnp.where(allowed, s, -jnp.inf)
            scores[here, chunk_at(chunk)] = s
            most = top[here, :]
            for lane in range(0, CHUNK, HEAD):
                most = jnp.maximum(most, s[:, lane : lane + HEAD])
            top[here, :] = most

    pl.loop(0, plain)(lambda chunk: score(chunk, False))

    @pl.when(chunks > plain)
    def last():
        score(plain, True)

    top[...] = jnp.broadcast_to(jnp.max(top[...], axis=1, keepdims=True), top.shape)

    def weigh(chunk, first):
        values_now = values[chunk_at(chunk), :]
        for h in range(GROUP):
            here = slice(h * TOK, (h + 1) * TOK)
            most = top[here, :]
            weights = jnp.concatenate(
                [
                    jnp.exp2(scores[here, chunk_at(chunk, lane, HEAD)] - most).astype(BF16)
                    for lane in range(0, CHUNK, HEAD)
                ],
                1,
            )
            rows = jnp.dot(weights, values_now, preferred_element_type=F32)
            mixed[here, :] = rows if first else mixed[here, :] + rows

    @pl.when(chunks > 0)
    def some_keys():
        weigh(0, True)

    @pl.when(chunks == 0)
    def no_keys():
        mixed[...] = jnp.zeros(mixed.shape, F32)

    pl.loop(1, chunks)(lambda chunk: weigh(chunk, False))

    lane = lax.broadcasted_iota(jnp.int32, (TOK, HEAD), 1)
    stats = jnp.zeros((TOK, HEAD), F32)
    for h in range(GROUP):
        here = slice(h * TOK, (h + 1) * TOK)
        total = mixed[here, HEAD:]
        safe = jnp.where(total > 0.0, total, 1.0)
        out_ref[:TOK, h * HEAD : (h + 1) * HEAD] = (mixed[here, :HEAD] / safe).astype(BF16)
        stats = jnp.where(lane == h, top[here, :], jnp.where(lane == GROUP + h, total, stats))
    rows = stats.T
    tops, totals = rows[:GROUP], rows[GROUP : 2 * GROUP]
    some = totals > 0.0
    level = jnp.where(some, tops + jnp.log2(jnp.where(some, totals, 1.0)), NEG)
    high = level.astype(BF16).astype(F32)
    middle = (level - high).astype(BF16).astype(F32)
    low = level - high - middle
    pad = jnp.zeros((ROWS - TOK - 3 * GROUP, TOK), F32)
    out_ref[TOK:, :TOK] = jnp.concatenate([high, middle, low, pad], 0).astype(BF16)
    out_ref[TOK:, TOK:] = jnp.zeros((ROWS - TOK, 2 * HEAD), BF16)


def attend(step, place, keys, values, queries):
    return pl.pallas_call(
        functools.partial(attend_kernel, step),
        out_shape=jax.ShapeDtypeStruct((ROWS, GROUP * HEAD), BF16),
        in_specs=[
            pl.BlockSpec(memory_space=pltpu.SMEM),
            *[pl.BlockSpec(memory_space=pltpu.VMEM)] * 3,
        ],
        scratch_shapes=[
            pltpu.VMEM((ROWS_Q, KEYS), F32),
            pltpu.VMEM((ROWS_Q, HEAD), F32),
            pltpu.VMEM((ROWS_Q, 2 * HEAD), F32),
        ],
        compiler_params=vmem(24),
        cost_estimate=pl.CostEstimate(
            flops=4 * ROWS_Q * KEYS * HEAD, bytes_accessed=2 << 20, transcendentals=ROWS_Q * KEYS
        ),
        name="attend",
    )(place, keys, values, queries)


def layer_norm(values, norm_scale, norm_shift):
    widened = values.astype(F32)
    center = jnp.mean(widened, axis=-1, keepdims=True)
    spread = jnp.mean(jnp.square(widened - center), axis=-1, keepdims=True)
    return ((widened - center) * lax.rsqrt(spread + 1e-06) * norm_scale + norm_shift).astype(BF16)


def combine_kernel(*refs):
    *parts, out_ref = refs
    levels = []
    for ref in parts:
        rows = ref[TOK:, :TOK].astype(F32)
        levels.append(
            [rows[h : h + 1] + rows[4 + h : 5 + h] + rows[8 + h : 9 + h] for h in range(GROUP)]
        )
    weights = []
    for h in range(GROUP):
        most = functools.reduce(jnp.maximum, [level[h] for level in levels])
        raised = [jnp.exp2(level[h] - most) for level in levels]
        total = sum(raised)
        weights += [r / total for r in raised]
    rows = jnp.concatenate([*weights, jnp.zeros((HEAD - len(weights), TOK), F32)], 0).T
    for h in range(GROUP):
        lanes = slice(h * HEAD, (h + 1) * HEAD)
        mixed = sum(
            rows[:, 4 * h + i : 4 * h + i + 1] * ref[:TOK, lanes].astype(F32)
            for i, ref in enumerate(parts)
        )
        out_ref[:, lanes] = mixed.astype(BF16)


def combine(parts):
    return pl.pallas_call(
        combine_kernel,
        out_shape=jax.ShapeDtypeStruct((TOK, GROUP * HEAD), BF16),
        compiler_params=vmem(6),
        name="combine",
    )(*parts)


def body(
    patches,
    patch_gain,
    patch_shift,
    encoder_up,
    encoder_down,
    proj_weight,
    hidden_text,
    slot_source,
    norm_gain,
    kv_weight,
    queries,
):
    z_at, y_at = lax.axis_index(Z), lax.axis_index("y")
    x_at, core = lax.axis_index("x"), lax.axis_index("core")

    place = jnp.stack([z_at, y_at]).astype(jnp.int32)

    normed_patches = layer_norm(patches, patch_gain, patch_shift)
    enc_hidden = jax.nn.gelu(
        jnp.dot(normed_patches, encoder_up, preferred_element_type=F32), approximate=False
    ).astype(BF16)
    partial_out = jnp.dot(enc_hidden, encoder_down, preferred_element_type=F32).astype(BF16)
    halves = partial_out.reshape(2, HALF, -1)
    half = pick(halves, core).astype(F32) + shift(pick(halves, 1 - core), "core", 1).astype(F32)
    sent = half.astype(BF16)
    sent, hidden_text = lax.optimization_barrier((sent, hidden_text))

    give, keep = project(text_project_kernel, [hidden_text], norm_gain, kv_weight, core, TOK, [])
    text_pieces = add_pair(keep, shift(give, "core", 1), x_at)
    for step in (2, 1, 3):
        half = half + shift(sent, "x", step).astype(F32)
    half = (half + pick(patches.reshape(2, HALF, -1), core).astype(F32)).astype(BF16)
    half, text_pieces = lax.optimization_barrier((half, text_pieces))
    text_got = exchange(text_pieces)
    other = shift(half, "core", 1)

    give, keep = project(
        image_project_kernel,
        [half, other, proj_weight],
        norm_gain,
        kv_weight,
        core,
        IMG,
        [pltpu.VMEM(patches.shape, BF16)],
    )
    give, keep, text_got = lax.optimization_barrier((give, keep, text_got))
    image_got = exchange(add_pair(keep, shift(give, "core", 1), x_at))
    blocks = ring_gather(finish_rows(slot_source, text_got, image_got))
    asked = {step: shift(queries, "y", 4 - step) for step in (2, 1, 3)}

    frequencies = jnp.exp(
        jnp.arange(HALF, dtype=F32) * (-2.0 * math.log(500000.0) / (2 * HALF))
    )
    lane = jnp.arange(TOK + HEAD, dtype=jnp.int32)
    positions = jnp.where(lane < TOK, lane, ((lane - TOK) * 4 + y_at) * TOK)
    angles = positions.astype(F32)[None, :] * frequencies[:, None]
    factor = jnp.where(lane < TOK, SCALE * LOG2E, 1.0)[None, :]
    tables = (jnp.cos(angles) * factor, jnp.sin(angles) * factor)
    keys, values = merge(place, blocks, *tables)
    received = []
    for step in (2, 1, 3):
        received.append(shift(attend(step, place, keys, values, asked[step]), "y", step))
    return combine([attend(0, place, keys, values, queries), *received])


def solution(mesh):
    split = Mesh(mesh.devices.reshape(4, 2, 4, 4, 2), ("zh", "zl", "y", "x", "core"))
    seq = ("zh", "zl", "y")
    in_specs = (
        P(seq, None),
        P(),
        P(),
        P(None, TP),
        P(TP, None),
        P(None, TP),
        P(seq, TP),
        P(seq),
        P(TP),
        P(None, TP),
        P(seq, TP),
    )
    return jax.shard_map(
        body, mesh=split, in_specs=in_specs, out_specs=P(seq, TP), check_vma=False
    )
```

```python
import functools
import math

import jax
import jax.numpy as jnp
from jax import lax
from jax.experimental import pallas as pl
from jax.experimental.pallas import tpu as pltpu
from jax.sharding import Mesh
from jax.sharding import PartitionSpec as P

D = 8192
HEAD = 128
HALF = 64
GROUP = 4
TOK = 256
IMG = 128
ROWS = 272
TP = ("x", "core")
Z = ("zh", "zl")
BF16 = jnp.bfloat16
F32 = jnp.float32
NEG = -1e30
LOG2E = math.log2(math.e)
WIDE = TOK + IMG
KEYS = 2048
CHUNK = 1024
PER = CHUNK // TOK
ROWS_Q = GROUP * TOK
SCALE = HEAD ** (-0.5)


def shift(values, axis, step):
    count = lax.axis_size(axis)
    return lax.ppermute(values, axis, [(i, (i + step) % count) for i in range(count)])


def pick(values, index):
    return lax.dynamic_index_in_dim(values, index, 0, keepdims=False)


def vmem(mib):
    return pltpu.CompilerParams(vmem_limit_bytes=mib * 1024 * 1024)


def split_squares(column, count):
    row = jnp.broadcast_to(column, (count, HEAD)).T[:16]
    high = row.astype(BF16).astype(F32)
    at = lax.broadcasted_iota(jnp.int32, row.shape, 0)
    return jnp.where(at == 0, high, jnp.where(at == 1, row - high, 0.0)).astype(BF16)


def head_rows(core, features, tail, weight_ref, give_ref, keep_ref):
    for x_at in range(4):
        for own, ref in ((0, give_ref), (1, keep_ref)):
            head = 2 * x_at + jnp.where(own == 1, core, 1 - core)
            weight = weight_ref[pl.ds(pl.multiple_of(head * TOK, TOK), TOK), :]
            rows = lax.dot_general(
                weight, features, (((1,), (1,)), ((), ())), preferred_element_type=F32
            )
            ref[x_at, :TOK, :] = rows.astype(BF16)
            ref[x_at, TOK:, :] = tail


def gain_features(features, gain_ref):
    widened = features.astype(F32)
    squares = jnp.sum(jnp.square(widened), axis=1, keepdims=True)
    return (widened * gain_ref[...]).astype(BF16), split_squares(squares, features.shape[0])


def text_project_kernel(core, hidden_ref, gain_ref, weight_ref, give_ref, keep_ref):
    gained, tail = gain_features(hidden_ref[...], gain_ref)
    head_rows(core[0], gained, tail, weight_ref, give_ref, keep_ref)


def image_project_kernel(
    core, half_ref, other_ref, proj_ref, gain_ref, weight_ref, give_ref, keep_ref, encoded
):
    at = pl.multiple_of(core[0] * HALF, HALF)
    encoded[pl.ds(at, HALF), :] = half_ref[...]
    encoded[pl.ds(HALF - at, HALF), :] = other_ref[...]
    image = jnp.dot(encoded[...], proj_ref[...], preferred_element_type=F32).astype(BF16)
    gained, tail = gain_features(image, gain_ref)
    head_rows(core[0], gained, tail, weight_ref, give_ref, keep_ref)


def project(kernel, features, norm_gain, kv_weight, core, count, scratch):
    mine = jnp.reshape(core, (1,)).astype(jnp.int32)
    shape = jax.ShapeDtypeStruct((4, ROWS, count), BF16)
    return pl.pallas_call(
        kernel,
        out_shape=(shape, shape),
        in_specs=[
            pl.BlockSpec(memory_space=pltpu.SMEM),
            *[pl.BlockSpec(memory_space=pltpu.VMEM)] * (len(features) + 2),
        ],
        scratch_shapes=scratch,
        compiler_params=vmem(8),
        name="project",
    )(mine, *features, norm_gain[None, :], kv_weight)


def pair_kernel(place, keep_ref, got_ref, own_ref, two_ref, one_ref, three_ref):
    for step, ref in ((2, two_ref), (1, one_ref), (3, three_ref), (0, own_ref)):
        at = lax.rem(place[0] + step, 4)
        total = keep_ref[at].astype(F32) + got_ref[at].astype(F32)
        ref[...] = total.astype(ref.dtype)


def add_pair(keep, got, x_at):
    part = keep.shape[1:]
    return pl.pallas_call(
        pair_kernel,
        out_shape=(jax.ShapeDtypeStruct(part, F32), *[jax.ShapeDtypeStruct(part, BF16)] * 3),
        in_specs=[
            pl.BlockSpec(memory_space=pltpu.SMEM),
            *[pl.BlockSpec(memory_space=pltpu.VMEM)] * 2,
        ],
        compiler_params=vmem(6),
        name="add_pair",
    )(jnp.reshape(x_at, (1,)).astype(jnp.int32), keep, got)


def finish_kernel(slots, *refs):
    *inputs, out_ref = refs
    for lanes, pieces in ((slice(0, TOK), inputs[:4]), (slice(TOK, WIDE), inputs[4:])):
        total = pieces[0][...]
        for ref in pieces[1:]:
            total = total + ref[...].astype(F32)
        inverse = lax.rsqrt((total[TOK : TOK + 1] + total[TOK + 1 : TOK + 2]) / D + 1e-05)
        out_ref[:TOK, lanes] = (total[:TOK] * inverse).astype(BF16)
    lane = lax.broadcasted_iota(jnp.int32, (ROWS - TOK, WIDE), 1)
    out_ref[TOK:, :] = jnp.where(lane < IMG, slots[0], slots[1]).astype(F32).astype(BF16)


def finish_rows(slots, text, image):
    return pl.pallas_call(
        finish_kernel,
        out_shape=jax.ShapeDtypeStruct((ROWS, WIDE), BF16),
        in_specs=[
            pl.BlockSpec(memory_space=pltpu.SMEM),
            *[pl.BlockSpec(memory_space=pltpu.VMEM)] * 8,
        ],
        compiler_params=vmem(6),
        name="finish_rows",
    )(slots, *text, *image)


def ring_gather(block, queries):
    asked, blocks, up, down = {}, [block], block, block
    for step in (2, 1, 3):
        up, down = shift(up, Z, 1), shift(down, Z, 7)
        blocks += [up, down]
        down, queries = lax.optimization_barrier((down, queries))
        asked[step] = shift(queries, "y", 4 - step)
    return [*blocks, shift(up[:IMG], Z, 1), shift(down[IMG:], Z, 7)], asked


def exchange(pieces):
    own, two, one, three = pieces
    return [own, shift(two, "x", 2), shift(one, "x", 1), shift(three, "x", 3)]


def merge_kernel(place, *refs):
    *blocks, cos_ref, sin_ref, keys, values, gathered = refs
    for step, ref in zip((0, 7, 1, 6, 2, 5, 3), blocks):
        gathered[lax.rem(place[0] + step, 8)] = ref[...]
    far = lax.rem(place[0] + 4, 8)
    gathered[far, :IMG, :] = blocks[7][...]
    gathered[far, IMG:, :] = blocks[8][...]
    values[:, HEAD:] = jnp.ones((KEYS, HEAD), BF16)
    for block in range(8):
        for slot in range(2):
            lanes = slice(slot * IMG, (slot + 1) * IMG)
            here = slice(block * TOK + slot * IMG, block * TOK + (slot + 1) * IMG)
            text = gathered[block, :, lanes].astype(F32)
            source = text[TOK : TOK + 1, :]
            rows = text[:TOK, :]
            for r in range(4):
                image = gathered[2 * r + block % 2, :TOK, TOK:]
                rows = jnp.where(source == float(r), image.astype(F32), rows)
            inner_cos, inner_sin = cos_ref[:, lanes], sin_ref[:, lanes]
            outer_cos = cos_ref[:, TOK + block : TOK + block + 1]
            outer_sin = sin_ref[:, TOK + block : TOK + block + 1]
            cosine = inner_cos * outer_cos - inner_sin * outer_sin
            sine = inner_sin * outer_cos + inner_cos * outer_sin
            first, second = rows[:HALF], rows[HALF:HEAD]
            keys[:HALF, here] = (first * cosine - second * sine).astype(BF16)
            keys[HALF:, here] = (second * cosine + first * sine).astype(BF16)
            values[here, :HEAD] = rows[HEAD:].T.astype(BF16)


def merge(place, blocks, cosine, sine):
    return pl.pallas_call(
        merge_kernel,
        out_shape=(
            jax.ShapeDtypeStruct((HEAD, KEYS), BF16),
            jax.ShapeDtypeStruct((KEYS, 2 * HEAD), BF16),
        ),
        in_specs=[
            pl.BlockSpec(memory_space=pltpu.SMEM),
            *[pl.BlockSpec(memory_space=pltpu.VMEM)] * (len(blocks) + 2),
        ],
        scratch_shapes=[pltpu.VMEM((8, ROWS, WIDE), BF16)],
        compiler_params=vmem(10),
        name="merge",
    )(place, *blocks, cosine, sine)


def attend_kernel(step, place, keys, values, query_ref, out_ref, scores, top, mixed):
    z_at, y_at = place[0], place[1]
    block_at = lax.rem(y_at + step, 4)
    full = z_at + jnp.where(y_at < block_at, 1, 0)
    count = z_at + jnp.where(y_at <= block_at, 1, 0)
    plain = full // PER
    chunks = (count + PER - 1) // PER
    top[...] = jnp.full(top.shape, NEG, F32)

    def chunk_at(chunk, offset=0, size=CHUNK):
        return pl.ds(pl.multiple_of(chunk * CHUNK + offset, HEAD), size)

    def score(chunk, masked):
        keys_now = keys[:, chunk_at(chunk)]
        if masked:
            key_at = lax.broadcasted_iota(jnp.int32, (TOK, CHUNK), 1)
            key_at = key_at + (key_at // TOK) * (3 * TOK)
            query_at = lax.broadcasted_iota(jnp.int32, (TOK, CHUNK), 0)
            offset = ((PER * chunk - z_at) * 4 + y_at - block_at) * TOK
            allowed = key_at + offset <= query_at
        for h in range(GROUP):
            here = slice(h * TOK, (h + 1) * TOK)
            s = jnp.dot(
                query_ref[:, h * HEAD : (h + 1) * HEAD], keys_now, preferred_element_type=F32
            )
            if masked:
                s = jnp.where(allowed, s, -jnp.inf)
            scores[here, chunk_at(chunk)] = s
            most = top[here, :]
            for lane in range(0, CHUNK, HEAD):
                most = jnp.maximum(most, s[:, lane : lane + HEAD])
            top[here, :] = most

    pl.loop(0, plain)(lambda chunk: score(chunk, False))

    @pl.when(chunks > plain)
    def last():
        score(plain, True)

    top[...] = jnp.broadcast_to(jnp.max(top[...], axis=1, keepdims=True), top.shape)

    def weigh(chunk, first):
        values_now = values[chunk_at(chunk), :]
        for h in range(GROUP):
            here = slice(h * TOK, (h + 1) * TOK)
            most = top[here, :]
            weights = jnp.concatenate(
                [
                    jnp.exp2(scores[here, chunk_at(chunk, lane, HEAD)] - most).astype(BF16)
                    for lane in range(0, CHUNK, HEAD)
                ],
                1,
            )
            rows = jnp.dot(weights, values_now, preferred_element_type=F32)
            mixed[here, :] = rows if first else mixed[here, :] + rows

    @pl.when(chunks > 0)
    def some_keys():
        weigh(0, True)

    @pl.when(chunks == 0)
    def no_keys():
        mixed[...] = jnp.zeros(mixed.shape, F32)

    pl.loop(1, chunks)(lambda chunk: weigh(chunk, False))

    lane = lax.broadcasted_iota(jnp.int32, (TOK, HEAD), 1)
    stats = jnp.zeros((TOK, HEAD), F32)
    for h in range(GROUP):
        here = slice(h * TOK, (h + 1) * TOK)
        total = mixed[here, HEAD:]
        safe = jnp.where(total > 0.0, total, 1.0)
        out_ref[:TOK, h * HEAD : (h + 1) * HEAD] = (mixed[here, :HEAD] / safe).astype(BF16)
        stats = jnp.where(lane == h, top[here, :], jnp.where(lane == GROUP + h, total, stats))
    rows = stats.T
    tops, totals = rows[:GROUP], rows[GROUP : 2 * GROUP]
    some = totals > 0.0
    level = jnp.where(some, tops + jnp.log2(jnp.where(some, totals, 1.0)), NEG)
    high = level.astype(BF16).astype(F32)
    middle = (level - high).astype(BF16).astype(F32)
    low = level - high - middle
    pad = jnp.zeros((ROWS - TOK - 3 * GROUP, TOK), F32)
    out_ref[TOK:, :TOK] = jnp.concatenate([high, middle, low, pad], 0).astype(BF16)
    out_ref[TOK:, TOK:] = jnp.zeros((ROWS - TOK, 2 * HEAD), BF16)


def attend(step, place, keys, values, queries):
    return pl.pallas_call(
        functools.partial(attend_kernel, step),
        out_shape=jax.ShapeDtypeStruct((ROWS, GROUP * HEAD), BF16),
        in_specs=[
            pl.BlockSpec(memory_space=pltpu.SMEM),
            *[pl.BlockSpec(memory_space=pltpu.VMEM)] * 3,
        ],
        scratch_shapes=[
            pltpu.VMEM((ROWS_Q, KEYS), F32),
            pltpu.VMEM((ROWS_Q, HEAD), F32),
            pltpu.VMEM((ROWS_Q, 2 * HEAD), F32),
        ],
        compiler_params=vmem(24),
        cost_estimate=pl.CostEstimate(
            flops=4 * ROWS_Q * KEYS * HEAD, bytes_accessed=2 << 20, transcendentals=ROWS_Q * KEYS
        ),
        name="attend",
    )(place, keys, values, queries)


def layer_norm(values, norm_scale, norm_shift):
    widened = values.astype(F32)
    first = widened[:, :1]
    offset = jnp.mean(widened - first, axis=-1, keepdims=True)
    spread = jnp.mean(jnp.square(widened - first), axis=-1, keepdims=True) - jnp.square(offset)
    spread = jnp.maximum(spread, 0.0)
    return ((widened - first - offset) * lax.rsqrt(spread + 1e-06) * norm_scale + norm_shift).astype(BF16)


def combine_kernel(*refs):
    *parts, out_ref = refs
    levels = []
    for ref in parts:
        rows = ref[TOK:, :TOK].astype(F32)
        levels.append(
            [rows[h : h + 1] + rows[4 + h : 5 + h] + rows[8 + h : 9 + h] for h in range(GROUP)]
        )
    weights = []
    for h in range(GROUP):
        most = functools.reduce(jnp.maximum, [level[h] for level in levels])
        raised = [jnp.exp2(level[h] - most) for level in levels]
        total = sum(raised)
        weights += [r / total for r in raised]
    rows = jnp.concatenate([*weights, jnp.zeros((HEAD - len(weights), TOK), F32)], 0).T
    for h in range(GROUP):
        lanes = slice(h * HEAD, (h + 1) * HEAD)
        mixed = sum(
            rows[:, 4 * h + i : 4 * h + i + 1] * ref[:TOK, lanes].astype(F32)
            for i, ref in enumerate(parts)
        )
        out_ref[:, lanes] = mixed.astype(BF16)


def combine(parts):
    return pl.pallas_call(
        combine_kernel,
        out_shape=jax.ShapeDtypeStruct((TOK, GROUP * HEAD), BF16),
        compiler_params=vmem(6),
        name="combine",
    )(*parts)


def body(
    patches,
    patch_gain,
    patch_shift,
    encoder_up,
    encoder_down,
    proj_weight,
    hidden_text,
    slot_source,
    norm_gain,
    kv_weight,
    queries,
):
    z_at, y_at = lax.axis_index(Z), lax.axis_index("y")
    x_at, core = lax.axis_index("x"), lax.axis_index("core")

    place = jnp.stack([z_at, y_at]).astype(jnp.int32)

    normed_patches = layer_norm(patches, patch_gain, patch_shift)
    enc_hidden = jax.nn.gelu(
        jnp.dot(normed_patches, encoder_up, preferred_element_type=F32), approximate=False
    ).astype(BF16)
    partial_out = jnp.dot(enc_hidden, encoder_down, preferred_element_type=F32).astype(BF16)
    halves = partial_out.reshape(2, HALF, -1)
    half = pick(halves, core).astype(F32) + shift(pick(halves, 1 - core), "core", 1).astype(F32)
    sent = half.astype(BF16)
    sent, hidden_text = lax.optimization_barrier((sent, hidden_text))

    give, keep = project(text_project_kernel, [hidden_text], norm_gain, kv_weight, core, TOK, [])
    text_pieces = add_pair(keep, shift(give, "core", 1), x_at)
    for step in (2, 1, 3):
        half = half + shift(sent, "x", step).astype(F32)
    half = (half + pick(patches.reshape(2, HALF, -1), core).astype(F32)).astype(BF16)
    half, text_pieces = lax.optimization_barrier((half, text_pieces))
    text_got = exchange(text_pieces)
    other = shift(half, "core", 1)

    give, keep = project(
        image_project_kernel,
        [half, other, proj_weight],
        norm_gain,
        kv_weight,
        core,
        IMG,
        [pltpu.VMEM(patches.shape, BF16)],
    )
    give, keep, text_got = lax.optimization_barrier((give, keep, text_got))
    image_got = exchange(add_pair(keep, shift(give, "core", 1), x_at))
    blocks, asked = ring_gather(finish_rows(slot_source, text_got, image_got), queries)

    frequencies = jnp.exp(
        jnp.arange(HALF, dtype=F32) * (-2.0 * math.log(500000.0) / (2 * HALF))
    )
    lane = jnp.arange(TOK + HEAD, dtype=jnp.int32)
    positions = jnp.where(lane < TOK, lane, ((lane - TOK) * 4 + y_at) * TOK)
    angles = positions.astype(F32)[None, :] * frequencies[:, None]
    factor = jnp.where(lane < TOK, SCALE * LOG2E, 1.0)[None, :]
    tables = (jnp.cos(angles) * factor, jnp.sin(angles) * factor)
    keys, values = merge(place, blocks, *tables)
    received = []
    for step in (2, 1, 3):
        received.append(shift(attend(step, place, keys, values, asked[step]), "y", step))
    return combine([attend(0, place, keys, values, queries), *received])


def solution(mesh):
    split = Mesh(mesh.devices.reshape(4, 2, 4, 4, 2), ("zh", "zl", "y", "x", "core"))
    seq = ("zh", "zl", "y")
    in_specs = (
        P(seq, None),
        P(),
        P(),
        P(None, TP),
        P(TP, None),
        P(None, TP),
        P(seq, TP),
        P(seq),
        P(TP),
        P(None, TP),
        P(seq, TP),
    )
    return jax.shard_map(
        body, mesh=split, in_specs=in_specs, out_specs=P(seq, TP), check_vma=False
    )
```

```python
import functools
import math

import jax
import jax.numpy as jnp
from jax import lax
from jax.experimental import pallas as pl
from jax.experimental.pallas import tpu as pltpu
from jax.sharding import Mesh
from jax.sharding import PartitionSpec as P

D = 8192
HEAD = 128
HALF = 64
GROUP = 4
TOK = 256
IMG = 128
ROWS = 272
TP = ("x", "core")
Z = ("zh", "zl")
BF16 = jnp.bfloat16
F32 = jnp.float32
NEG = -1e30
LOG2E = math.log2(math.e)
WIDE = TOK + IMG
KEYS = 2048
CHUNK = 1024
PER = CHUNK // TOK
ROWS_Q = GROUP * TOK
SCALE = HEAD ** (-0.5)


def shift(values, axis, step):
    count = lax.axis_size(axis)
    return lax.ppermute(values, axis, [(i, (i + step) % count) for i in range(count)])


def pick(values, index):
    return lax.dynamic_index_in_dim(values, index, 0, keepdims=False)


def vmem(mib):
    return pltpu.CompilerParams(vmem_limit_bytes=mib * 1024 * 1024)


def split_squares(column, count):
    row = jnp.broadcast_to(column, (count, HEAD)).T[:16]
    high = row.astype(BF16).astype(F32)
    at = lax.broadcasted_iota(jnp.int32, row.shape, 0)
    return jnp.where(at == 0, high, jnp.where(at == 1, row - high, 0.0)).astype(BF16)


def head_rows(core, features, tail, weight_ref, give_ref, keep_ref):
    for x_at in range(4):
        for own, ref in ((0, give_ref), (1, keep_ref)):
            head = 2 * x_at + jnp.where(own == 1, core, 1 - core)
            weight = weight_ref[pl.ds(pl.multiple_of(head * TOK, TOK), TOK), :]
            rows = lax.dot_general(
                weight, features, (((1,), (1,)), ((), ())), preferred_element_type=F32
            )
            ref[x_at, :TOK, :] = rows.astype(BF16)
            ref[x_at, TOK:, :] = tail


def gain_features(features, gain_ref):
    widened = features.astype(F32)
    squares = jnp.sum(jnp.square(widened), axis=1, keepdims=True)
    return (widened * gain_ref[...]).astype(BF16), split_squares(squares, features.shape[0])


def text_project_kernel(core, hidden_ref, gain_ref, weight_ref, give_ref, keep_ref):
    gained, tail = gain_features(hidden_ref[...], gain_ref)
    head_rows(core[0], gained, tail, weight_ref, give_ref, keep_ref)


def image_project_kernel(
    core, half_ref, other_ref, proj_ref, gain_ref, weight_ref, give_ref, keep_ref, encoded
):
    at = pl.multiple_of(core[0] * HALF, HALF)
    encoded[pl.ds(at, HALF), :] = half_ref[...]
    encoded[pl.ds(HALF - at, HALF), :] = other_ref[...]
    image = jnp.dot(encoded[...], proj_ref[...], preferred_element_type=F32).astype(BF16)
    gained, tail = gain_features(image, gain_ref)
    head_rows(core[0], gained, tail, weight_ref, give_ref, keep_ref)


def project(kernel, features, norm_gain, kv_weight, core, count, scratch):
    mine = jnp.reshape(core, (1,)).astype(jnp.int32)
    shape = jax.ShapeDtypeStruct((4, ROWS, count), BF16)
    return pl.pallas_call(
        kernel,
        out_shape=(shape, shape),
        in_specs=[
            pl.BlockSpec(memory_space=pltpu.SMEM),
            *[pl.BlockSpec(memory_space=pltpu.VMEM)] * (len(features) + 2),
        ],
        scratch_shapes=scratch,
        compiler_params=vmem(8),
        name="project",
    )(mine, *features, norm_gain[None, :], kv_weight)


def pair_kernel(place, keep_ref, got_ref, own_ref, two_ref, one_ref, three_ref):
    for step, ref in ((2, two_ref), (1, one_ref), (3, three_ref), (0, own_ref)):
        at = lax.rem(place[0] + step, 4)
        total = keep_ref[at].astype(F32) + got_ref[at].astype(F32)
        ref[...] = total.astype(ref.dtype)


def add_pair(keep, got, x_at):
    part = keep.shape[1:]
    return pl.pallas_call(
        pair_kernel,
        out_shape=(jax.ShapeDtypeStruct(part, F32), *[jax.ShapeDtypeStruct(part, BF16)] * 3),
        in_specs=[
            pl.BlockSpec(memory_space=pltpu.SMEM),
            *[pl.BlockSpec(memory_space=pltpu.VMEM)] * 2,
        ],
        compiler_params=vmem(6),
        name="add_pair",
    )(jnp.reshape(x_at, (1,)).astype(jnp.int32), keep, got)


def finish_kernel(slots, *refs):
    *inputs, out_ref = refs
    for lanes, pieces in ((slice(0, TOK), inputs[:4]), (slice(TOK, WIDE), inputs[4:])):
        total = pieces[0][...]
        for ref in pieces[1:]:
            total = total + ref[...].astype(F32)
        inverse = lax.rsqrt((total[TOK : TOK + 1] + total[TOK + 1 : TOK + 2]) / D + 1e-05)
        out_ref[:TOK, lanes] = (total[:TOK] * inverse).astype(BF16)
    lane = lax.broadcasted_iota(jnp.int32, (ROWS - TOK, WIDE), 1)
    out_ref[TOK:, :] = jnp.where(lane < IMG, slots[0], slots[1]).astype(F32).astype(BF16)


def finish_rows(slots, text, image):
    return pl.pallas_call(
        finish_kernel,
        out_shape=jax.ShapeDtypeStruct((ROWS, WIDE), BF16),
        in_specs=[
            pl.BlockSpec(memory_space=pltpu.SMEM),
            *[pl.BlockSpec(memory_space=pltpu.VMEM)] * 8,
        ],
        compiler_params=vmem(6),
        name="finish_rows",
    )(slots, *text, *image)


def ring_gather(block):
    blocks, up, down = [block], block, block
    for _ in range(3):
        up, down = shift(up, Z, 1), shift(down, Z, 7)
        blocks += [up, down]
    return [*blocks, shift(up[:IMG], Z, 1), shift(down[IMG:], Z, 7)]


def exchange(pieces):
    own, two, one, three = pieces
    return [own, shift(two, "x", 2), shift(one, "x", 1), shift(three, "x", 3)]


def merge_kernel(place, *refs):
    *blocks, cos_ref, sin_ref, keys, values, gathered = refs
    for step, ref in zip((0, 7, 1, 6, 2, 5, 3), blocks):
        gathered[lax.rem(place[0] + step, 8)] = ref[...]
    far = lax.rem(place[0] + 4, 8)
    gathered[far, :IMG, :] = blocks[7][...]
    gathered[far, IMG:, :] = blocks[8][...]
    values[:, HEAD:] = jnp.ones((KEYS, HEAD), BF16)
    for block in range(8):
        for slot in range(2):
            lanes = slice(slot * IMG, (slot + 1) * IMG)
            here = slice(block * TOK + slot * IMG, block * TOK + (slot + 1) * IMG)
            text = gathered[block, :, lanes].astype(F32)
            source = text[TOK : TOK + 1, :]
            rows = text[:TOK, :]
            for r in range(4):
                image = gathered[2 * r + block % 2, :TOK, TOK:]
                rows = jnp.where(source == float(r), image.astype(F32), rows)
            inner_cos, inner_sin = cos_ref[:, lanes], sin_ref[:, lanes]
            outer_cos = cos_ref[:, TOK + block : TOK + block + 1]
            outer_sin = sin_ref[:, TOK + block : TOK + block + 1]
            cosine = inner_cos * outer_cos - inner_sin * outer_sin
            sine = inner_sin * outer_cos + inner_cos * outer_sin
            first, second = rows[:HALF], rows[HALF:HEAD]
            keys[:HALF, here] = (first * cosine - second * sine).astype(BF16)
            keys[HALF:, here] = (second * cosine + first * sine).astype(BF16)
            values[here, :HEAD] = rows[HEAD:].T.astype(BF16)


def merge(place, blocks, cosine, sine):
    return pl.pallas_call(
        merge_kernel,
        out_shape=(
            jax.ShapeDtypeStruct((HEAD, KEYS), BF16),
            jax.ShapeDtypeStruct((KEYS, 2 * HEAD), BF16),
        ),
        in_specs=[
            pl.BlockSpec(memory_space=pltpu.SMEM),
            *[pl.BlockSpec(memory_space=pltpu.VMEM)] * (len(blocks) + 2),
        ],
        scratch_shapes=[pltpu.VMEM((8, ROWS, WIDE), BF16)],
        compiler_params=vmem(10),
        name="merge",
    )(place, *blocks, cosine, sine)


def attend_kernel(step, place, keys, values, query_ref, out_ref, scores, top, mixed):
    z_at, y_at = place[0], place[1]
    block_at = lax.rem(y_at + step, 4)
    full = z_at + jnp.where(y_at < block_at, 1, 0)
    count = z_at + jnp.where(y_at <= block_at, 1, 0)
    plain = full // PER
    chunks = (count + PER - 1) // PER
    top[...] = jnp.full(top.shape, NEG, F32)

    def chunk_at(chunk, offset=0, size=CHUNK):
        return pl.ds(pl.multiple_of(chunk * CHUNK + offset, HEAD), size)

    def score(chunk, masked):
        keys_now = keys[:, chunk_at(chunk)]
        if masked:
            key_at = lax.broadcasted_iota(jnp.int32, (TOK, CHUNK), 1)
            key_at = key_at + (key_at // TOK) * (3 * TOK)
            query_at = lax.broadcasted_iota(jnp.int32, (TOK, CHUNK), 0)
            offset = ((PER * chunk - z_at) * 4 + y_at - block_at) * TOK
            allowed = key_at + offset <= query_at
        for h in range(GROUP):
            here = slice(h * TOK, (h + 1) * TOK)
            s = jnp.dot(
                query_ref[block_at, :, h * HEAD : (h + 1) * HEAD], keys_now, preferred_element_type=F32
            )
            if masked:
                s = jnp.where(allowed, s, -jnp.inf)
            scores[here, chunk_at(chunk)] = s
            most = top[here, :]
            for lane in range(0, CHUNK, HEAD):
                most = jnp.maximum(most, s[:, lane : lane + HEAD])
            top[here, :] = most

    pl.loop(0, plain)(lambda chunk: score(chunk, False))

    @pl.when(chunks > plain)
    def last():
        score(plain, True)

    top[...] = jnp.broadcast_to(jnp.max(top[...], axis=1, keepdims=True), top.shape)

    def weigh(chunk, first):
        values_now = values[chunk_at(chunk), :]
        for h in range(GROUP):
            here = slice(h * TOK, (h + 1) * TOK)
            most = top[here, :]
            weights = jnp.concatenate(
                [
                    jnp.exp2(scores[here, chunk_at(chunk, lane, HEAD)] - most).astype(BF16)
                    for lane in range(0, CHUNK, HEAD)
                ],
                1,
            )
            rows = jnp.dot(weights, values_now, preferred_element_type=F32)
            mixed[here, :] = rows if first else mixed[here, :] + rows

    @pl.when(chunks > 0)
    def some_keys():
        weigh(0, True)

    @pl.when(chunks == 0)
    def no_keys():
        mixed[...] = jnp.zeros(mixed.shape, F32)

    pl.loop(1, chunks)(lambda chunk: weigh(chunk, False))

    lane = lax.broadcasted_iota(jnp.int32, (TOK, HEAD), 1)
    stats = jnp.zeros((TOK, HEAD), F32)
    for h in range(GROUP):
        here = slice(h * TOK, (h + 1) * TOK)
        total = mixed[here, HEAD:]
        safe = jnp.where(total > 0.0, total, 1.0)
        out_ref[:TOK, h * HEAD : (h + 1) * HEAD] = (mixed[here, :HEAD] / safe).astype(BF16)
        stats = jnp.where(lane == h, top[here, :], jnp.where(lane == GROUP + h, total, stats))
    rows = stats.T
    tops, totals = rows[:GROUP], rows[GROUP : 2 * GROUP]
    some = totals > 0.0
    level = jnp.where(some, tops + jnp.log2(jnp.where(some, totals, 1.0)), NEG)
    high = level.astype(BF16).astype(F32)
    middle = (level - high).astype(BF16).astype(F32)
    low = level - high - middle
    pad = jnp.zeros((ROWS - TOK - 3 * GROUP, TOK), F32)
    out_ref[TOK:, :TOK] = jnp.concatenate([high, middle, low, pad], 0).astype(BF16)
    out_ref[TOK:, TOK:] = jnp.zeros((ROWS - TOK, 2 * HEAD), BF16)


def attend(step, place, keys, values, queries):
    return pl.pallas_call(
        functools.partial(attend_kernel, step),
        out_shape=jax.ShapeDtypeStruct((ROWS, GROUP * HEAD), BF16),
        in_specs=[
            pl.BlockSpec(memory_space=pltpu.SMEM),
            *[pl.BlockSpec(memory_space=pltpu.VMEM)] * 3,
        ],
        scratch_shapes=[
            pltpu.VMEM((ROWS_Q, KEYS), F32),
            pltpu.VMEM((ROWS_Q, HEAD), F32),
            pltpu.VMEM((ROWS_Q, 2 * HEAD), F32),
        ],
        compiler_params=vmem(24),
        cost_estimate=pl.CostEstimate(
            flops=4 * ROWS_Q * KEYS * HEAD, bytes_accessed=2 << 20, transcendentals=ROWS_Q * KEYS
        ),
        name="attend",
    )(place, keys, values, queries)


def layer_norm(values, norm_scale, norm_shift):
    widened = values.astype(F32)
    first = widened[:, :1]
    offset = jnp.mean(widened - first, axis=-1, keepdims=True)
    spread = jnp.mean(jnp.square(widened - first), axis=-1, keepdims=True) - jnp.square(offset)
    spread = jnp.maximum(spread, 0.0)
    return ((widened - first - offset) * lax.rsqrt(spread + 1e-06) * norm_scale + norm_shift).astype(BF16)


def combine_kernel(*refs):
    *parts, out_ref = refs
    levels = []
    for ref in parts:
        rows = ref[TOK:, :TOK].astype(F32)
        levels.append(
            [rows[h : h + 1] + rows[4 + h : 5 + h] + rows[8 + h : 9 + h] for h in range(GROUP)]
        )
    weights = []
    for h in range(GROUP):
        most = functools.reduce(jnp.maximum, [level[h] for level in levels])
        raised = [jnp.exp2(level[h] - most) for level in levels]
        total = sum(raised)
        weights += [r / total for r in raised]
    rows = jnp.concatenate([*weights, jnp.zeros((HEAD - len(weights), TOK), F32)], 0).T
    for h in range(GROUP):
        lanes = slice(h * HEAD, (h + 1) * HEAD)
        mixed = sum(
            rows[:, 4 * h + i : 4 * h + i + 1] * ref[:TOK, lanes].astype(F32)
            for i, ref in enumerate(parts)
        )
        out_ref[:, lanes] = mixed.astype(BF16)


def combine(parts):
    return pl.pallas_call(
        combine_kernel,
        out_shape=jax.ShapeDtypeStruct((TOK, GROUP * HEAD), BF16),
        compiler_params=vmem(6),
        name="combine",
    )(*parts)


def body(
    patches,
    patch_gain,
    patch_shift,
    encoder_up,
    encoder_down,
    proj_weight,
    hidden_text,
    slot_source,
    norm_gain,
    kv_weight,
    queries,
):
    z_at, y_at = lax.axis_index(Z), lax.axis_index("y")
    x_at, core = lax.axis_index("x"), lax.axis_index("core")

    place = jnp.stack([z_at, y_at]).astype(jnp.int32)

    normed_patches = layer_norm(patches, patch_gain, patch_shift)
    enc_hidden = jax.nn.gelu(
        jnp.dot(normed_patches, encoder_up, preferred_element_type=F32), approximate=False
    ).astype(BF16)
    partial_out = jnp.dot(enc_hidden, encoder_down, preferred_element_type=F32).astype(BF16)
    halves = partial_out.reshape(2, HALF, -1)
    half = pick(halves, core).astype(F32) + shift(pick(halves, 1 - core), "core", 1).astype(F32)
    sent = half.astype(BF16)
    sent, hidden_text, queries = lax.optimization_barrier((sent, hidden_text, queries))
    queries_all = lax.all_to_all(
        jnp.broadcast_to(queries[None], (4, *queries.shape)), "y", 0, 0, tiled=True
    )

    give, keep = project(text_project_kernel, [hidden_text], norm_gain, kv_weight, core, TOK, [])
    text_pieces = add_pair(keep, shift(give, "core", 1), x_at)
    for step in (2, 1, 3):
        half = half + shift(sent, "x", step).astype(F32)
    half = (half + pick(patches.reshape(2, HALF, -1), core).astype(F32)).astype(BF16)
    half, text_pieces = lax.optimization_barrier((half, text_pieces))
    text_got = exchange(text_pieces)
    other = shift(half, "core", 1)

    give, keep = project(
        image_project_kernel,
        [half, other, proj_weight],
        norm_gain,
        kv_weight,
        core,
        IMG,
        [pltpu.VMEM(patches.shape, BF16)],
    )
    give, keep, text_got, queries_all = lax.optimization_barrier((give, keep, text_got, queries_all))
    image_got = exchange(add_pair(keep, shift(give, "core", 1), x_at))
    blocks = ring_gather(finish_rows(slot_source, text_got, image_got))

    frequencies = jnp.exp(
        jnp.arange(HALF, dtype=F32) * (-2.0 * math.log(500000.0) / (2 * HALF))
    )
    lane = jnp.arange(TOK + HEAD, dtype=jnp.int32)
    positions = jnp.where(lane < TOK, lane, ((lane - TOK) * 4 + y_at) * TOK)
    angles = positions.astype(F32)[None, :] * frequencies[:, None]
    factor = jnp.where(lane < TOK, SCALE * LOG2E, 1.0)[None, :]
    tables = (jnp.cos(angles) * factor, jnp.sin(angles) * factor)
    keys, values = merge(place, blocks, *tables)
    received = []
    for step in (2, 1, 3):
        received.append(shift(attend(step, place, keys, values, queries_all), "y", step))
    return combine([attend(0, place, keys, values, queries_all), *received])


def solution(mesh):
    split = Mesh(mesh.devices.reshape(4, 2, 4, 4, 2), ("zh", "zl", "y", "x", "core"))
    seq = ("zh", "zl", "y")
    in_specs = (
        P(seq, None),
        P(),
        P(),
        P(None, TP),
        P(TP, None),
        P(None, TP),
        P(seq, TP),
        P(seq),
        P(TP),
        P(None, TP),
        P(seq, TP),
    )
    return jax.shard_map(
        body, mesh=split, in_specs=in_specs, out_specs=P(seq, TP), check_vma=False
    )
```

```python
import functools
import math

import jax
import jax.numpy as jnp
from jax import lax
from jax.experimental import pallas as pl
from jax.experimental.pallas import tpu as pltpu
from jax.sharding import Mesh
from jax.sharding import PartitionSpec as P

D = 8192
HEAD = 128
HALF = 64
GROUP = 4
TOK = 256
IMG = 128
ROWS = 272
TP = ("x", "core")
Z = ("zh", "zl")
BF16 = jnp.bfloat16
F32 = jnp.float32
NEG = -1e30
LOG2E = math.log2(math.e)
WIDE = TOK + IMG
KEYS = 2048
CHUNK = 1024
PER = CHUNK // TOK
ROWS_Q = GROUP * TOK
SCALE = HEAD ** (-0.5)


def shift(values, axis, step):
    count = lax.axis_size(axis)
    return lax.ppermute(values, axis, [(i, (i + step) % count) for i in range(count)])


def pick(values, index):
    return lax.dynamic_index_in_dim(values, index, 0, keepdims=False)


def vmem(mib):
    return pltpu.CompilerParams(vmem_limit_bytes=mib * 1024 * 1024)


def split_squares(column, count):
    row = jnp.broadcast_to(column, (count, HEAD)).T[:16]
    high = row.astype(BF16).astype(F32)
    at = lax.broadcasted_iota(jnp.int32, row.shape, 0)
    return jnp.where(at == 0, high, jnp.where(at == 1, row - high, 0.0)).astype(BF16)


def head_rows(core, features, tail, weight_ref, give_ref, keep_ref):
    @pl.loop(0, 4)
    def one_chip(x_at):
        for own, ref in ((0, give_ref), (1, keep_ref)):
            head = 2 * x_at + jnp.where(own == 1, core, 1 - core)
            weight = weight_ref[pl.ds(pl.multiple_of(head * TOK, TOK), TOK), :]
            rows = lax.dot_general(
                weight, features, (((1,), (1,)), ((), ())), preferred_element_type=F32
            )
            ref[x_at, :TOK, :] = rows.astype(BF16)
            ref[x_at, TOK:, :] = tail


def gain_features(features, gain_ref):
    widened = features.astype(F32)
    squares = jnp.sum(jnp.square(widened), axis=1, keepdims=True)
    return (widened * gain_ref[...]).astype(BF16), split_squares(squares, features.shape[0])


def text_project_kernel(core, hidden_ref, gain_ref, weight_ref, give_ref, keep_ref):
    gained, tail = gain_features(hidden_ref[...], gain_ref)
    head_rows(core[0], gained, tail, weight_ref, give_ref, keep_ref)


def image_project_kernel(
    core, half_ref, other_ref, proj_ref, gain_ref, weight_ref, give_ref, keep_ref, encoded
):
    at = pl.multiple_of(core[0] * HALF, HALF)
    encoded[pl.ds(at, HALF), :] = half_ref[...]
    encoded[pl.ds(HALF - at, HALF), :] = other_ref[...]
    image = jnp.dot(encoded[...], proj_ref[...], preferred_element_type=F32).astype(BF16)
    gained, tail = gain_features(image, gain_ref)
    head_rows(core[0], gained, tail, weight_ref, give_ref, keep_ref)


def project(kernel, features, norm_gain, kv_weight, core, count, scratch):
    mine = jnp.reshape(core, (1,)).astype(jnp.int32)
    shape = jax.ShapeDtypeStruct((4, ROWS, count), BF16)
    return pl.pallas_call(
        kernel,
        out_shape=(shape, shape),
        in_specs=[
            pl.BlockSpec(memory_space=pltpu.SMEM),
            *[pl.BlockSpec(memory_space=pltpu.VMEM)] * (len(features) + 2),
        ],
        scratch_shapes=scratch,
        compiler_params=vmem(8),
        name="project",
    )(mine, *features, norm_gain[None, :], kv_weight)


def pair_kernel(place, keep_ref, got_ref, own_ref, two_ref, one_ref, three_ref):
    for step, ref in ((2, two_ref), (1, one_ref), (3, three_ref), (0, own_ref)):
        at = lax.rem(place[0] + step, 4)
        total = keep_ref[at].astype(F32) + got_ref[at].astype(F32)
        ref[...] = total.astype(ref.dtype)


def add_pair(keep, got, x_at):
    part = keep.shape[1:]
    return pl.pallas_call(
        pair_kernel,
        out_shape=(jax.ShapeDtypeStruct(part, F32), *[jax.ShapeDtypeStruct(part, BF16)] * 3),
        in_specs=[
            pl.BlockSpec(memory_space=pltpu.SMEM),
            *[pl.BlockSpec(memory_space=pltpu.VMEM)] * 2,
        ],
        compiler_params=vmem(6),
        name="add_pair",
    )(jnp.reshape(x_at, (1,)).astype(jnp.int32), keep, got)


def finish_kernel(slots, *refs):
    *inputs, out_ref = refs
    for lanes, pieces in ((slice(0, TOK), inputs[:4]), (slice(TOK, WIDE), inputs[4:])):
        total = pieces[0][...]
        for ref in pieces[1:]:
            total = total + ref[...].astype(F32)
        inverse = lax.rsqrt((total[TOK : TOK + 1] + total[TOK + 1 : TOK + 2]) / D + 1e-05)
        out_ref[:TOK, lanes] = (total[:TOK] * inverse).astype(BF16)
    lane = lax.broadcasted_iota(jnp.int32, (ROWS - TOK, WIDE), 1)
    out_ref[TOK:, :] = jnp.where(lane < IMG, slots[0], slots[1]).astype(F32).astype(BF16)


def finish_rows(slots, text, image):
    return pl.pallas_call(
        finish_kernel,
        out_shape=jax.ShapeDtypeStruct((ROWS, WIDE), BF16),
        in_specs=[
            pl.BlockSpec(memory_space=pltpu.SMEM),
            *[pl.BlockSpec(memory_space=pltpu.VMEM)] * 8,
        ],
        compiler_params=vmem(6),
        name="finish_rows",
    )(slots, *text, *image)


def ring_gather(block):
    blocks, up, down = [block], block, block
    for _ in range(3):
        up, down = shift(up, Z, 1), shift(down, Z, 7)
        blocks += [up, down]
    return [*blocks, shift(up[:IMG], Z, 1), shift(down[IMG:], Z, 7)]


def exchange(pieces):
    own, two, one, three = pieces
    return [own, shift(two, "x", 2), shift(one, "x", 1), shift(three, "x", 3)]


def merge_kernel(place, *refs):
    *blocks, cos_ref, sin_ref, outer_cos_ref, outer_sin_ref, keys, values, gathered = refs
    for step, ref in zip((0, 7, 1, 6, 2, 5, 3), blocks):
        gathered[lax.rem(place[0] + step, 8)] = ref[...]
    far = lax.rem(place[0] + 4, 8)
    gathered[far, :IMG, :] = blocks[7][...]
    gathered[far, IMG:, :] = blocks[8][...]
    values[:, HEAD:] = jnp.ones((KEYS, HEAD), BF16)

    @pl.loop(0, 8)
    def one_block(block):
        outer_cos, outer_sin = outer_cos_ref[block], outer_sin_ref[block]
        for slot in range(2):
            lanes = slice(slot * IMG, (slot + 1) * IMG)
            here = pl.ds(pl.multiple_of(block * TOK + slot * IMG, IMG), IMG)
            text = gathered[block, :, lanes].astype(F32)
            source = text[TOK : TOK + 1, :]
            rows = text[:TOK, :]
            for r in range(4):
                image = gathered[2 * r + lax.rem(block, 2), :TOK, TOK:]
                rows = jnp.where(source == float(r), image.astype(F32), rows)
            inner_cos, inner_sin = cos_ref[:, lanes], sin_ref[:, lanes]
            cosine = inner_cos * outer_cos - inner_sin * outer_sin
            sine = inner_sin * outer_cos + inner_cos * outer_sin
            first, second = rows[:HALF], rows[HALF:HEAD]
            keys[:HALF, here] = (first * cosine - second * sine).astype(BF16)
            keys[HALF:, here] = (second * cosine + first * sine).astype(BF16)
            values[here, :HEAD] = rows[HEAD:].T.astype(BF16)


def merge(place, blocks, tables):
    return pl.pallas_call(
        merge_kernel,
        out_shape=(
            jax.ShapeDtypeStruct((HEAD, KEYS), BF16),
            jax.ShapeDtypeStruct((KEYS, 2 * HEAD), BF16),
        ),
        in_specs=[
            pl.BlockSpec(memory_space=pltpu.SMEM),
            *[pl.BlockSpec(memory_space=pltpu.VMEM)] * (len(blocks) + len(tables)),
        ],
        scratch_shapes=[pltpu.VMEM((8, ROWS, WIDE), BF16)],
        compiler_params=vmem(10),
        name="merge",
    )(place, *blocks, *tables)


def attend_kernel(step, place, keys, values, query_ref, out_ref, scores, top, mixed):
    z_at, y_at = place[0], place[1]
    block_at = lax.rem(y_at + step, 4)
    count = z_at + jnp.where(y_at <= block_at, 1, 0)
    chunks = (count + PER - 1) // PER
    top[...] = jnp.full(top.shape, NEG, F32)

    def chunk_at(chunk, offset=0, size=CHUNK):
        return pl.ds(pl.multiple_of(chunk * CHUNK + offset, HEAD), size)

    key_at = lax.broadcasted_iota(jnp.int32, (TOK, CHUNK), 1)
    reach = lax.broadcasted_iota(jnp.int32, (TOK, CHUNK), 0) - key_at - (key_at // TOK) * (3 * TOK)

    @pl.loop(0, chunks)
    def score(chunk):
        keys_now = keys[:, chunk_at(chunk)]
        allowed = reach >= ((PER * chunk - z_at) * 4 + y_at - block_at) * TOK
        for h in range(GROUP):
            here = slice(h * TOK, (h + 1) * TOK)
            s = jnp.dot(
                query_ref[:, h * HEAD : (h + 1) * HEAD], keys_now, preferred_element_type=F32
            )
            s = jnp.where(allowed, s, -jnp.inf)
            scores[here, chunk_at(chunk)] = s
            most = top[here, :]
            for lane in range(0, CHUNK, HEAD):
                most = jnp.maximum(most, s[:, lane : lane + HEAD])
            top[here, :] = most

    top[...] = jnp.broadcast_to(jnp.max(top[...], axis=1, keepdims=True), top.shape)

    mixed[...] = jnp.zeros(mixed.shape, F32)

    @pl.loop(0, chunks)
    def weigh(chunk):
        values_now = values[chunk_at(chunk), :]
        for h in range(GROUP):
            here = slice(h * TOK, (h + 1) * TOK)
            most = top[here, :]
            weights = jnp.concatenate(
                [
                    jnp.exp2(scores[here, chunk_at(chunk, lane, HEAD)] - most).astype(BF16)
                    for lane in range(0, CHUNK, HEAD)
                ],
                1,
            )
            rows = jnp.dot(weights, values_now, preferred_element_type=F32)
            mixed[here, :] += rows

    lane = lax.broadcasted_iota(jnp.int32, (TOK, HEAD), 1)
    stats = jnp.zeros((TOK, HEAD), F32)
    for h in range(GROUP):
        here = slice(h * TOK, (h + 1) * TOK)
        total = mixed[here, HEAD:]
        safe = jnp.where(total > 0.0, total, 1.0)
        out_ref[:TOK, h * HEAD : (h + 1) * HEAD] = (mixed[here, :HEAD] / safe).astype(BF16)
        stats = jnp.where(lane == h, top[here, :], jnp.where(lane == GROUP + h, total, stats))
    rows = stats.T
    tops, totals = rows[:GROUP], rows[GROUP : 2 * GROUP]
    some = totals > 0.0
    level = jnp.where(some, tops + jnp.log2(jnp.where(some, totals, 1.0)), NEG)
    high = level.astype(BF16).astype(F32)
    middle = (level - high).astype(BF16).astype(F32)
    low = level - high - middle
    pad = jnp.zeros((ROWS - TOK - 3 * GROUP, TOK), F32)
    out_ref[TOK:, :TOK] = jnp.concatenate([high, middle, low, pad], 0).astype(BF16)
    out_ref[TOK:, TOK:] = jnp.zeros((ROWS - TOK, 2 * HEAD), BF16)


def attend(step, place, keys, values, queries):
    return pl.pallas_call(
        functools.partial(attend_kernel, step),
        out_shape=jax.ShapeDtypeStruct((ROWS, GROUP * HEAD), BF16),
        in_specs=[
            pl.BlockSpec(memory_space=pltpu.SMEM),
            *[pl.BlockSpec(memory_space=pltpu.VMEM)] * 3,
        ],
        scratch_shapes=[
            pltpu.VMEM((ROWS_Q, KEYS), F32),
            pltpu.VMEM((ROWS_Q, HEAD), F32),
            pltpu.VMEM((ROWS_Q, 2 * HEAD), F32),
        ],
        compiler_params=vmem(24),
        cost_estimate=pl.CostEstimate(
            flops=4 * ROWS_Q * KEYS * HEAD, bytes_accessed=2 << 20, transcendentals=ROWS_Q * KEYS
        ),
        name="attend",
    )(place, keys, values, queries)


def layer_norm(values, norm_scale, norm_shift):
    widened = values.astype(F32)
    center = jnp.mean(widened, axis=-1, keepdims=True)
    spread = jnp.mean(jnp.square(widened - center), axis=-1, keepdims=True)
    return ((widened - center) * lax.rsqrt(spread + 1e-06) * norm_scale + norm_shift).astype(BF16)


def combine_kernel(*refs):
    *parts, out_ref = refs
    levels = []
    for ref in parts:
        rows = ref[TOK:, :TOK].astype(F32)
        levels.append(
            [rows[h : h + 1] + rows[4 + h : 5 + h] + rows[8 + h : 9 + h] for h in range(GROUP)]
        )
    weights = []
    for h in range(GROUP):
        most = functools.reduce(jnp.maximum, [level[h] for level in levels])
        raised = [jnp.exp2(level[h] - most) for level in levels]
        total = sum(raised)
        weights += [r / total for r in raised]
    rows = jnp.concatenate([*weights, jnp.zeros((HEAD - len(weights), TOK), F32)], 0).T
    for h in range(GROUP):
        lanes = slice(h * HEAD, (h + 1) * HEAD)
        mixed = sum(
            rows[:, 4 * h + i : 4 * h + i + 1] * ref[:TOK, lanes].astype(F32)
            for i, ref in enumerate(parts)
        )
        out_ref[:, lanes] = mixed.astype(BF16)


def combine(parts):
    return pl.pallas_call(
        combine_kernel,
        out_shape=jax.ShapeDtypeStruct((TOK, GROUP * HEAD), BF16),
        compiler_params=vmem(6),
        name="combine",
    )(*parts)


def body(
    patches,
    patch_gain,
    patch_shift,
    encoder_up,
    encoder_down,
    proj_weight,
    hidden_text,
    slot_source,
    norm_gain,
    kv_weight,
    queries,
):
    z_at, y_at = lax.axis_index(Z), lax.axis_index("y")
    x_at, core = lax.axis_index("x"), lax.axis_index("core")

    place = jnp.stack([z_at, y_at]).astype(jnp.int32)

    normed_patches = layer_norm(patches, patch_gain, patch_shift)
    enc_hidden = jax.nn.gelu(
        jnp.dot(normed_patches, encoder_up, preferred_element_type=F32), approximate=False
    ).astype(BF16)
    partial_out = jnp.dot(enc_hidden, encoder_down, preferred_element_type=F32).astype(BF16)
    halves = partial_out.reshape(2, HALF, -1)
    half = pick(halves, core).astype(F32) + shift(pick(halves, 1 - core), "core", 1).astype(F32)
    sent = half.astype(BF16)
    sent, hidden_text = lax.optimization_barrier((sent, hidden_text))

    give, keep = project(text_project_kernel, [hidden_text], norm_gain, kv_weight, core, TOK, [])
    text_pieces = add_pair(keep, shift(give, "core", 1), x_at)
    for step in (2, 1, 3):
        half = half + shift(sent, "x", step).astype(F32)
    half = (half + pick(patches.reshape(2, HALF, -1), core).astype(F32)).astype(BF16)
    half, text_pieces = lax.optimization_barrier((half, text_pieces))
    text_got = exchange(text_pieces)
    other = shift(half, "core", 1)

    give, keep = project(
        image_project_kernel,
        [half, other, proj_weight],
        norm_gain,
        kv_weight,
        core,
        IMG,
        [pltpu.VMEM(patches.shape, BF16)],
    )
    give, keep, text_got = lax.optimization_barrier((give, keep, text_got))
    image_got = exchange(add_pair(keep, shift(give, "core", 1), x_at))
    blocks = ring_gather(finish_rows(slot_source, text_got, image_got))
    asked = {step: shift(queries, "y", 4 - step) for step in (2, 1, 3)}

    frequencies = jnp.exp(
        jnp.arange(HALF, dtype=F32) * (-2.0 * math.log(500000.0) / (2 * HALF))
    )
    inner = jnp.arange(TOK, dtype=F32)[None, :] * frequencies[:, None]
    starts = ((jnp.arange(8, dtype=jnp.int32) * 4 + y_at) * TOK).astype(F32)
    outer = jnp.broadcast_to(starts[:, None, None] * frequencies[None, :, None], (8, HALF, HEAD))
    factor = SCALE * LOG2E
    tables = (jnp.cos(inner) * factor, jnp.sin(inner) * factor, jnp.cos(outer), jnp.sin(outer))
    keys, values = merge(place, blocks, tables)
    received = []
    for step in (2, 1, 3):
        received.append(shift(attend(step, place, keys, values, asked[step]), "y", step))
    return combine([attend(0, place, keys, values, queries), *received])


def solution(mesh):
    split = Mesh(mesh.devices.reshape(4, 2, 4, 4, 2), ("zh", "zl", "y", "x", "core"))
    seq = ("zh", "zl", "y")
    in_specs = (
        P(seq, None),
        P(),
        P(),
        P(None, TP),
        P(TP, None),
        P(None, TP),
        P(seq, TP),
        P(seq),
        P(TP),
        P(None, TP),
        P(seq, TP),
    )
    return jax.shard_map(
        body, mesh=split, in_specs=in_specs, out_specs=P(seq, TP), check_vma=False
    )
```

```python
import functools
import math

import jax
import jax.numpy as jnp
from jax import lax
from jax.experimental import pallas as pl
from jax.experimental.pallas import tpu as pltpu
from jax.sharding import Mesh
from jax.sharding import PartitionSpec as P

D = 8192
HEAD = 128
HALF = 64
GROUP = 4
TOK = 256
IMG = 128
ROWS = 272
TP = ("x", "core")
Z = ("zh", "zl")
BF16 = jnp.bfloat16
F32 = jnp.float32
NEG = -1e30
LOG2E = math.log2(math.e)
WIDE = TOK + IMG
KEYS = 2048
CHUNK = 1024
PER = CHUNK // TOK
ROWS_Q = GROUP * TOK
SCALE = HEAD ** (-0.5)


def shift(values, axis, step):
    count = lax.axis_size(axis)
    return lax.ppermute(values, axis, [(i, (i + step) % count) for i in range(count)])


def pick(values, index):
    return lax.dynamic_index_in_dim(values, index, 0, keepdims=False)


def vmem(mib):
    return pltpu.CompilerParams(vmem_limit_bytes=mib * 1024 * 1024)


def split_squares(column, count):
    row = jnp.broadcast_to(column, (count, HEAD)).T[:16]
    high = row.astype(BF16).astype(F32)
    at = lax.broadcasted_iota(jnp.int32, row.shape, 0)
    return jnp.where(at == 0, high, jnp.where(at == 1, row - high, 0.0)).astype(BF16)


def head_rows(core, features, tail, weight_ref, give_ref, keep_ref):
    for x_at in range(4):
        for own, ref in ((0, give_ref), (1, keep_ref)):
            head = 2 * x_at + jnp.where(own == 1, core, 1 - core)
            weight = weight_ref[pl.ds(pl.multiple_of(head * TOK, TOK), TOK), :]
            rows = lax.dot_general(
                weight, features, (((1,), (1,)), ((), ())), preferred_element_type=F32
            )
            ref[x_at, :TOK, :] = rows.astype(BF16)
            ref[x_at, TOK:, :] = tail


def gain_features(features, gain_ref):
    widened = features.astype(F32)
    squares = jnp.sum(jnp.square(widened), axis=1, keepdims=True)
    return (widened * gain_ref[...]).astype(BF16), split_squares(squares, features.shape[0])


def text_project_kernel(core, hidden_ref, gain_ref, weight_ref, give_ref, keep_ref):
    gained, tail = gain_features(hidden_ref[...], gain_ref)
    head_rows(core[0], gained, tail, weight_ref, give_ref, keep_ref)


def image_project_kernel(
    core, half_ref, other_ref, proj_ref, gain_ref, weight_ref, give_ref, keep_ref, encoded
):
    at = pl.multiple_of(core[0] * HALF, HALF)
    encoded[pl.ds(at, HALF), :] = half_ref[...]
    encoded[pl.ds(HALF - at, HALF), :] = other_ref[...]
    image = jnp.dot(encoded[...], proj_ref[...], preferred_element_type=F32).astype(BF16)
    gained, tail = gain_features(image, gain_ref)
    head_rows(core[0], gained, tail, weight_ref, give_ref, keep_ref)


def project(kernel, features, norm_gain, kv_weight, core, count, scratch):
    mine = jnp.reshape(core, (1,)).astype(jnp.int32)
    shape = jax.ShapeDtypeStruct((4, ROWS, count), BF16)
    return pl.pallas_call(
        kernel,
        out_shape=(shape, shape),
        in_specs=[
            pl.BlockSpec(memory_space=pltpu.SMEM),
            *[pl.BlockSpec(memory_space=pltpu.VMEM)] * (len(features) + 2),
        ],
        scratch_shapes=scratch,
        compiler_params=vmem(8),
        name="project",
    )(mine, *features, norm_gain[None, :], kv_weight)


def pair_kernel(place, keep_ref, got_ref, own_ref, two_ref, one_ref, three_ref):
    for step, ref in ((2, two_ref), (1, one_ref), (3, three_ref), (0, own_ref)):
        at = lax.rem(place[0] + step, 4)
        total = keep_ref[at].astype(F32) + got_ref[at].astype(F32)
        ref[...] = total.astype(ref.dtype)


def add_pair(keep, got, x_at):
    part = keep.shape[1:]
    return pl.pallas_call(
        pair_kernel,
        out_shape=(jax.ShapeDtypeStruct(part, F32), *[jax.ShapeDtypeStruct(part, BF16)] * 3),
        in_specs=[
            pl.BlockSpec(memory_space=pltpu.SMEM),
            *[pl.BlockSpec(memory_space=pltpu.VMEM)] * 2,
        ],
        compiler_params=vmem(6),
        name="add_pair",
    )(jnp.reshape(x_at, (1,)).astype(jnp.int32), keep, got)


def finish_kernel(slots, *refs):
    *inputs, out_ref = refs
    for lanes, pieces in ((slice(0, TOK), inputs[:4]), (slice(TOK, WIDE), inputs[4:])):
        total = pieces[0][...]
        for ref in pieces[1:]:
            total = total + ref[...].astype(F32)
        inverse = lax.rsqrt((total[TOK : TOK + 1] + total[TOK + 1 : TOK + 2]) / D + 1e-05)
        out_ref[:TOK, lanes] = (total[:TOK] * inverse).astype(BF16)
    lane = lax.broadcasted_iota(jnp.int32, (ROWS - TOK, WIDE), 1)
    out_ref[TOK:, :] = jnp.where(lane < IMG, slots[0], slots[1]).astype(F32).astype(BF16)


def finish_rows(slots, text, image):
    return pl.pallas_call(
        finish_kernel,
        out_shape=jax.ShapeDtypeStruct((ROWS, WIDE), BF16),
        in_specs=[
            pl.BlockSpec(memory_space=pltpu.SMEM),
            *[pl.BlockSpec(memory_space=pltpu.VMEM)] * 8,
        ],
        compiler_params=vmem(6),
        name="finish_rows",
    )(slots, *text, *image)


def ring_gather(block):
    blocks, up, down = [block], block, block
    for _ in range(3):
        up, down = shift(up, Z, 1), shift(down, Z, 7)
        blocks += [up, down]
    return [*blocks, shift(up[:IMG], Z, 1), shift(down[IMG:], Z, 7)]


def exchange(pieces):
    own, two, one, three = pieces
    return [own, shift(two, "x", 2), shift(one, "x", 1), shift(three, "x", 3)]


def merge_kernel(place, *refs):
    *blocks, cos_ref, sin_ref, outer_cos_ref, outer_sin_ref, keys, values, gathered = refs
    for step, ref in zip((0, 7, 1, 6, 2, 5, 3), blocks):
        gathered[lax.rem(place[0] + step, 8)] = ref[...]
    far = lax.rem(place[0] + 4, 8)
    gathered[far, :IMG, :] = blocks[7][...]
    gathered[far, IMG:, :] = blocks[8][...]
    values[:, HEAD:] = jnp.ones((KEYS, HEAD), BF16)

    @pl.loop(0, 8)
    def one_block(block):
        outer_cos, outer_sin = outer_cos_ref[block], outer_sin_ref[block]
        for slot in range(2):
            lanes = slice(slot * IMG, (slot + 1) * IMG)
            here = pl.ds(pl.multiple_of(block * TOK + slot * IMG, IMG), IMG)
            text = gathered[block, :, lanes].astype(F32)
            source = text[TOK : TOK + 1, :]
            rows = text[:TOK, :]
            for r in range(4):
                image = gathered[2 * r + lax.rem(block, 2), :TOK, TOK:]
                rows = jnp.where(source == float(r), image.astype(F32), rows)
            inner_cos, inner_sin = cos_ref[:, lanes], sin_ref[:, lanes]
            cosine = inner_cos * outer_cos - inner_sin * outer_sin
            sine = inner_sin * outer_cos + inner_cos * outer_sin
            first, second = rows[:HALF], rows[HALF:HEAD]
            keys[:HALF, here] = (first * cosine - second * sine).astype(BF16)
            keys[HALF:, here] = (second * cosine + first * sine).astype(BF16)
            values[here, :HEAD] = rows[HEAD:].T.astype(BF16)


def merge(place, blocks, tables):
    return pl.pallas_call(
        merge_kernel,
        out_shape=(
            jax.ShapeDtypeStruct((HEAD, KEYS), BF16),
            jax.ShapeDtypeStruct((KEYS, 2 * HEAD), BF16),
        ),
        in_specs=[
            pl.BlockSpec(memory_space=pltpu.SMEM),
            *[pl.BlockSpec(memory_space=pltpu.VMEM)] * (len(blocks) + len(tables)),
        ],
        scratch_shapes=[pltpu.VMEM((8, ROWS, WIDE), BF16)],
        compiler_params=vmem(10),
        name="merge",
    )(place, *blocks, *tables)


def attend_kernel(step, place, keys, values, query_ref, out_ref, scores, top, mixed):
    z_at, y_at = place[0], place[1]
    block_at = lax.rem(y_at + step, 4)
    count = z_at + jnp.where(y_at <= block_at, 1, 0)
    chunks = (count + PER - 1) // PER
    top[...] = jnp.full(top.shape, NEG, F32)

    def chunk_at(chunk, offset=0, size=CHUNK):
        return pl.ds(pl.multiple_of(chunk * CHUNK + offset, HEAD), size)

    key_at = lax.broadcasted_iota(jnp.int32, (TOK, CHUNK), 1)
    reach = lax.broadcasted_iota(jnp.int32, (TOK, CHUNK), 0) - key_at - (key_at // TOK) * (3 * TOK)

    @pl.loop(0, chunks)
    def score(chunk):
        keys_now = keys[:, chunk_at(chunk)]
        allowed = reach >= ((PER * chunk - z_at) * 4 + y_at - block_at) * TOK
        for h in range(GROUP):
            here = slice(h * TOK, (h + 1) * TOK)
            s = jnp.dot(
                query_ref[:, h * HEAD : (h + 1) * HEAD], keys_now, preferred_element_type=F32
            )
            s = jnp.where(allowed, s, -jnp.inf)
            scores[here, chunk_at(chunk)] = s
            most = top[here, :]
            for lane in range(0, CHUNK, HEAD):
                most = jnp.maximum(most, s[:, lane : lane + HEAD])
            top[here, :] = most

    top[...] = jnp.broadcast_to(jnp.max(top[...], axis=1, keepdims=True), top.shape)

    mixed[...] = jnp.zeros(mixed.shape, F32)

    @pl.loop(0, chunks)
    def weigh(chunk):
        values_now = values[chunk_at(chunk), :]
        for h in range(GROUP):
            here = slice(h * TOK, (h + 1) * TOK)
            most = top[here, :]
            weights = jnp.concatenate(
                [
                    jnp.exp2(scores[here, chunk_at(chunk, lane, HEAD)] - most).astype(BF16)
                    for lane in range(0, CHUNK, HEAD)
                ],
                1,
            )
            rows = jnp.dot(weights, values_now, preferred_element_type=F32)
            mixed[here, :] += rows

    lane = lax.broadcasted_iota(jnp.int32, (TOK, HEAD), 1)
    stats = jnp.zeros((TOK, HEAD), F32)
    for h in range(GROUP):
        here = slice(h * TOK, (h + 1) * TOK)
        total = mixed[here, HEAD:]
        safe = jnp.where(total > 0.0, total, 1.0)
        out_ref[:TOK, h * HEAD : (h + 1) * HEAD] = (mixed[here, :HEAD] / safe).astype(BF16)
        stats = jnp.where(lane == h, top[here, :], jnp.where(lane == GROUP + h, total, stats))
    rows = stats.T
    tops, totals = rows[:GROUP], rows[GROUP : 2 * GROUP]
    some = totals > 0.0
    level = jnp.where(some, tops + jnp.log2(jnp.where(some, totals, 1.0)), NEG)
    high = level.astype(BF16).astype(F32)
    middle = (level - high).astype(BF16).astype(F32)
    low = level - high - middle
    pad = jnp.zeros((ROWS - TOK - 3 * GROUP, TOK), F32)
    out_ref[TOK:, :TOK] = jnp.concatenate([high, middle, low, pad], 0).astype(BF16)
    out_ref[TOK:, TOK:] = jnp.zeros((ROWS - TOK, 2 * HEAD), BF16)


def attend(step, place, keys, values, queries):
    return pl.pallas_call(
        functools.partial(attend_kernel, step),
        out_shape=jax.ShapeDtypeStruct((ROWS, GROUP * HEAD), BF16),
        in_specs=[
            pl.BlockSpec(memory_space=pltpu.SMEM),
            *[pl.BlockSpec(memory_space=pltpu.VMEM)] * 3,
        ],
        scratch_shapes=[
            pltpu.VMEM((ROWS_Q, KEYS), F32),
            pltpu.VMEM((ROWS_Q, HEAD), F32),
            pltpu.VMEM((ROWS_Q, 2 * HEAD), F32),
        ],
        compiler_params=vmem(24),
        cost_estimate=pl.CostEstimate(
            flops=4 * ROWS_Q * KEYS * HEAD, bytes_accessed=2 << 20, transcendentals=ROWS_Q * KEYS
        ),
        name="attend",
    )(place, keys, values, queries)


def layer_norm(values, norm_scale, norm_shift):
    widened = values.astype(F32)
    center = jnp.mean(widened, axis=-1, keepdims=True)
    spread = jnp.mean(jnp.square(widened - center), axis=-1, keepdims=True)
    return ((widened - center) * lax.rsqrt(spread + 1e-06) * norm_scale + norm_shift).astype(BF16)


def combine_kernel(*refs):
    *parts, out_ref = refs
    levels = []
    for ref in parts:
        rows = ref[TOK:, :TOK].astype(F32)
        levels.append(
            [rows[h : h + 1] + rows[4 + h : 5 + h] + rows[8 + h : 9 + h] for h in range(GROUP)]
        )
    weights = []
    for h in range(GROUP):
        most = functools.reduce(jnp.maximum, [level[h] for level in levels])
        raised = [jnp.exp2(level[h] - most) for level in levels]
        total = sum(raised)
        weights += [r / total for r in raised]
    rows = jnp.concatenate([*weights, jnp.zeros((HEAD - len(weights), TOK), F32)], 0).T
    for h in range(GROUP):
        lanes = slice(h * HEAD, (h + 1) * HEAD)
        mixed = sum(
            rows[:, 4 * h + i : 4 * h + i + 1] * ref[:TOK, lanes].astype(F32)
            for i, ref in enumerate(parts)
        )
        out_ref[:, lanes] = mixed.astype(BF16)


def combine(parts):
    return pl.pallas_call(
        combine_kernel,
        out_shape=jax.ShapeDtypeStruct((TOK, GROUP * HEAD), BF16),
        compiler_params=vmem(6),
        name="combine",
    )(*parts)


def body(
    patches,
    patch_gain,
    patch_shift,
    encoder_up,
    encoder_down,
    proj_weight,
    hidden_text,
    slot_source,
    norm_gain,
    kv_weight,
    queries,
):
    z_at, y_at = lax.axis_index(Z), lax.axis_index("y")
    x_at, core = lax.axis_index("x"), lax.axis_index("core")

    place = jnp.stack([z_at, y_at]).astype(jnp.int32)

    normed_patches = layer_norm(patches, patch_gain, patch_shift)
    enc_hidden = jax.nn.gelu(
        jnp.dot(normed_patches, encoder_up, preferred_element_type=F32), approximate=False
    ).astype(BF16)
    partial_out = jnp.dot(enc_hidden, encoder_down, preferred_element_type=F32).astype(BF16)
    halves = partial_out.reshape(2, HALF, -1)
    half = pick(halves, core).astype(F32) + shift(pick(halves, 1 - core), "core", 1).astype(F32)
    sent = half.astype(BF16)
    sent, hidden_text = lax.optimization_barrier((sent, hidden_text))

    give, keep = project(text_project_kernel, [hidden_text], norm_gain, kv_weight, core, TOK, [])
    text_pieces = add_pair(keep, shift(give, "core", 1), x_at)
    for step in (2, 1, 3):
        half = half + shift(sent, "x", step).astype(F32)
    half = (half + pick(patches.reshape(2, HALF, -1), core).astype(F32)).astype(BF16)
    half, text_pieces = lax.optimization_barrier((half, text_pieces))
    text_got = exchange(text_pieces)
    other = shift(half, "core", 1)

    give, keep = project(
        image_project_kernel,
        [half, other, proj_weight],
        norm_gain,
        kv_weight,
        core,
        IMG,
        [pltpu.VMEM(patches.shape, BF16)],
    )
    give, keep, text_got = lax.optimization_barrier((give, keep, text_got))
    image_got = exchange(add_pair(keep, shift(give, "core", 1), x_at))
    blocks = ring_gather(finish_rows(slot_source, text_got, image_got))
    asked = {step: shift(queries, "y", 4 - step) for step in (2, 1, 3)}

    frequencies = jnp.exp(
        jnp.arange(HALF, dtype=F32) * (-2.0 * math.log(500000.0) / (2 * HALF))
    )
    inner = jnp.arange(TOK, dtype=F32)[None, :] * frequencies[:, None]
    starts = ((jnp.arange(8, dtype=jnp.int32) * 4 + y_at) * TOK).astype(F32)
    outer = jnp.broadcast_to(starts[:, None, None] * frequencies[None, :, None], (8, HALF, HEAD))
    factor = SCALE * LOG2E
    tables = (jnp.cos(inner) * factor, jnp.sin(inner) * factor, jnp.cos(outer), jnp.sin(outer))
    keys, values = merge(place, blocks, tables)
    received = []
    for step in (2, 1, 3):
        received.append(shift(attend(step, place, keys, values, asked[step]), "y", step))
    return combine([attend(0, place, keys, values, queries), *received])


def solution(mesh):
    split = Mesh(mesh.devices.reshape(4, 2, 4, 4, 2), ("zh", "zl", "y", "x", "core"))
    seq = ("zh", "zl", "y")
    in_specs = (
        P(seq, None),
        P(),
        P(),
        P(None, TP),
        P(TP, None),
        P(None, TP),
        P(seq, TP),
        P(seq),
        P(TP),
        P(None, TP),
        P(seq, TP),
    )
    return jax.shard_map(
        body, mesh=split, in_specs=in_specs, out_specs=P(seq, TP), check_vma=False
    )
```

```python
import functools
import math

import jax
import jax.numpy as jnp
from jax import lax
from jax.experimental import pallas as pl
from jax.experimental.pallas import tpu as pltpu
from jax.sharding import Mesh
from jax.sharding import PartitionSpec as P

D = 8192
HEAD = 128
HALF = 64
GROUP = 4
TOK = 256
IMG = 128
ROWS = 272
TP = ("x", "core")
Z = ("zh", "zl")
BF16 = jnp.bfloat16
F32 = jnp.float32
NEG = -1e30
LOG2E = math.log2(math.e)
WIDE = TOK + IMG
KEYS = 2048
CHUNK = 1024
PER = CHUNK // TOK
ROWS_Q = GROUP * TOK
SCALE = HEAD ** (-0.5)


def shift(values, axis, step):
    count = lax.axis_size(axis)
    return lax.ppermute(values, axis, [(i, (i + step) % count) for i in range(count)])


def pick(values, index):
    return lax.dynamic_index_in_dim(values, index, 0, keepdims=False)


def vmem(mib):
    return pltpu.CompilerParams(vmem_limit_bytes=mib * 1024 * 1024)


def split_squares(column, count):
    row = jnp.broadcast_to(column, (count, HEAD)).T[:16]
    high = row.astype(BF16).astype(F32)
    at = lax.broadcasted_iota(jnp.int32, row.shape, 0)
    return jnp.where(at == 0, high, jnp.where(at == 1, row - high, 0.0)).astype(BF16)


def head_rows(core, features, tail, weight_ref, give_ref, keep_ref):
    for x_at in range(4):
        for own, ref in ((0, give_ref), (1, keep_ref)):
            head = 2 * x_at + jnp.where(own == 1, core, 1 - core)
            weight = weight_ref[pl.ds(pl.multiple_of(head * TOK, TOK), TOK), :]
            rows = lax.dot_general(
                weight, features, (((1,), (1,)), ((), ())), preferred_element_type=F32
            )
            ref[x_at, :TOK, :] = rows.astype(BF16)
            ref[x_at, TOK:, :] = tail


def gain_features(features, gain_ref):
    widened = features.astype(F32)
    squares = jnp.sum(jnp.square(widened), axis=1, keepdims=True)
    return (widened * gain_ref[...]).astype(BF16), split_squares(squares, features.shape[0])


def text_project_kernel(core, hidden_ref, gain_ref, weight_ref, give_ref, keep_ref):
    gained, tail = gain_features(hidden_ref[...], gain_ref)
    head_rows(core[0], gained, tail, weight_ref, give_ref, keep_ref)


def image_project_kernel(
    core, half_ref, other_ref, proj_ref, gain_ref, weight_ref, give_ref, keep_ref, encoded
):
    at = pl.multiple_of(core[0] * HALF, HALF)
    encoded[pl.ds(at, HALF), :] = half_ref[...]
    encoded[pl.ds(HALF - at, HALF), :] = other_ref[...]
    image = jnp.dot(encoded[...], proj_ref[...], preferred_element_type=F32).astype(BF16)
    gained, tail = gain_features(image, gain_ref)
    head_rows(core[0], gained, tail, weight_ref, give_ref, keep_ref)


def project(kernel, features, norm_gain, kv_weight, core, count, scratch):
    mine = jnp.reshape(core, (1,)).astype(jnp.int32)
    shape = jax.ShapeDtypeStruct((4, ROWS, count), BF16)
    return pl.pallas_call(
        kernel,
        out_shape=(shape, shape),
        in_specs=[
            pl.BlockSpec(memory_space=pltpu.SMEM),
            *[pl.BlockSpec(memory_space=pltpu.VMEM)] * (len(features) + 2),
        ],
        scratch_shapes=scratch,
        compiler_params=vmem(8),
        name="project",
    )(mine, *features, norm_gain[None, :], kv_weight)


def pair_kernel(place, keep_ref, got_ref, own_ref, two_ref, one_ref, three_ref):
    for step, ref in ((2, two_ref), (1, one_ref), (3, three_ref), (0, own_ref)):
        at = lax.rem(place[0] + step, 4)
        total = keep_ref[at].astype(F32) + got_ref[at].astype(F32)
        ref[...] = total.astype(ref.dtype)


def add_pair(keep, got, x_at):
    part = keep.shape[1:]
    return pl.pallas_call(
        pair_kernel,
        out_shape=(jax.ShapeDtypeStruct(part, F32), *[jax.ShapeDtypeStruct(part, BF16)] * 3),
        in_specs=[
            pl.BlockSpec(memory_space=pltpu.SMEM),
            *[pl.BlockSpec(memory_space=pltpu.VMEM)] * 2,
        ],
        compiler_params=vmem(6),
        name="add_pair",
    )(jnp.reshape(x_at, (1,)).astype(jnp.int32), keep, got)


def finish_kernel(slots, *refs):
    *inputs, out_ref = refs
    for lanes, pieces in ((slice(0, TOK), inputs[:4]), (slice(TOK, WIDE), inputs[4:])):
        total = pieces[0][...]
        for ref in pieces[1:]:
            total = total + ref[...].astype(F32)
        inverse = lax.rsqrt((total[TOK : TOK + 1] + total[TOK + 1 : TOK + 2]) / D + 1e-05)
        out_ref[:TOK, lanes] = (total[:TOK] * inverse).astype(BF16)
    lane = lax.broadcasted_iota(jnp.int32, (ROWS - TOK, WIDE), 1)
    out_ref[TOK:, :] = jnp.where(lane < IMG, slots[0], slots[1]).astype(F32).astype(BF16)


def finish_rows(slots, text, image):
    return pl.pallas_call(
        finish_kernel,
        out_shape=jax.ShapeDtypeStruct((ROWS, WIDE), BF16),
        in_specs=[
            pl.BlockSpec(memory_space=pltpu.SMEM),
            *[pl.BlockSpec(memory_space=pltpu.VMEM)] * 8,
        ],
        compiler_params=vmem(6),
        name="finish_rows",
    )(slots, *text, *image)


def ring_gather(block, asked):
    up1, down1 = shift(block, Z, 1), shift(block, Z, 7)
    up2, down2 = shift(up1, Z, 1), shift(down1, Z, 7)
    up2, down2, asked = lax.optimization_barrier((up2, down2, asked))
    up3, down3 = shift(up2, Z, 1), shift(down2, Z, 7)
    far = [shift(up2[:IMG], Z, 2), shift(down2[IMG:], Z, 6)]
    return [block, up1, down1, up2, down2, up3, down3, *far], asked


def exchange(pieces):
    own, two, one, three = pieces
    return [own, shift(two, "x", 2), shift(one, "x", 1), shift(three, "x", 3)]


def merge_kernel(place, *refs):
    *blocks, cos_ref, sin_ref, outer_cos_ref, outer_sin_ref, keys, values, gathered = refs
    for step, ref in zip((0, 7, 1, 6, 2, 5, 3), blocks):
        gathered[lax.rem(place[0] + step, 8)] = ref[...]
    far = lax.rem(place[0] + 4, 8)
    gathered[far, :IMG, :] = blocks[7][...]
    gathered[far, IMG:, :] = blocks[8][...]
    values[:, HEAD:] = jnp.ones((KEYS, HEAD), BF16)

    @pl.loop(0, 8)
    def one_block(block):
        outer_cos, outer_sin = outer_cos_ref[block], outer_sin_ref[block]
        for slot in range(2):
            lanes = slice(slot * IMG, (slot + 1) * IMG)
            here = pl.ds(pl.multiple_of(block * TOK + slot * IMG, IMG), IMG)
            text = gathered[block, :, lanes].astype(F32)
            source = text[TOK : TOK + 1, :]
            rows = text[:TOK, :]
            for r in range(4):
                image = gathered[2 * r + lax.rem(block, 2), :TOK, TOK:]
                rows = jnp.where(source == float(r), image.astype(F32), rows)
            inner_cos, inner_sin = cos_ref[:, lanes], sin_ref[:, lanes]
            cosine = inner_cos * outer_cos - inner_sin * outer_sin
            sine = inner_sin * outer_cos + inner_cos * outer_sin
            first, second = rows[:HALF], rows[HALF:HEAD]
            keys[:HALF, here] = (first * cosine - second * sine).astype(BF16)
            keys[HALF:, here] = (second * cosine + first * sine).astype(BF16)
            values[here, :HEAD] = rows[HEAD:].T.astype(BF16)


def merge(place, blocks, tables):
    return pl.pallas_call(
        merge_kernel,
        out_shape=(
            jax.ShapeDtypeStruct((HEAD, KEYS), BF16),
            jax.ShapeDtypeStruct((KEYS, 2 * HEAD), BF16),
        ),
        in_specs=[
            pl.BlockSpec(memory_space=pltpu.SMEM),
            *[pl.BlockSpec(memory_space=pltpu.VMEM)] * (len(blocks) + len(tables)),
        ],
        scratch_shapes=[pltpu.VMEM((8, ROWS, WIDE), BF16)],
        compiler_params=vmem(10),
        name="merge",
    )(place, *blocks, *tables)


def attend_kernel(step, place, keys, values, query_ref, out_ref, scores, top, mixed):
    z_at, y_at = place[0], place[1]
    block_at = lax.rem(y_at + step, 4)
    count = z_at + jnp.where(y_at <= block_at, 1, 0)
    chunks = (count + PER - 1) // PER
    top[...] = jnp.full(top.shape, NEG, F32)

    def chunk_at(chunk, offset=0, size=CHUNK):
        return pl.ds(pl.multiple_of(chunk * CHUNK + offset, HEAD), size)

    key_at = lax.broadcasted_iota(jnp.int32, (TOK, CHUNK), 1)
    reach = lax.broadcasted_iota(jnp.int32, (TOK, CHUNK), 0) - key_at - (key_at // TOK) * (3 * TOK)

    @pl.loop(0, chunks)
    def score(chunk):
        keys_now = keys[:, chunk_at(chunk)]
        allowed = reach >= ((PER * chunk - z_at) * 4 + y_at - block_at) * TOK
        for h in range(GROUP):
            here = slice(h * TOK, (h + 1) * TOK)
            s = jnp.dot(
                query_ref[:, h * HEAD : (h + 1) * HEAD], keys_now, preferred_element_type=F32
            )
            s = jnp.where(allowed, s, -jnp.inf)
            scores[here, chunk_at(chunk)] = s
            most = top[here, :]
            for lane in range(0, CHUNK, HEAD):
                most = jnp.maximum(most, s[:, lane : lane + HEAD])
            top[here, :] = most

    top[...] = jnp.broadcast_to(jnp.max(top[...], axis=1, keepdims=True), top.shape)

    mixed[...] = jnp.zeros(mixed.shape, F32)

    @pl.loop(0, chunks)
    def weigh(chunk):
        values_now = values[chunk_at(chunk), :]
        for h in range(GROUP):
            here = slice(h * TOK, (h + 1) * TOK)
            most = top[here, :]
            weights = jnp.concatenate(
                [
                    jnp.exp2(scores[here, chunk_at(chunk, lane, HEAD)] - most).astype(BF16)
                    for lane in range(0, CHUNK, HEAD)
                ],
                1,
            )
            rows = jnp.dot(weights, values_now, preferred_element_type=F32)
            mixed[here, :] += rows

    lane = lax.broadcasted_iota(jnp.int32, (TOK, HEAD), 1)
    stats = jnp.zeros((TOK, HEAD), F32)
    for h in range(GROUP):
        here = slice(h * TOK, (h + 1) * TOK)
        total = mixed[here, HEAD:]
        safe = jnp.where(total > 0.0, total, 1.0)
        out_ref[:TOK, h * HEAD : (h + 1) * HEAD] = (mixed[here, :HEAD] / safe).astype(BF16)
        stats = jnp.where(lane == h, top[here, :], jnp.where(lane == GROUP + h, total, stats))
    rows = stats.T
    tops, totals = rows[:GROUP], rows[GROUP : 2 * GROUP]
    some = totals > 0.0
    level = jnp.where(some, tops + jnp.log2(jnp.where(some, totals, 1.0)), NEG)
    high = level.astype(BF16).astype(F32)
    middle = (level - high).astype(BF16).astype(F32)
    low = level - high - middle
    pad = jnp.zeros((ROWS - TOK - 3 * GROUP, TOK), F32)
    out_ref[TOK:, :TOK] = jnp.concatenate([high, middle, low, pad], 0).astype(BF16)
    out_ref[TOK:, TOK:] = jnp.zeros((ROWS - TOK, 2 * HEAD), BF16)


def attend(step, place, keys, values, queries):
    return pl.pallas_call(
        functools.partial(attend_kernel, step),
        out_shape=jax.ShapeDtypeStruct((ROWS, GROUP * HEAD), BF16),
        in_specs=[
            pl.BlockSpec(memory_space=pltpu.SMEM),
            *[pl.BlockSpec(memory_space=pltpu.VMEM)] * 3,
        ],
        scratch_shapes=[
            pltpu.VMEM((ROWS_Q, KEYS), F32),
            pltpu.VMEM((ROWS_Q, HEAD), F32),
            pltpu.VMEM((ROWS_Q, 2 * HEAD), F32),
        ],
        compiler_params=vmem(24),
        cost_estimate=pl.CostEstimate(
            flops=4 * ROWS_Q * KEYS * HEAD, bytes_accessed=2 << 20, transcendentals=ROWS_Q * KEYS
        ),
        name="attend",
    )(place, keys, values, queries)


def layer_norm(values, norm_scale, norm_shift):
    widened = values.astype(F32)
    center = jnp.mean(widened, axis=-1, keepdims=True)
    spread = jnp.mean(jnp.square(widened - center), axis=-1, keepdims=True)
    return ((widened - center) * lax.rsqrt(spread + 1e-06) * norm_scale + norm_shift).astype(BF16)


def combine_kernel(*refs):
    *parts, out_ref = refs
    levels = []
    for ref in parts:
        rows = ref[TOK:, :TOK].astype(F32)
        levels.append(
            [rows[h : h + 1] + rows[4 + h : 5 + h] + rows[8 + h : 9 + h] for h in range(GROUP)]
        )
    weights = []
    for h in range(GROUP):
        most = functools.reduce(jnp.maximum, [level[h] for level in levels])
        raised = [jnp.exp2(level[h] - most) for level in levels]
        total = sum(raised)
        weights += [r / total for r in raised]
    rows = jnp.concatenate([*weights, jnp.zeros((HEAD - len(weights), TOK), F32)], 0).T
    for h in range(GROUP):
        lanes = slice(h * HEAD, (h + 1) * HEAD)
        mixed = sum(
            rows[:, 4 * h + i : 4 * h + i + 1] * ref[:TOK, lanes].astype(F32)
            for i, ref in enumerate(parts)
        )
        out_ref[:, lanes] = mixed.astype(BF16)


def combine(parts):
    return pl.pallas_call(
        combine_kernel,
        out_shape=jax.ShapeDtypeStruct((TOK, GROUP * HEAD), BF16),
        compiler_params=vmem(6),
        name="combine",
    )(*parts)


def body(
    patches,
    patch_gain,
    patch_shift,
    encoder_up,
    encoder_down,
    proj_weight,
    hidden_text,
    slot_source,
    norm_gain,
    kv_weight,
    queries,
):
    z_at, y_at = lax.axis_index(Z), lax.axis_index("y")
    x_at, core = lax.axis_index("x"), lax.axis_index("core")

    place = jnp.stack([z_at, y_at]).astype(jnp.int32)

    normed_patches = layer_norm(patches, patch_gain, patch_shift)
    enc_hidden = jax.nn.gelu(
        jnp.dot(normed_patches, encoder_up, preferred_element_type=F32), approximate=False
    ).astype(BF16)
    partial_out = jnp.dot(enc_hidden, encoder_down, preferred_element_type=F32).astype(BF16)
    halves = partial_out.reshape(2, HALF, -1)
    half = pick(halves, core).astype(F32) + shift(pick(halves, 1 - core), "core", 1).astype(F32)
    sent = half.astype(BF16)
    sent, hidden_text = lax.optimization_barrier((sent, hidden_text))

    give, keep = project(text_project_kernel, [hidden_text], norm_gain, kv_weight, core, TOK, [])
    text_pieces = add_pair(keep, shift(give, "core", 1), x_at)
    for step in (2, 1, 3):
        half = half + shift(sent, "x", step).astype(F32)
    half = (half + pick(patches.reshape(2, HALF, -1), core).astype(F32)).astype(BF16)
    half, text_pieces = lax.optimization_barrier((half, text_pieces))
    text_got = exchange(text_pieces)
    other = shift(half, "core", 1)

    give, keep = project(
        image_project_kernel,
        [half, other, proj_weight],
        norm_gain,
        kv_weight,
        core,
        IMG,
        [pltpu.VMEM(patches.shape, BF16)],
    )
    give, keep, text_got = lax.optimization_barrier((give, keep, text_got))
    image_got = exchange(add_pair(keep, shift(give, "core", 1), x_at))
    asked = {step: shift(queries, "y", 4 - step) for step in (2, 1, 3)}
    blocks, asked = ring_gather(finish_rows(slot_source, text_got, image_got), asked)

    frequencies = jnp.exp(
        jnp.arange(HALF, dtype=F32) * (-2.0 * math.log(500000.0) / (2 * HALF))
    )
    inner = jnp.arange(TOK, dtype=F32)[None, :] * frequencies[:, None]
    starts = ((jnp.arange(8, dtype=jnp.int32) * 4 + y_at) * TOK).astype(F32)
    outer = jnp.broadcast_to(starts[:, None, None] * frequencies[None, :, None], (8, HALF, HEAD))
    factor = SCALE * LOG2E
    tables = (jnp.cos(inner) * factor, jnp.sin(inner) * factor, jnp.cos(outer), jnp.sin(outer))
    keys, values = merge(place, blocks, tables)
    received = []
    for step in (2, 1, 3):
        received.append(shift(attend(step, place, keys, values, asked[step]), "y", step))
    return combine([attend(0, place, keys, values, queries), *received])


def solution(mesh):
    split = Mesh(mesh.devices.reshape(4, 2, 4, 4, 2), ("zh", "zl", "y", "x", "core"))
    seq = ("zh", "zl", "y")
    in_specs = (
        P(seq, None),
        P(),
        P(),
        P(None, TP),
        P(TP, None),
        P(None, TP),
        P(seq, TP),
        P(seq),
        P(TP),
        P(None, TP),
        P(seq, TP),
    )
    return jax.shard_map(
        body, mesh=split, in_specs=in_specs, out_specs=P(seq, TP), check_vma=False
    )
```

```python
import functools
import math

import jax
import jax.numpy as jnp
from jax import lax
from jax.experimental import pallas as pl
from jax.experimental.pallas import tpu as pltpu
from jax.sharding import Mesh
from jax.sharding import PartitionSpec as P

D = 8192
HEAD = 128
HALF = 64
GROUP = 4
TOK = 256
IMG = 128
ROWS = 272
TP = ("x", "core")
Z = ("zh", "zl")
BF16 = jnp.bfloat16
F32 = jnp.float32
NEG = -1e30
LOG2E = math.log2(math.e)
WIDE = TOK + IMG
KEYS = 2048
CHUNK = 1024
PER = CHUNK // TOK
ROWS_Q = GROUP * TOK
SCALE = HEAD ** (-0.5)


def shift(values, axis, step):
    count = lax.axis_size(axis)
    return lax.ppermute(values, axis, [(i, (i + step) % count) for i in range(count)])


def pick(values, index):
    return lax.dynamic_index_in_dim(values, index, 0, keepdims=False)


def vmem(mib):
    return pltpu.CompilerParams(vmem_limit_bytes=mib * 1024 * 1024)


def split_squares(column, count):
    row = jnp.broadcast_to(column, (count, HEAD)).T[:16]
    high = row.astype(BF16).astype(F32)
    at = lax.broadcasted_iota(jnp.int32, row.shape, 0)
    return jnp.where(at == 0, high, jnp.where(at == 1, row - high, 0.0)).astype(BF16)


def head_rows(core, features, tail, weight_ref, give_ref, keep_ref):
    for x_at in range(4):
        for own, ref in ((0, give_ref), (1, keep_ref)):
            head = 2 * x_at + jnp.where(own == 1, core, 1 - core)
            weight = weight_ref[pl.ds(pl.multiple_of(head * TOK, TOK), TOK), :]
            rows = lax.dot_general(
                weight, features, (((1,), (1,)), ((), ())), preferred_element_type=F32
            )
            ref[x_at, :TOK, :] = rows.astype(BF16)
            ref[x_at, TOK:, :] = tail


def gain_features(features, gain_ref):
    widened = features.astype(F32)
    squares = jnp.sum(jnp.square(widened), axis=1, keepdims=True)
    return (widened * gain_ref[...]).astype(BF16), split_squares(squares, features.shape[0])


def text_project_kernel(core, hidden_ref, gain_ref, weight_ref, give_ref, keep_ref):
    gained, tail = gain_features(hidden_ref[...], gain_ref)
    head_rows(core[0], gained, tail, weight_ref, give_ref, keep_ref)


def image_project_kernel(
    core, half_ref, other_ref, proj_ref, gain_ref, weight_ref, give_ref, keep_ref, encoded
):
    at = pl.multiple_of(core[0] * HALF, HALF)
    encoded[pl.ds(at, HALF), :] = half_ref[...]
    encoded[pl.ds(HALF - at, HALF), :] = other_ref[...]
    image = jnp.dot(encoded[...], proj_ref[...], preferred_element_type=F32).astype(BF16)
    gained, tail = gain_features(image, gain_ref)
    head_rows(core[0], gained, tail, weight_ref, give_ref, keep_ref)


def project(kernel, features, norm_gain, kv_weight, core, count, scratch):
    mine = jnp.reshape(core, (1,)).astype(jnp.int32)
    shape = jax.ShapeDtypeStruct((4, ROWS, count), BF16)
    return pl.pallas_call(
        kernel,
        out_shape=(shape, shape),
        in_specs=[
            pl.BlockSpec(memory_space=pltpu.SMEM),
            *[pl.BlockSpec(memory_space=pltpu.VMEM)] * (len(features) + 2),
        ],
        scratch_shapes=scratch,
        compiler_params=vmem(8),
        name="project",
    )(mine, *features, norm_gain[None, :], kv_weight)


def pair_kernel(place, keep_ref, got_ref, own_ref, two_ref, one_ref, three_ref):
    for step, ref in ((2, two_ref), (1, one_ref), (3, three_ref), (0, own_ref)):
        at = lax.rem(place[0] + step, 4)
        total = keep_ref[at].astype(F32) + got_ref[at].astype(F32)
        ref[...] = total.astype(ref.dtype)


def add_pair(keep, got, x_at):
    part = keep.shape[1:]
    return pl.pallas_call(
        pair_kernel,
        out_shape=(jax.ShapeDtypeStruct(part, F32), *[jax.ShapeDtypeStruct(part, BF16)] * 3),
        in_specs=[
            pl.BlockSpec(memory_space=pltpu.SMEM),
            *[pl.BlockSpec(memory_space=pltpu.VMEM)] * 2,
        ],
        compiler_params=vmem(6),
        name="add_pair",
    )(jnp.reshape(x_at, (1,)).astype(jnp.int32), keep, got)


def finish_kernel(slots, *refs):
    *inputs, out_ref = refs
    for lanes, pieces in ((slice(0, TOK), inputs[:4]), (slice(TOK, WIDE), inputs[4:])):
        total = pieces[0][...]
        for ref in pieces[1:]:
            total = total + ref[...].astype(F32)
        inverse = lax.rsqrt((total[TOK : TOK + 1] + total[TOK + 1 : TOK + 2]) / D + 1e-05)
        out_ref[:TOK, lanes] = (total[:TOK] * inverse).astype(BF16)
    lane = lax.broadcasted_iota(jnp.int32, (ROWS - TOK, WIDE), 1)
    out_ref[TOK:, :] = jnp.where(lane < IMG, slots[0], slots[1]).astype(F32).astype(BF16)


def finish_rows(slots, text, image):
    return pl.pallas_call(
        finish_kernel,
        out_shape=jax.ShapeDtypeStruct((ROWS, WIDE), BF16),
        in_specs=[
            pl.BlockSpec(memory_space=pltpu.SMEM),
            *[pl.BlockSpec(memory_space=pltpu.VMEM)] * 8,
        ],
        compiler_params=vmem(6),
        name="finish_rows",
    )(slots, *text, *image)


def ring_gather(block):
    blocks, up, down = [block], block, block
    for _ in range(3):
        up, down = shift(up, Z, 1), shift(down, Z, 7)
        blocks += [up, down]
    return [*blocks, shift(up[:IMG], Z, 1), shift(down[IMG:], Z, 7)]


def exchange(pieces):
    own, two, one, three = pieces
    return [own, shift(two, "x", 2), shift(one, "x", 1), shift(three, "x", 3)]


def merge_kernel(place, *refs):
    *blocks, cos_ref, sin_ref, outer_cos_ref, outer_sin_ref, keys, values, gathered = refs
    for step, ref in zip((0, 7, 1, 6, 2, 5, 3), blocks):
        gathered[lax.rem(place[0] + step, 8)] = ref[...]
    far = lax.rem(place[0] + 4, 8)
    gathered[far, :IMG, :] = blocks[7][...]
    gathered[far, IMG:, :] = blocks[8][...]
    values[:, HEAD:] = jnp.ones((KEYS, HEAD), BF16)

    @pl.loop(0, 8)
    def one_block(block):
        outer_cos, outer_sin = outer_cos_ref[block], outer_sin_ref[block]
        for slot in range(2):
            lanes = slice(slot * IMG, (slot + 1) * IMG)
            here = pl.ds(pl.multiple_of(block * TOK + slot * IMG, IMG), IMG)
            text = gathered[block, :, lanes].astype(F32)
            source = text[TOK : TOK + 1, :]
            rows = text[:TOK, :]
            for r in range(4):
                image = gathered[2 * r + lax.rem(block, 2), :TOK, TOK:]
                rows = jnp.where(source == float(r), image.astype(F32), rows)
            inner_cos, inner_sin = cos_ref[:, lanes], sin_ref[:, lanes]
            cosine = inner_cos * outer_cos - inner_sin * outer_sin
            sine = inner_sin * outer_cos + inner_cos * outer_sin
            first, second = rows[:HALF], rows[HALF:HEAD]
            keys[:HALF, here] = (first * cosine - second * sine).astype(BF16)
            keys[HALF:, here] = (second * cosine + first * sine).astype(BF16)
            values[here, :HEAD] = rows[HEAD:].T.astype(BF16)


def merge(place, blocks, tables):
    return pl.pallas_call(
        merge_kernel,
        out_shape=(
            jax.ShapeDtypeStruct((HEAD, KEYS), BF16),
            jax.ShapeDtypeStruct((KEYS, 2 * HEAD), BF16),
        ),
        in_specs=[
            pl.BlockSpec(memory_space=pltpu.SMEM),
            *[pl.BlockSpec(memory_space=pltpu.VMEM)] * (len(blocks) + len(tables)),
        ],
        scratch_shapes=[pltpu.VMEM((8, ROWS, WIDE), BF16)],
        compiler_params=vmem(10),
        name="merge",
    )(place, *blocks, *tables)


def attend_kernel(step, place, keys, values, query_ref, out_ref, scores, top, mixed):
    z_at, y_at = place[0], place[1]
    block_at = lax.rem(y_at + step, 4)
    full = z_at + jnp.where(y_at < block_at, 1, 0)
    count = z_at + jnp.where(y_at <= block_at, 1, 0)
    plain = full // PER
    chunks = (count + PER - 1) // PER
    top[...] = jnp.full(top.shape, NEG, F32)

    def chunk_at(chunk, offset=0, size=CHUNK):
        return pl.ds(pl.multiple_of(chunk * CHUNK + offset, HEAD), size)

    def score(chunk, masked):
        keys_now = keys[:, chunk_at(chunk)]
        if masked:
            key_at = lax.broadcasted_iota(jnp.int32, (TOK, CHUNK), 1)
            key_at = key_at + (key_at // TOK) * (3 * TOK)
            query_at = lax.broadcasted_iota(jnp.int32, (TOK, CHUNK), 0)
            offset = ((PER * chunk - z_at) * 4 + y_at - block_at) * TOK
            allowed = key_at + offset <= query_at
        for h in range(GROUP):
            here = slice(h * TOK, (h + 1) * TOK)
            s = jnp.dot(
                query_ref[:, h * HEAD : (h + 1) * HEAD], keys_now, preferred_element_type=F32
            )
            if masked:
                s = jnp.where(allowed, s, -jnp.inf)
            scores[here, chunk_at(chunk)] = s
            most = top[here, :]
            for lane in range(0, CHUNK, HEAD):
                most = jnp.maximum(most, s[:, lane : lane + HEAD])
            top[here, :] = most

    pl.loop(0, plain)(lambda chunk: score(chunk, False))

    @pl.when(chunks > plain)
    def last():
        score(plain, True)

    top[...] = jnp.broadcast_to(jnp.max(top[...], axis=1, keepdims=True), top.shape)

    mixed[...] = jnp.zeros(mixed.shape, F32)

    @pl.loop(0, chunks)
    def weigh(chunk):
        values_now = values[chunk_at(chunk), :]
        for h in range(GROUP):
            here = slice(h * TOK, (h + 1) * TOK)
            most = top[here, :]
            weights = jnp.concatenate(
                [
                    jnp.exp2(scores[here, chunk_at(chunk, lane, HEAD)] - most).astype(BF16)
                    for lane in range(0, CHUNK, HEAD)
                ],
                1,
            )
            rows = jnp.dot(weights, values_now, preferred_element_type=F32)
            mixed[here, :] += rows

    lane = lax.broadcasted_iota(jnp.int32, (TOK, HEAD), 1)
    stats = jnp.zeros((TOK, HEAD), F32)
    for h in range(GROUP):
        here = slice(h * TOK, (h + 1) * TOK)
        total = mixed[here, HEAD:]
        safe = jnp.where(total > 0.0, total, 1.0)
        out_ref[:TOK, h * HEAD : (h + 1) * HEAD] = (mixed[here, :HEAD] / safe).astype(BF16)
        stats = jnp.where(lane == h, top[here, :], jnp.where(lane == GROUP + h, total, stats))
    rows = stats.T
    tops, totals = rows[:GROUP], rows[GROUP : 2 * GROUP]
    some = totals > 0.0
    level = jnp.where(some, tops + jnp.log2(jnp.where(some, totals, 1.0)), NEG)
    high = level.astype(BF16).astype(F32)
    middle = (level - high).astype(BF16).astype(F32)
    low = level - high - middle
    pad = jnp.zeros((ROWS - TOK - 3 * GROUP, TOK), F32)
    out_ref[TOK:, :TOK] = jnp.concatenate([high, middle, low, pad], 0).astype(BF16)
    out_ref[TOK:, TOK:] = jnp.zeros((ROWS - TOK, 2 * HEAD), BF16)


def attend(step, place, keys, values, queries):
    return pl.pallas_call(
        functools.partial(attend_kernel, step),
        out_shape=jax.ShapeDtypeStruct((ROWS, GROUP * HEAD), BF16),
        in_specs=[
            pl.BlockSpec(memory_space=pltpu.SMEM),
            *[pl.BlockSpec(memory_space=pltpu.VMEM)] * 3,
        ],
        scratch_shapes=[
            pltpu.VMEM((ROWS_Q, KEYS), F32),
            pltpu.VMEM((ROWS_Q, HEAD), F32),
            pltpu.VMEM((ROWS_Q, 2 * HEAD), F32),
        ],
        compiler_params=vmem(24),
        cost_estimate=pl.CostEstimate(
            flops=4 * ROWS_Q * KEYS * HEAD, bytes_accessed=2 << 20, transcendentals=ROWS_Q * KEYS
        ),
        name="attend",
    )(place, keys, values, queries)


def layer_norm(values, norm_scale, norm_shift):
    widened = values.astype(F32)
    center = jnp.mean(widened, axis=-1, keepdims=True)
    spread = jnp.mean(jnp.square(widened - center), axis=-1, keepdims=True)
    return ((widened - center) * lax.rsqrt(spread + 1e-06) * norm_scale + norm_shift).astype(BF16)


def combine_kernel(*refs):
    *parts, out_ref = refs
    levels = []
    for ref in parts:
        rows = ref[TOK:, :TOK].astype(F32)
        levels.append(
            [rows[h : h + 1] + rows[4 + h : 5 + h] + rows[8 + h : 9 + h] for h in range(GROUP)]
        )
    weights = []
    for h in range(GROUP):
        most = functools.reduce(jnp.maximum, [level[h] for level in levels])
        raised = [jnp.exp2(level[h] - most) for level in levels]
        total = sum(raised)
        weights += [r / total for r in raised]
    rows = jnp.concatenate([*weights, jnp.zeros((HEAD - len(weights), TOK), F32)], 0).T
    for h in range(GROUP):
        lanes = slice(h * HEAD, (h + 1) * HEAD)
        mixed = sum(
            rows[:, 4 * h + i : 4 * h + i + 1] * ref[:TOK, lanes].astype(F32)
            for i, ref in enumerate(parts)
        )
        out_ref[:, lanes] = mixed.astype(BF16)


def combine(parts):
    return pl.pallas_call(
        combine_kernel,
        out_shape=jax.ShapeDtypeStruct((TOK, GROUP * HEAD), BF16),
        compiler_params=vmem(6),
        name="combine",
    )(*parts)


def body(
    patches,
    patch_gain,
    patch_shift,
    encoder_up,
    encoder_down,
    proj_weight,
    hidden_text,
    slot_source,
    norm_gain,
    kv_weight,
    queries,
):
    z_at, y_at = lax.axis_index(Z), lax.axis_index("y")
    x_at, core = lax.axis_index("x"), lax.axis_index("core")

    place = jnp.stack([z_at, y_at]).astype(jnp.int32)

    normed_patches = layer_norm(patches, patch_gain, patch_shift)
    enc_hidden = jax.nn.gelu(
        jnp.dot(normed_patches, encoder_up, preferred_element_type=F32), approximate=False
    ).astype(BF16)
    partial_out = jnp.dot(enc_hidden, encoder_down, preferred_element_type=F32).astype(BF16)
    halves = partial_out.reshape(2, HALF, -1)
    half = pick(halves, core).astype(F32) + shift(pick(halves, 1 - core), "core", 1).astype(F32)
    sent = half.astype(BF16)
    sent, hidden_text = lax.optimization_barrier((sent, hidden_text))

    give, keep = project(text_project_kernel, [hidden_text], norm_gain, kv_weight, core, TOK, [])
    text_pieces = add_pair(keep, shift(give, "core", 1), x_at)
    for step in (2, 1, 3):
        half = half + shift(sent, "x", step).astype(F32)
    half = (half + pick(patches.reshape(2, HALF, -1), core).astype(F32)).astype(BF16)
    half, text_pieces = lax.optimization_barrier((half, text_pieces))
    text_got = exchange(text_pieces)
    other = shift(half, "core", 1)

    give, keep = project(
        image_project_kernel,
        [half, other, proj_weight],
        norm_gain,
        kv_weight,
        core,
        IMG,
        [pltpu.VMEM(patches.shape, BF16)],
    )
    give, keep, text_got = lax.optimization_barrier((give, keep, text_got))
    image_got = exchange(add_pair(keep, shift(give, "core", 1), x_at))
    blocks = ring_gather(finish_rows(slot_source, text_got, image_got))
    asked = {step: shift(queries, "y", 4 - step) for step in (2, 1, 3)}

    frequencies = jnp.exp(
        jnp.arange(HALF, dtype=F32) * (-2.0 * math.log(500000.0) / (2 * HALF))
    )
    inner = jnp.arange(TOK, dtype=F32)[None, :] * frequencies[:, None]
    starts = ((jnp.arange(8, dtype=jnp.int32) * 4 + y_at) * TOK).astype(F32)
    outer = jnp.broadcast_to(starts[:, None, None] * frequencies[None, :, None], (8, HALF, HEAD))
    factor = SCALE * LOG2E
    tables = (jnp.cos(inner) * factor, jnp.sin(inner) * factor, jnp.cos(outer), jnp.sin(outer))
    keys, values = merge(place, blocks, tables)
    received = []
    for step in (2, 1, 3):
        received.append(shift(attend(step, place, keys, values, asked[step]), "y", step))
    return combine([attend(0, place, keys, values, queries), *received])


def solution(mesh):
    split = Mesh(mesh.devices.reshape(4, 2, 4, 4, 2), ("zh", "zl", "y", "x", "core"))
    seq = ("zh", "zl", "y")
    in_specs = (
        P(seq, None),
        P(),
        P(),
        P(None, TP),
        P(TP, None),
        P(None, TP),
        P(seq, TP),
        P(seq),
        P(TP),
        P(None, TP),
        P(seq, TP),
    )
    return jax.shard_map(
        body, mesh=split, in_specs=in_specs, out_specs=P(seq, TP), check_vma=False
    )
```

```python
import functools
import math

import jax
import jax.numpy as jnp
from jax import lax
from jax.experimental import pallas as pl
from jax.experimental.pallas import tpu as pltpu
from jax.sharding import Mesh
from jax.sharding import PartitionSpec as P

D = 8192
HEAD = 128
HALF = 64
GROUP = 4
TOK = 256
IMG = 128
ROWS = 272
TP = ("x", "core")
Z = ("zh", "zl")
BF16 = jnp.bfloat16
F32 = jnp.float32
NEG = -1e30
LOG2E = math.log2(math.e)
WIDE = TOK + IMG
KEYS = 2048
CHUNK = 1024
PER = CHUNK // TOK
ROWS_Q = GROUP * TOK
SCALE = HEAD ** (-0.5)


def shift(values, axis, step):
    count = lax.axis_size(axis)
    return lax.ppermute(values, axis, [(i, (i + step) % count) for i in range(count)])


def pick(values, index):
    return lax.dynamic_index_in_dim(values, index, 0, keepdims=False)


def vmem(mib):
    return pltpu.CompilerParams(vmem_limit_bytes=mib * 1024 * 1024)


def split_squares(column, count):
    row = jnp.broadcast_to(column, (count, HEAD)).T[:16]
    high = row.astype(BF16).astype(F32)
    at = lax.broadcasted_iota(jnp.int32, row.shape, 0)
    return jnp.where(at == 0, high, jnp.where(at == 1, row - high, 0.0)).astype(BF16)


def head_rows(core, features, tail, weight_ref, give_ref, keep_ref):
    for x_at in range(4):
        for own, ref in ((0, give_ref), (1, keep_ref)):
            head = 2 * x_at + jnp.where(own == 1, core, 1 - core)
            weight = weight_ref[pl.ds(pl.multiple_of(head * TOK, TOK), TOK), :]
            rows = lax.dot_general(
                weight, features, (((1,), (1,)), ((), ())), preferred_element_type=F32
            )
            ref[x_at, :TOK, :] = rows.astype(BF16)
            ref[x_at, TOK:, :] = tail


def gain_features(features, gain_ref):
    widened = features.astype(F32)
    squares = jnp.sum(jnp.square(widened), axis=1, keepdims=True)
    return (widened * gain_ref[...]).astype(BF16), split_squares(squares, features.shape[0])


def text_project_kernel(core, hidden_ref, gain_ref, weight_ref, give_ref, keep_ref):
    gained, tail = gain_features(hidden_ref[...], gain_ref)
    head_rows(core[0], gained, tail, weight_ref, give_ref, keep_ref)


def image_project_kernel(
    core, half_ref, other_ref, proj_ref, gain_ref, weight_ref, give_ref, keep_ref, encoded
):
    at = pl.multiple_of(core[0] * HALF, HALF)
    encoded[pl.ds(at, HALF), :] = half_ref[...]
    encoded[pl.ds(HALF - at, HALF), :] = other_ref[...]
    image = jnp.dot(encoded[...], proj_ref[...], preferred_element_type=F32).astype(BF16)
    gained, tail = gain_features(image, gain_ref)
    head_rows(core[0], gained, tail, weight_ref, give_ref, keep_ref)


def project(kernel, features, norm_gain, kv_weight, core, count, scratch):
    mine = jnp.reshape(core, (1,)).astype(jnp.int32)
    shape = jax.ShapeDtypeStruct((4, ROWS, count), BF16)
    return pl.pallas_call(
        kernel,
        out_shape=(shape, shape),
        in_specs=[
            pl.BlockSpec(memory_space=pltpu.SMEM),
            *[pl.BlockSpec(memory_space=pltpu.VMEM)] * (len(features) + 2),
        ],
        scratch_shapes=scratch,
        compiler_params=vmem(8),
        name="project",
    )(mine, *features, norm_gain[None, :], kv_weight)


def pair_kernel(place, keep_ref, got_ref, own_ref, two_ref, one_ref, three_ref):
    for step, ref in ((2, two_ref), (1, one_ref), (3, three_ref), (0, own_ref)):
        at = lax.rem(place[0] + step, 4)
        total = keep_ref[at].astype(F32) + got_ref[at].astype(F32)
        ref[...] = total.astype(ref.dtype)


def add_pair(keep, got, x_at):
    part = keep.shape[1:]
    return pl.pallas_call(
        pair_kernel,
        out_shape=(jax.ShapeDtypeStruct(part, F32), *[jax.ShapeDtypeStruct(part, BF16)] * 3),
        in_specs=[
            pl.BlockSpec(memory_space=pltpu.SMEM),
            *[pl.BlockSpec(memory_space=pltpu.VMEM)] * 2,
        ],
        compiler_params=vmem(6),
        name="add_pair",
    )(jnp.reshape(x_at, (1,)).astype(jnp.int32), keep, got)


def finish_kernel(slots, *refs):
    *inputs, out_ref = refs
    for lanes, pieces in ((slice(0, TOK), inputs[:4]), (slice(TOK, WIDE), inputs[4:])):
        total = pieces[0][...]
        for ref in pieces[1:]:
            total = total + ref[...].astype(F32)
        inverse = lax.rsqrt((total[TOK : TOK + 1] + total[TOK + 1 : TOK + 2]) / D + 1e-05)
        out_ref[:TOK, lanes] = (total[:TOK] * inverse).astype(BF16)
    lane = lax.broadcasted_iota(jnp.int32, (ROWS - TOK, WIDE), 1)
    out_ref[TOK:, :] = jnp.where(lane < IMG, slots[0], slots[1]).astype(F32).astype(BF16)


def finish_rows(slots, text, image):
    return pl.pallas_call(
        finish_kernel,
        out_shape=jax.ShapeDtypeStruct((ROWS, WIDE), BF16),
        in_specs=[
            pl.BlockSpec(memory_space=pltpu.SMEM),
            *[pl.BlockSpec(memory_space=pltpu.VMEM)] * 8,
        ],
        compiler_params=vmem(6),
        name="finish_rows",
    )(slots, *text, *image)


def ring_gather(block):
    blocks, up, down = [block], block, block
    for _ in range(3):
        up, down = shift(up, Z, 1), shift(down, Z, 7)
        blocks += [up, down]
    return [*blocks, shift(up[:IMG], Z, 1), shift(down[IMG:], Z, 7)]


def exchange(pieces):
    own, two, one, three = pieces
    return [own, shift(two, "x", 2), shift(one, "x", 1), shift(three, "x", 3)]


def merge_kernel(place, *refs):
    *blocks, cos_ref, sin_ref, outer_cos_ref, outer_sin_ref, keys, values, gathered = refs
    for step, ref in zip((0, 7, 1, 6, 2, 5, 3), blocks):
        gathered[lax.rem(place[0] + step, 8)] = ref[...]
    far = lax.rem(place[0] + 4, 8)
    gathered[far, :IMG, :] = blocks[7][...]
    gathered[far, IMG:, :] = blocks[8][...]
    values[:, HEAD:] = jnp.ones((KEYS, HEAD), BF16)

    @pl.loop(0, 8)
    def one_block(block):
        outer_cos, outer_sin = outer_cos_ref[block], outer_sin_ref[block]
        for slot in range(2):
            lanes = slice(slot * IMG, (slot + 1) * IMG)
            here = pl.ds(pl.multiple_of(block * TOK + slot * IMG, IMG), IMG)
            text = gathered[block, :, lanes].astype(F32)
            source = text[TOK : TOK + 1, :]
            rows = text[:TOK, :]
            for r in range(4):
                image = gathered[2 * r + lax.rem(block, 2), :TOK, TOK:]
                rows = jnp.where(source == float(r), image.astype(F32), rows)
            inner_cos, inner_sin = cos_ref[:, lanes], sin_ref[:, lanes]
            cosine = inner_cos * outer_cos - inner_sin * outer_sin
            sine = inner_sin * outer_cos + inner_cos * outer_sin
            first, second = rows[:HALF], rows[HALF:HEAD]
            keys[:HALF, here] = (first * cosine - second * sine).astype(BF16)
            keys[HALF:, here] = (second * cosine + first * sine).astype(BF16)
            values[here, :HEAD] = rows[HEAD:].T.astype(BF16)


def merge(place, blocks, tables):
    return pl.pallas_call(
        merge_kernel,
        out_shape=(
            jax.ShapeDtypeStruct((HEAD, KEYS), BF16),
            jax.ShapeDtypeStruct((KEYS, 2 * HEAD), BF16),
        ),
        in_specs=[
            pl.BlockSpec(memory_space=pltpu.SMEM),
            *[pl.BlockSpec(memory_space=pltpu.VMEM)] * (len(blocks) + len(tables)),
        ],
        scratch_shapes=[pltpu.VMEM((8, ROWS, WIDE), BF16)],
        compiler_params=vmem(10),
        name="merge",
    )(place, *blocks, *tables)


def attend_kernel(step, place, keys, values, query_ref, out_ref, scores, top, mixed):
    z_at, y_at = place[0], place[1]
    block_at = lax.rem(y_at + step, 4)
    full = z_at + jnp.where(y_at < block_at, 1, 0)
    count = z_at + jnp.where(y_at <= block_at, 1, 0)
    plain = full // PER
    chunks = (count + PER - 1) // PER
    top[...] = jnp.full(top.shape, NEG, F32)

    def chunk_at(chunk, offset=0, size=CHUNK):
        return pl.ds(pl.multiple_of(chunk * CHUNK + offset, HEAD), size)

    def score(chunk, masked):
        keys_now = keys[:, chunk_at(chunk)]
        if masked:
            key_at = lax.broadcasted_iota(jnp.int32, (TOK, CHUNK), 1)
            key_at = key_at + (key_at // TOK) * (3 * TOK)
            query_at = lax.broadcasted_iota(jnp.int32, (TOK, CHUNK), 0)
            offset = ((PER * chunk - z_at) * 4 + y_at - block_at) * TOK
            allowed = key_at + offset <= query_at
        for h in range(GROUP):
            here = slice(h * TOK, (h + 1) * TOK)
            s = jnp.dot(
                query_ref[:, h * HEAD : (h + 1) * HEAD], keys_now, preferred_element_type=F32
            )
            if masked:
                s = jnp.where(allowed, s, -jnp.inf)
            scores[here, chunk_at(chunk)] = s
            most = top[here, :]
            for lane in range(0, CHUNK, HEAD):
                most = jnp.maximum(most, s[:, lane : lane + HEAD])
            top[here, :] = most

    pl.loop(0, plain)(lambda chunk: score(chunk, False))

    @pl.when(chunks > plain)
    def last():
        score(plain, True)

    top[...] = jnp.broadcast_to(jnp.max(top[...], axis=1, keepdims=True), top.shape)

    mixed[...] = jnp.zeros(mixed.shape, F32)

    @pl.loop(0, chunks)
    def weigh(chunk):
        values_now = values[chunk_at(chunk), :]
        for h in range(GROUP):
            here = slice(h * TOK, (h + 1) * TOK)
            most = top[here, :]
            weights = jnp.concatenate(
                [
                    jnp.exp2(scores[here, chunk_at(chunk, lane, HEAD)] - most).astype(BF16)
                    for lane in range(0, CHUNK, HEAD)
                ],
                1,
            )
            rows = jnp.dot(weights, values_now, preferred_element_type=F32)
            mixed[here, :] += rows

    lane = lax.broadcasted_iota(jnp.int32, (TOK, HEAD), 1)
    stats = jnp.zeros((TOK, HEAD), F32)
    for h in range(GROUP):
        here = slice(h * TOK, (h + 1) * TOK)
        total = mixed[here, HEAD:]
        safe = jnp.where(total > 0.0, total, 1.0)
        out_ref[:TOK, h * HEAD : (h + 1) * HEAD] = (mixed[here, :HEAD] / safe).astype(BF16)
        stats = jnp.where(lane == h, top[here, :], jnp.where(lane == GROUP + h, total, stats))
    rows = stats.T
    tops, totals = rows[:GROUP], rows[GROUP : 2 * GROUP]
    some = totals > 0.0
    level = jnp.where(some, tops + jnp.log2(jnp.where(some, totals, 1.0)), NEG)
    high = level.astype(BF16).astype(F32)
    middle = (level - high).astype(BF16).astype(F32)
    low = level - high - middle
    pad = jnp.zeros((ROWS - TOK - 3 * GROUP, TOK), F32)
    out_ref[TOK:, :TOK] = jnp.concatenate([high, middle, low, pad], 0).astype(BF16)
    out_ref[TOK:, TOK:] = jnp.zeros((ROWS - TOK, 2 * HEAD), BF16)


def attend(step, place, keys, values, queries):
    return pl.pallas_call(
        functools.partial(attend_kernel, step),
        out_shape=jax.ShapeDtypeStruct((ROWS, GROUP * HEAD), BF16),
        in_specs=[
            pl.BlockSpec(memory_space=pltpu.SMEM),
            *[pl.BlockSpec(memory_space=pltpu.VMEM)] * 3,
        ],
        scratch_shapes=[
            pltpu.VMEM((ROWS_Q, KEYS), F32),
            pltpu.VMEM((ROWS_Q, HEAD), F32),
            pltpu.VMEM((ROWS_Q, 2 * HEAD), F32),
        ],
        compiler_params=vmem(24),
        cost_estimate=pl.CostEstimate(
            flops=4 * ROWS_Q * KEYS * HEAD, bytes_accessed=2 << 20, transcendentals=ROWS_Q * KEYS
        ),
        name="attend",
    )(place, keys, values, queries)


def layer_norm(values, norm_scale, norm_shift):
    widened = values.astype(F32)
    center = jnp.mean(widened, axis=-1, keepdims=True)
    spread = jnp.mean(jnp.square(widened - center), axis=-1, keepdims=True)
    return ((widened - center) * lax.rsqrt(spread + 1e-06) * norm_scale + norm_shift).astype(BF16)


def combine_kernel(*refs):
    *parts, out_ref = refs
    levels = []
    for ref in parts:
        rows = ref[TOK:, :TOK].astype(F32)
        levels.append(
            [rows[h : h + 1] + rows[4 + h : 5 + h] + rows[8 + h : 9 + h] for h in range(GROUP)]
        )
    weights = []
    for h in range(GROUP):
        most = functools.reduce(jnp.maximum, [level[h] for level in levels])
        raised = [jnp.exp2(level[h] - most) for level in levels]
        total = sum(raised)
        weights += [r / total for r in raised]
    rows = jnp.concatenate([*weights, jnp.zeros((HEAD - len(weights), TOK), F32)], 0).T
    for h in range(GROUP):
        lanes = slice(h * HEAD, (h + 1) * HEAD)
        mixed = sum(
            rows[:, 4 * h + i : 4 * h + i + 1] * ref[:TOK, lanes].astype(F32)
            for i, ref in enumerate(parts)
        )
        out_ref[:, lanes] = mixed.astype(BF16)


def combine(parts):
    return pl.pallas_call(
        combine_kernel,
        out_shape=jax.ShapeDtypeStruct((TOK, GROUP * HEAD), BF16),
        compiler_params=vmem(6),
        name="combine",
    )(*parts)


def body(
    patches,
    patch_gain,
    patch_shift,
    encoder_up,
    encoder_down,
    proj_weight,
    hidden_text,
    slot_source,
    norm_gain,
    kv_weight,
    queries,
):
    z_at, y_at = lax.axis_index(Z), lax.axis_index("y")
    x_at, core = lax.axis_index("x"), lax.axis_index("core")

    place = jnp.stack([z_at, y_at]).astype(jnp.int32)

    normed_patches = layer_norm(patches, patch_gain, patch_shift)
    enc_hidden = jax.nn.gelu(
        jnp.dot(normed_patches, encoder_up, preferred_element_type=F32), approximate=False
    ).astype(BF16)
    partial_out = jnp.dot(enc_hidden, encoder_down, preferred_element_type=F32).astype(BF16)
    halves = partial_out.reshape(2, HALF, -1)
    half = pick(halves, core).astype(F32) + shift(pick(halves, 1 - core), "core", 1).astype(F32)
    sent = half.astype(BF16)
    sent, hidden_text = lax.optimization_barrier((sent, hidden_text))

    give, keep = project(text_project_kernel, [hidden_text], norm_gain, kv_weight, core, TOK, [])
    text_pieces = add_pair(keep, shift(give, "core", 1), x_at)
    for step in (2, 1, 3):
        half = half + shift(sent, "x", step).astype(F32)
    half = (half + pick(patches.reshape(2, HALF, -1), core).astype(F32)).astype(BF16)
    half, text_pieces = lax.optimization_barrier((half, text_pieces))
    text_got = exchange(text_pieces)
    other = shift(half, "core", 1)

    give, keep = project(
        image_project_kernel,
        [half, other, proj_weight],
        norm_gain,
        kv_weight,
        core,
        IMG,
        [pltpu.VMEM(patches.shape, BF16)],
    )
    give, keep, text_got = lax.optimization_barrier((give, keep, text_got))
    image_got = exchange(add_pair(keep, shift(give, "core", 1), x_at))
    block = finish_rows(slot_source, text_got, image_got)
    block, queries_later = lax.optimization_barrier((block, queries))
    blocks = ring_gather(block)
    asked = {step: shift(queries_later, "y", 4 - step) for step in (2, 1, 3)}

    frequencies = jnp.exp(
        jnp.arange(HALF, dtype=F32) * (-2.0 * math.log(500000.0) / (2 * HALF))
    )
    inner = jnp.arange(TOK, dtype=F32)[None, :] * frequencies[:, None]
    starts = ((jnp.arange(8, dtype=jnp.int32) * 4 + y_at) * TOK).astype(F32)
    outer = jnp.broadcast_to(starts[:, None, None] * frequencies[None, :, None], (8, HALF, HEAD))
    factor = SCALE * LOG2E
    tables = (jnp.cos(inner) * factor, jnp.sin(inner) * factor, jnp.cos(outer), jnp.sin(outer))
    keys, values = merge(place, blocks, tables)
    received = []
    for step in (2, 1, 3):
        received.append(shift(attend(step, place, keys, values, asked[step]), "y", step))
    return combine([attend(0, place, keys, values, queries), *received])


def solution(mesh):
    split = Mesh(mesh.devices.reshape(4, 2, 4, 4, 2), ("zh", "zl", "y", "x", "core"))
    seq = ("zh", "zl", "y")
    in_specs = (
        P(seq, None),
        P(),
        P(),
        P(None, TP),
        P(TP, None),
        P(None, TP),
        P(seq, TP),
        P(seq),
        P(TP),
        P(None, TP),
        P(seq, TP),
    )
    return jax.shard_map(
        body, mesh=split, in_specs=in_specs, out_specs=P(seq, TP), check_vma=False
    )
```
